256 devices in a mesh: row: 16 (over z, core), col: 16 (over y, x).
Axes of the slice: x: 4, y: 4, z: 8, core: 2. Of those that a mesh axis runs over, the one named last changes fastest.
Arguments:
- csm_real: float32 [8192, 8192], P('row', 'col'), as said below
- csm_imag: float32 [8192, 8192], P('row', 'col'), as said below
- start_block: float32 [2, 8192, 256], P(None, ('col', 'row')), may hold values from -6 to 6
- mic_coords: int32 [2, 8192], P(None, 'col'), may hold values from 0 to 127
- grid_coords: int32 [2, 32768], P(None, 'row'), may hold values from 0 to 4092
- bin_index: int32 [], replicated, may hold values from 1 to 63
Outputs:
- basis: float32 [2, 8192, 256], P(None, ('col', 'row'))
- beam_map: float32 [32768], P(('row', 'col'))
The draws below stay inside these ranges and needn't reach their ends.
Inputs may be any that keep to these rules, and one draw needn't show every extreme that they name: csm_real is symmetric and csm_imag antisymmetric; the matrix they form is Hermitian with a positive diagonal. `csm_imag`: antisymmetric: the imaginary part of the same Hermitian matrix.
All inputs are finite; a program needn't handle non-finite values.
Results may differ from the reference program's by a relative error of at most 0.0003.
Values sent between devices are 32-bit elements; how exact they have to be, the bound alone decides.
No kernel may reach another device: no remote copies, remote signals or barrier semaphores. Data moves between devices by JAX's collectives and lax.ppermute only.
A program may use at most 64 MiB of HBM per device.

```python
import math
import jax
import jax.numpy as jnp
from jax import lax

M = 8192
K = 256
GRID = 32768
ITERS = 2
NU = 4


def noise_square(key):
    return jax.random.normal(key, (M, M), jnp.float32)


def draw_csm_real(key, part):
    key = jax.random.fold_in(key, 11)
    noise = noise_square(jax.random.fold_in(key, 1))
    spread = 0.7 / (2.0 * M) ** 0.5
    loading = jax.random.uniform(jax.random.fold_in(key, 2), (M,), jnp.float32, 2.5, 4.5)
    return (noise + noise.T) * (spread / 2.0 ** 0.5) + jnp.diag(loading)


def draw_csm_imag(key, part):
    key = jax.random.fold_in(key, 23)
    noise = noise_square(jax.random.fold_in(key, 1))
    spread = 0.7 / (2.0 * M) ** 0.5
    return (noise - noise.T) * (spread / 2.0 ** 0.5)


def set_ends(drawn, key, least, high):
    longest = drawn.shape.index(max(drawn.shape))
    spots = []
    for shift in (0, 1):
        where = [jax.random.randint(jax.random.fold_in(key, axis), (), 0, length) for axis, length in enumerate(drawn.shape)]
        where[longest] = (where[longest] + shift) % drawn.shape[longest]
        spots.append(tuple(where))
    return drawn.at[spots[0]].set(least).at[spots[1]].set(high)


def block_scale(stream_key, dims, shards, smallest, high):
    factor_of, own = 1.0, jax.random.fold_in(stream_key, 6)
    for axis_at, parts in shards:
        steps = jnp.exp(jax.random.uniform(jax.random.fold_in(own, axis_at), (parts,), jnp.float32, smallest / len(shards), high / len(shards)))
        factor_of = factor_of * jnp.repeat(steps, dims[axis_at] // parts).reshape([-1 if axis == axis_at else 1 for axis in range(len(dims))])
    return factor_of


def bell_draw(rng, shape, scale, most, shards=(), kind=jnp.bfloat16):
    drawn = scale * jax.random.normal(rng, shape, jnp.float32)
    if shards:
        drawn = drawn * block_scale(rng, shape, shards, -0.22, 0.18)
    return jnp.clip(drawn, -most, most).astype(kind)


def setup_inputs(seed: int = 0) -> dict:
    splits = jax.random.split(jax.random.key(seed), 7)
    return {
        "csm_real": draw_csm_real(jax.random.fold_in(splits[6], 71), 0),
        "csm_imag": draw_csm_imag(jax.random.fold_in(splits[6], 71), 0),
        "start_block": bell_draw(splits[2], (2, M, K), 1.0, 6.0, ((1, 256),), jnp.float32),
        "mic_coords": set_ends(jax.random.randint(splits[3], (2, M), 0, 128), jax.random.fold_in(splits[3], 1), 0, 127).astype(jnp.int32),
        "grid_coords": set_ends(jax.random.randint(splits[4], (2, GRID), 0, 4093), jax.random.fold_in(splits[4], 1), 0, 4092).astype(jnp.int32),
        "bin_index": jax.random.randint(splits[5], (), 1, 64).astype(jnp.int32),
    }


HIGH = lax.Precision.HIGHEST

def solve_right(lower, block_part):
    return lax.linalg.triangular_solve(lower, block_part, left_side=False, lower=True, transpose_a=True)

def apply_inverse(lower, block):
    return jnp.stack([solve_right(lower, block[0]), solve_right(lower, block[1])])

def reference(csm_real, csm_imag, start_block, mic_coords, grid_coords, bin_index):
    block = start_block
    lower = jnp.eye(K, dtype=jnp.float32)
    for step in range(ITERS):
        top = jnp.dot(csm_real, block[0], precision=HIGH) - jnp.dot(csm_imag, block[1], precision=HIGH)
        bottom = jnp.dot(csm_imag, block[0], precision=HIGH) + jnp.dot(csm_real, block[1], precision=HIGH)
        product = jnp.stack([top, bottom])
        gram = jnp.einsum('ink,inl->kl', product, product, precision=HIGH)
        lower = jnp.linalg.cholesky(gram)
        block = apply_inverse(lower, product)
    weights = jnp.diagonal(lower) ** (1.0 / NU)
    width = math.gcd(GRID, 2048)
    coords = grid_coords.reshape(2, GRID // width, width).transpose(1, 0, 2)

    def project(piece):
        index = bin_index * (piece[0][:, None] * mic_coords[0][None, :] + piece[1][:, None] * mic_coords[1][None, :])
        angle = (index % 4093).astype(jnp.float32) * (2.0 * math.pi / 4093.0)
        cosine = jnp.cos(angle)
        sine = jnp.sin(angle)
        real_part = jnp.dot(cosine, block[0], precision=HIGH) - jnp.dot(sine, block[1], precision=HIGH)
        imag_part = jnp.dot(cosine, block[1], precision=HIGH) + jnp.dot(sine, block[0], precision=HIGH)
        power = jnp.dot(real_part * real_part + imag_part * imag_part, weights, precision=HIGH) / jnp.sum(weights)
        return power ** NU
    beam_map = lax.map(project, coords).reshape(GRID)
    return (block, beam_map)
```

```python
import math

import jax
import jax.numpy as jnp
from jax import lax
from jax.experimental import pallas as pl
from jax.experimental.pallas import tpu as pltpu
from jax.sharding import PartitionSpec as P

NU = 4
K = 256
MOD = 4093
HIGH = lax.Precision.HIGHEST

Z_GROUPS = [list(range(core, 16, 2)) for core in range(2)]
CORE_SWAP = [(index, index ^ 1) for index in range(16)]

PANEL = 64
MICRO = 16


def factor_kernel(gram_ref, upper_ref, inverse_ref, work_ref):
    rows = lax.broadcasted_iota(jnp.int32, (K, K), 0)
    cols = lax.broadcasted_iota(jnp.int32, (K, K), 1)
    work_ref[:, :K] = gram_ref[...]
    work_ref[:, K:] = (rows == cols).astype(jnp.float32)
    panel_row = lax.broadcasted_iota(jnp.int32, (PANEL, 128), 0)
    for start in range(0, K, PANEL):
        low = (start // 128) * 128
        high = K + ((start + PANEL + 127) // 128) * 128
        width = high - low
        offset = start - low
        panel = work_ref[start : start + PANEL, low:high]
        for first in range(0, PANEL, MICRO):
            columns = [
                jnp.broadcast_to(
                    panel[:, offset + first + k : offset + first + k + 1], (PANEL, 128)
                )
                for k in range(MICRO)
            ]
            for k in range(MICRO):
                j = first + k
                scale = jnp.where(panel_row > j, columns[k] * (1.0 / columns[k][j : j + 1, :]), 0.0)
                for later in range(k + 1, MICRO):
                    columns[later] = columns[later] - scale * columns[later][j : j + 1, :]
                panel = (
                    panel
                    - jnp.concatenate([scale] * (width // 128), axis=1) * panel[j : j + 1, :]
                )
        square_row = lax.broadcasted_iota(jnp.int32, (PANEL, PANEL), 0)
        square_col = lax.broadcasted_iota(jnp.int32, (PANEL, PANEL), 1)
        pivots = jnp.sum(
            jnp.where(square_row == square_col, panel[:, offset : offset + PANEL], 0.0),
            axis=1,
            keepdims=True,
        )
        panel = panel * (1.0 / jnp.sqrt(pivots))
        panel_cols = lax.broadcasted_iota(jnp.int32, (PANEL, K - low), 1) + low
        panel_rows = lax.broadcasted_iota(jnp.int32, (PANEL, K - low), 0) + start
        upper_ref[start : start + PANEL, :] = jnp.zeros((PANEL, K), jnp.float32)
        upper_ref[start : start + PANEL, low:K] = jnp.where(
            panel_cols >= panel_rows, panel[:, : K - low], 0.0
        )
        inverse_ref[start : start + PANEL, :] = jnp.zeros((PANEL, K), jnp.float32)
        inverse_ref[start : start + PANEL, : high - K] = panel[:, K - low :]
        after = start + PANEL
        if after < K:
            update = lax.dot_general(
                panel[:, after - low : K - low],
                panel,
                (((0,), (0,)), ((), ())),
                precision=HIGH,
                preferred_element_type=jnp.float32,
            )
            work_ref[after:, low:high] = work_ref[after:, low:high] - update


def factor(gram):
    return pl.pallas_call(
        factor_kernel,
        out_shape=(jax.ShapeDtypeStruct((K, K), jnp.float32),) * 2,
        scratch_shapes=[pltpu.VMEM((K, 2 * K), jnp.float32)],
        compiler_params=pltpu.CompilerParams(vmem_limit_bytes=16 * 2**20),
        cost_estimate=pl.CostEstimate(
            flops=4 * K**3, bytes_accessed=12 * K * K, transcendentals=K
        ),
        name="factor",
    )(gram)


def dot(a, b):
    return jnp.dot(a, b, precision=HIGH, preferred_element_type=jnp.float32)


def dot_tn(a, b):
    return lax.dot_general(
        a, b, (((0,), (0,)), ((), ())), precision=HIGH, preferred_element_type=jnp.float32
    )


def dot_nt(a, b):
    return lax.dot_general(
        a, b, (((1,), (1,)), ((), ())), precision=HIGH, preferred_element_type=jnp.float32
    )


def turned(block):
    return jnp.concatenate([-block[:, K:], block[:, :K]], axis=1)


def exchange(pieces, axis, groups=None):
    return lax.all_to_all(pieces, axis, 0, 0, tiled=True, axis_index_groups=groups)


def sum_col(whole):
    pieces = whole.reshape(16, whole.shape[0] // 16, whole.shape[1])
    return jnp.sum(exchange(pieces, "col"), axis=0)


def gather_col(piece):
    return exchange(jnp.broadcast_to(piece[None], (16,) + piece.shape), "col")


def sum_row(pieces, core):
    pieces = pieces.reshape((8, 2) + pieces.shape[1:])
    kept = lax.dynamic_index_in_dim(pieces, core, 1, keepdims=False)
    sent = lax.dynamic_index_in_dim(pieces, 1 - core, 1, keepdims=False)
    pair = kept + lax.ppermute(sent, "row", CORE_SWAP)
    return jnp.sum(exchange(pair, "row", Z_GROUPS), axis=0)


def gather_row(piece, core):
    mine = exchange(jnp.broadcast_to(piece[None], (8,) + piece.shape), "row", Z_GROUPS)
    other = lax.ppermute(mine, "row", CORE_SWAP)
    even = jnp.where(core == 0, mine, other)
    odd = jnp.where(core == 0, other, mine)
    both = jnp.stack([even, odd], axis=1)
    return both.reshape((16,) + piece.shape)


def steering(grid, mics, bin_index):
    reduced = ((bin_index * grid) % MOD).astype(jnp.float32)
    place = mics.astype(jnp.float32)
    index = reduced[0][:, None] * place[0][None, :] + reduced[1][:, None] * place[1][None, :]
    turns = index - jnp.round(index * (1.0 / MOD)) * float(MOD)
    angle = turns * (2.0 * math.pi / MOD)
    return jnp.cos(angle), jnp.sin(angle)


def gram_of(block):
    return dot_tn(block[:, :K], block[:, :K]) + dot_tn(block[:, K:], block[:, K:])


def body(csm_real, csm_imag, start_block, mic_coords, grid_coords, bin_index):
    row = lax.axis_index("row")
    core = row % 2
    start = jnp.concatenate([start_block[0], start_block[1]], axis=1)
    start = gather_row(start, core).reshape(512, 2 * K)
    first_partial = dot(csm_real, start) + dot(csm_imag, turned(start))
    first_rows = sum_col(first_partial)
    first = gather_col(first_rows).reshape(512, 2 * K)
    second_partial = dot_tn(csm_real, first) - dot_tn(csm_imag, turned(first))
    first_gram = gram_of(first).reshape(16, 16, K)
    first_gram = jnp.concatenate([first_gram[:, :8], first_gram[:, 8:]], axis=2)
    both = jnp.concatenate([second_partial.reshape(16, 32, 2 * K), first_gram], axis=1)
    both = sum_row(both, core)
    raw_rows = both[:32]
    both = gather_row(both, core)
    raw = both[:, :32].reshape(512, 2 * K)
    first_gram = jnp.concatenate([both[:, 32:, :K], both[:, 32:, K:]], axis=1).reshape(K, K)
    cosine, sine = lax.optimization_barrier(steering(grid_coords, mic_coords, bin_index))
    projected = sum_col(dot(cosine, raw) + dot(sine, turned(raw)))
    first_upper, first_inverse = factor(first_gram)
    del first_upper
    second = jnp.concatenate(
        [dot_nt(raw[:, :K], first_inverse), dot_nt(raw[:, K:], first_inverse)], axis=1
    )
    gram_slice = lax.dynamic_slice_in_dim(gram_of(second), row * 16, 16, axis=0)
    gram_slice = jnp.sum(gather_col(gram_slice), axis=0)
    second_gram = lax.all_gather(gram_slice, "row", axis=0, tiled=True)
    second_upper, second_inverse = factor(second_gram)
    weights = jnp.diagonal(second_upper) ** (1.0 / NU)
    both_inverse = dot(second_inverse, first_inverse)
    rows = jnp.stack(
        [dot_nt(raw_rows[:, :K], first_inverse), dot_nt(raw_rows[:, K:], first_inverse)]
    )
    basis = jnp.stack([dot_nt(rows[0], second_inverse), dot_nt(rows[1], second_inverse)])
    real_part = dot_nt(projected[:, :K], both_inverse)
    imag_part = dot_nt(projected[:, K:], both_inverse)
    power = dot(real_part * real_part + imag_part * imag_part, weights) / jnp.sum(weights)
    return (basis, power**NU)


def solution(mesh):
    in_specs = (
        P("row", "col"),
        P("row", "col"),
        P(None, ("col", "row"), None),
        P(None, "col"),
        P(None, "row"),
        P(),
    )
    out_specs = (P(None, ("col", "row"), None), P(("row", "col")))
    return jax.shard_map(body, mesh=mesh, in_specs=in_specs, out_specs=out_specs, check_vma=False)
```

```python
import jax
import jax.numpy as jnp
from jax import lax
from jax.experimental import pallas as pl
from jax.experimental.pallas import tpu as pltpu
from jax.sharding import PartitionSpec as P

NU = 4
K = 256
MOD = 4093
HIGH = lax.Precision.HIGHEST

Z_GROUPS = [list(range(core, 16, 2)) for core in range(2)]
CORE_SWAP = [(index, index ^ 1) for index in range(16)]

PAIR_SWAP = [(index, index ^ 1) for index in range(16)]
HALF_GROUPS = [list(range(half, 16, 2)) for half in range(2)]
HALF = K // 2
SMEM = pl.BlockSpec(memory_space=pltpu.SMEM)
HBM = pl.BlockSpec(memory_space=pltpu.HBM)
VMEM = pl.BlockSpec(memory_space=pltpu.VMEM)

PANEL = 64
MICRO = 16


def factor_kernel(gram_ref, upper_ref, inverse_ref, work_ref):
    rows = lax.broadcasted_iota(jnp.int32, (K, K), 0)
    cols = lax.broadcasted_iota(jnp.int32, (K, K), 1)
    work_ref[:, :K] = gram_ref[...]
    work_ref[:, K:] = (rows == cols).astype(jnp.float32)
    panel_row = lax.broadcasted_iota(jnp.int32, (PANEL, 128), 0)
    for start in range(0, K, PANEL):
        low = (start // 128) * 128
        high = K + ((start + PANEL + 127) // 128) * 128
        width = high - low
        offset = start - low
        panel = work_ref[start : start + PANEL, low:high]
        for first in range(0, PANEL, MICRO):
            columns = [
                jnp.broadcast_to(
                    panel[:, offset + first + k : offset + first + k + 1], (PANEL, 128)
                )
                for k in range(MICRO)
            ]
            for k in range(MICRO):
                j = first + k
                scale = jnp.where(panel_row > j, columns[k] * (1.0 / columns[k][j : j + 1, :]), 0.0)
                for later in range(k + 1, MICRO):
                    columns[later] = columns[later] - scale * columns[later][j : j + 1, :]
                panel = (
                    panel
                    - jnp.concatenate([scale] * (width // 128), axis=1) * panel[j : j + 1, :]
                )
        square_row = lax.broadcasted_iota(jnp.int32, (PANEL, PANEL), 0)
        square_col = lax.broadcasted_iota(jnp.int32, (PANEL, PANEL), 1)
        pivots = jnp.sum(
            jnp.where(square_row == square_col, panel[:, offset : offset + PANEL], 0.0),
            axis=1,
            keepdims=True,
        )
        panel = panel * (1.0 / jnp.sqrt(pivots))
        panel_cols = lax.broadcasted_iota(jnp.int32, (PANEL, K - low), 1) + low
        panel_rows = lax.broadcasted_iota(jnp.int32, (PANEL, K - low), 0) + start
        upper_ref[start : start + PANEL, :] = jnp.zeros((PANEL, K), jnp.float32)
        upper_ref[start : start + PANEL, low:K] = jnp.where(
            panel_cols >= panel_rows, panel[:, : K - low], 0.0
        )
        inverse_ref[start : start + PANEL, :] = jnp.zeros((PANEL, K), jnp.float32)
        inverse_ref[start : start + PANEL, : high - K] = panel[:, K - low :]
        after = start + PANEL
        if after < K:
            update = lax.dot_general(
                panel[:, after - low : K - low],
                panel,
                (((0,), (0,)), ((), ())),
                precision=HIGH,
                preferred_element_type=jnp.float32,
            )
            work_ref[after:, low:high] = work_ref[after:, low:high] - update


def factor(gram):
    return pl.pallas_call(
        factor_kernel,
        out_shape=(jax.ShapeDtypeStruct((K, K), jnp.float32),) * 2,
        scratch_shapes=[pltpu.VMEM((K, 2 * K), jnp.float32)],
        compiler_params=pltpu.CompilerParams(vmem_limit_bytes=16 * 2**20),
        cost_estimate=pl.CostEstimate(
            flops=4 * K**3, bytes_accessed=12 * K * K, transcendentals=K
        ),
        name="factor",
    )(gram)


def dot(a, b):
    return jnp.dot(a, b, precision=HIGH, preferred_element_type=jnp.float32)


def dot_tn(a, b):
    return lax.dot_general(
        a, b, (((0,), (0,)), ((), ())), precision=HIGH, preferred_element_type=jnp.float32
    )


def dot_nt(a, b):
    return lax.dot_general(
        a, b, (((1,), (1,)), ((), ())), precision=HIGH, preferred_element_type=jnp.float32
    )


def turned(block):
    return jnp.concatenate([-block[:, K:], block[:, :K]], axis=1)


def exchange(pieces, axis, groups=None):
    return lax.all_to_all(pieces, axis, 0, 0, tiled=True, axis_index_groups=groups)


def drain(copies):
    for copy in copies:
        copy.start()
    for copy in copies:
        copy.wait()


def spread_kernel(pieces_ref, total_ref, copies_ref, sems):
    total_ref[...] = jnp.sum(pieces_ref[...], axis=0)
    drain(
        [
            pltpu.make_async_copy(total_ref, copies_ref.at[index], sems.at[index])
            for index in range(copies_ref.shape[0])
        ]
    )


def spread(pieces, count):
    piece = pieces.shape[1:]
    return pl.pallas_call(
        spread_kernel,
        out_shape=(
            jax.ShapeDtypeStruct(piece, jnp.float32),
            pltpu.HBM((count,) + piece, jnp.float32),
        ),
        out_specs=(
            pl.BlockSpec(memory_space=pltpu.VMEM),
            pl.BlockSpec(memory_space=pltpu.HBM),
        ),
        scratch_shapes=[pltpu.SemaphoreType.DMA((count,))],
        compiler_params=pltpu.CompilerParams(vmem_limit_bytes=16 * 2**20),
        name="spread",
    )(pieces)


def stage_kernel(*refs):
    terms, out_ref, total_ref, sem = refs[:-3], refs[-3], refs[-2], refs[-1]
    total = terms[0][...]
    for term in terms[1:]:
        total = total + term[...]
    total_ref[...] = total
    drain([pltpu.make_async_copy(total_ref, out_ref, sem)])


def stage(*terms):
    shape = jax.ShapeDtypeStruct(terms[0].shape, jnp.float32)
    return pl.pallas_call(
        stage_kernel,
        out_shape=pltpu.HBM(shape.shape, jnp.float32),
        out_specs=pl.BlockSpec(memory_space=pltpu.HBM),
        scratch_shapes=[pltpu.VMEM(shape.shape, jnp.float32), pltpu.SemaphoreType.DMA],
        compiler_params=pltpu.CompilerParams(vmem_limit_bytes=16 * 2**20),
        name="stage",
    )(*terms)


def order_cores(mine, other, core):
    even = jnp.where(core == 0, mine, other)
    odd = jnp.where(core == 0, other, mine)
    return jnp.stack([even, odd], axis=1).reshape((16,) + mine.shape[1:])


SIN_TERMS = (
    3.1415926535362906,
    -5.167712764624546,
    2.550163318947043,
    -0.5992521978220368,
    0.08205040179571269,
    -0.007028386383306818,
)
COS_TERMS = (
    0.9999999997799041,
    -4.9348021370788295,
    4.058709159556314,
    -1.335212003049894,
    0.23493731381328964,
    -0.024396324346460163,
)


def polynomial(terms, x):
    value = terms[-1]
    for term in terms[-2::-1]:
        value = value * x + term
    return value


def halves(value):
    high = value.astype(jnp.bfloat16)
    return high, (value - high.astype(jnp.float32)).astype(jnp.bfloat16)


def spread_start_kernel(start_ref, copies_ref, total_ref, sems):
    total_ref[:, :K] = start_ref[0]
    total_ref[:, K:] = start_ref[1]
    drain(
        [
            pltpu.make_async_copy(total_ref, copies_ref.at[index], sems.at[index])
            for index in range(8)
        ]
    )


def spread_start(start):
    return pl.pallas_call(
        spread_start_kernel,
        out_shape=pltpu.HBM((8, 32, 2 * K), jnp.float32),
        in_specs=[VMEM],
        out_specs=HBM,
        scratch_shapes=[pltpu.VMEM((32, 2 * K), jnp.float32), pltpu.SemaphoreType.DMA((8,))],
        compiler_params=pltpu.CompilerParams(vmem_limit_bytes=8 * 2**20),
        name="spread_start",
    )(start)


def steering_kernel(grid_ref, mics_ref, *refs):
    index = (
        grid_ref[:, 0:1] * mics_ref[0:1, :] + grid_ref[:, 1:2] * mics_ref[1:2, :]
    )
    turns = (index - jnp.round(index * (1.0 / MOD)) * float(MOD)) * (1.0 / MOD)
    square = turns * turns
    half_sine = turns * polynomial(SIN_TERMS, square)
    half_cosine = polynomial(COS_TERMS, square)
    cosine = 1.0 - 2.0 * half_sine * half_sine
    sine = 2.0 * half_sine * half_cosine
    for value, high_ref, low_ref in ((cosine, refs[-4], refs[-3]), (sine, refs[-2], refs[-1])):
        high_ref[...], low_ref[...] = halves(value)


def steering(grid, mics, first, count, before=()):
    block = pl.BlockSpec((256, 1024), lambda i: (i + first, 0))
    return pl.pallas_call(
        steering_kernel,
        grid=(count,),
        in_specs=[
            pl.BlockSpec((256, 2), lambda i: (i + first, 0)),
            pl.BlockSpec((2, 1024), lambda i: (0, 0)),
        ]
        + [HBM] * len(before),
        out_specs=(block,) * 4,
        out_shape=(pltpu.HBM((2048, 1024), jnp.bfloat16),) * 4,
        input_output_aliases={2 + index: index for index in range(len(before))},
        compiler_params=pltpu.CompilerParams(vmem_limit_bytes=24 * 2**20),
        cost_estimate=pl.CostEstimate(
            flops=45 * 256 * 1024 * count, bytes_accessed=8 * 256 * 1024 * count, transcendentals=0
        ),
        name="steering",
    )(grid, mics, *before)


def second_gram_kernel(raw_ref, inverse_ref, row_ref, copies_ref, slice_ref, sems):
    own = pl.multiple_of(row_ref[0] * 16, 16)
    raw = jnp.concatenate([raw_ref[:, :K], raw_ref[:, K:]], axis=0)
    second = dot_nt(raw, inverse_ref[...])
    turned_slice = dot_nt(inverse_ref[pl.ds(own, 16), :], raw)
    slice_ref[...] = dot(turned_slice, second)
    drain(
        [
            pltpu.make_async_copy(slice_ref, copies_ref.at[index], sems.at[index])
            for index in range(16)
        ]
    )


def second_gram_slice(raw, inverse, row):
    return pl.pallas_call(
        second_gram_kernel,
        out_shape=pltpu.HBM((16, 16, K), jnp.float32),
        in_specs=[VMEM, VMEM, SMEM],
        out_specs=HBM,
        scratch_shapes=[pltpu.VMEM((16, K), jnp.float32), pltpu.SemaphoreType.DMA((16,))],
        compiler_params=pltpu.CompilerParams(vmem_limit_bytes=24 * 2**20),
        cost_estimate=pl.CostEstimate(
            flops=2 * 1024 * K * (K + 32), bytes_accessed=2**21, transcendentals=0
        ),
        name="second_gram",
    )(raw, inverse, row)


def project_kernel(
    raw_ref, near_ref, far_ref, half_ref, cos_high, cos_low, sin_high, sin_low,
    out_ref, high_ref, low_ref, slots, sems,
):
    step = pl.program_id(0)

    @pl.when(step == 0)
    def _():
        lower = half_ref[0] == 0
        real_part = jnp.where(lower, raw_ref[:, :HALF], raw_ref[:, HALF:K])
        imag_part = jnp.where(lower, raw_ref[:, K : K + HALF], raw_ref[:, K + HALF :])
        for start, real, imag in (
            (0, real_part, imag_part),
            (512, near_ref[:, :HALF], near_ref[:, HALF:]),
            (768, far_ref[:, :HALF], far_ref[:, HALF:]),
        ):
            size = real.shape[0]
            for base, value in (
                (0, jnp.concatenate([real, imag], axis=1)),
                (1024, jnp.concatenate([-imag, real], axis=1)),
            ):
                high, low = halves(value)
                high_ref[base + start : base + start + size, :] = high
                low_ref[base + start : base + start + size, :] = low

    high = jnp.concatenate([cos_high[...], sin_high[...]], axis=1)
    low = jnp.concatenate([cos_low[...], sin_low[...]], axis=1)
    product = jnp.dot(high, high_ref[...], preferred_element_type=jnp.float32)
    product += jnp.dot(high, low_ref[...], preferred_element_type=jnp.float32)
    product += jnp.dot(low, high_ref[...], preferred_element_type=jnp.float32)
    slots[step] = product

    def copy(index):
        return pltpu.make_async_copy(slots.at[index], out_ref.at[index], sems.at[index])

    copy(step).start()

    @pl.when(step == 7)
    def _():
        for index in range(8):
            copy(index).wait()


def project(raw, near, far, half, steered):
    block = pl.BlockSpec((256, 1024), lambda i: (i, 0))
    return pl.pallas_call(
        project_kernel,
        grid=(8,),
        in_specs=[
            pl.BlockSpec((512, 512), lambda i: (0, 0)),
            pl.BlockSpec((256, 256), lambda i: (0, 0)),
            pl.BlockSpec((256, 256), lambda i: (0, 0)),
            SMEM,
        ]
        + [block] * 4,
        out_specs=HBM,
        out_shape=pltpu.HBM((8, 256, 256), jnp.float32),
        scratch_shapes=[
            pltpu.VMEM((2048, 256), jnp.bfloat16),
            pltpu.VMEM((2048, 256), jnp.bfloat16),
            pltpu.VMEM((8, 256, 256), jnp.float32),
            pltpu.SemaphoreType.DMA((8,)),
        ],
        compiler_params=pltpu.CompilerParams(vmem_limit_bytes=32 * 2**20),
        cost_estimate=pl.CostEstimate(
            flops=3 * 2 * 2048 * 2048 * 256, bytes_accessed=18 * 2**20, transcendentals=0
        ),
        name="project",
    )(raw, near, far, half, *steered)


def gram_of(block):
    return dot_tn(block[:, :K], block[:, :K]) + dot_tn(block[:, K:], block[:, K:])


def halves_of_vectors(block, half):
    lower = jnp.concatenate([block[:, :HALF], block[:, K : K + HALF]], axis=1)
    upper = jnp.concatenate([block[:, HALF:K], block[:, K + HALF :]], axis=1)
    return jnp.where(half == 0, lower, upper), jnp.where(half == 0, upper, lower)


def body(csm_real, csm_imag, start_block, mic_coords, grid_coords, bin_index):
    row = lax.axis_index("row")
    core = row % 2
    half = lax.axis_index("col") % 2
    reduced = ((bin_index * grid_coords) % MOD).astype(jnp.float32).T
    beside = lax.ppermute(mic_coords, "col", PAIR_SWAP).reshape(2, 8, 2, 32)
    near_mics = jnp.where(core == 0, beside[:, :, 0], beside[:, :, 1]).reshape(2, 256)
    far_mics = jnp.where(core == 0, beside[:, :, 1], beside[:, :, 0]).reshape(2, 256)
    mics = jnp.concatenate([mic_coords, near_mics, far_mics], axis=1).astype(jnp.float32)

    steered = steering(reduced, mics, 0, 1)
    mine = exchange(spread_start(start_block), "row", Z_GROUPS)
    mine, steered = lax.optimization_barrier((mine, steered))
    other = lax.ppermute(mine, "row", CORE_SWAP)
    start = order_cores(mine, other, core).reshape(512, 2 * K)
    first_partial = stage(dot(csm_real, start) + dot(csm_imag, turned(start)))

    steered = steering(reduced, mics, 1, 2, steered)
    first_pieces = exchange(first_partial.reshape(16, 32, 2 * K), "col")
    first_pieces, steered = lax.optimization_barrier((first_pieces, steered))

    steered = steering(reduced, mics, 3, 2, steered)
    first = exchange(spread(first_pieces, 16)[1], "col").reshape(512, 2 * K)
    first, steered = lax.optimization_barrier((first, steered))
    second_partial = dot_tn(csm_real, first) - dot_tn(csm_imag, turned(first))
    first_gram = gram_of(first).reshape(16, 16, K)
    first_gram = jnp.concatenate([first_gram[:, :8], first_gram[:, 8:]], axis=2)
    both = jnp.concatenate([second_partial.reshape(16, 32, 2 * K), first_gram], axis=1)
    both = both.reshape(8, 2, 40, 2 * K)
    kept = lax.dynamic_index_in_dim(both, core, 1, keepdims=False)
    sent = lax.dynamic_index_in_dim(both, 1 - core, 1, keepdims=False)
    pair = stage(kept, lax.ppermute(sent, "row", CORE_SWAP))

    steered = steering(reduced, mics, 5, 2, steered)
    pieces = exchange(pair, "row", Z_GROUPS)
    pieces, steered = lax.optimization_barrier((pieces, steered))
    own, spread_out = spread(pieces, 8)
    raw_rows = own[:32]

    steered = steering(reduced, mics, 7, 1, steered)
    beside_rows = lax.ppermute(halves_of_vectors(raw_rows, half)[1], "col", PAIR_SWAP)
    mine = exchange(spread_out, "row", Z_GROUPS)
    mine, beside_rows, steered = lax.optimization_barrier((mine, beside_rows, steered))
    other = lax.ppermute(mine, "row", CORE_SWAP)
    both = order_cores(mine, other, core)
    raw = both[:, :32].reshape(512, 2 * K)
    first_gram = jnp.concatenate([both[:, 32:, :K], both[:, 32:, K:]], axis=1).reshape(K, K)

    near = exchange(spread(beside_rows[None], 8)[1], "row", Z_GROUPS)
    first_upper, first_inverse = factor(first_gram)
    del first_upper
    near, first_inverse = lax.optimization_barrier((near, first_inverse))
    far = lax.ppermute(near, "row", CORE_SWAP)
    gram_pieces = exchange(second_gram_slice(raw, first_inverse, row.reshape(1)), "col")
    part = project(raw, near.reshape(256, K), far.reshape(256, K), half.reshape(1), steered)
    part, gram_pieces = lax.optimization_barrier((part, gram_pieces))
    pieces = exchange(part, "col", HALF_GROUPS)
    second_gram = lax.all_gather(jnp.sum(gram_pieces, axis=0), "row", axis=0, tiled=True)
    second_upper, second_inverse = factor(second_gram)
    diagonal = jnp.sum(jnp.where(jnp.eye(K, dtype=bool), second_upper, 0.0), axis=0)
    weights = diagonal ** (1.0 / NU)
    both_inverse = dot(second_inverse, first_inverse)
    rows = jnp.stack(
        [dot_nt(raw_rows[:, :K], first_inverse), dot_nt(raw_rows[:, K:], first_inverse)]
    )
    basis = jnp.stack([dot_nt(rows[0], second_inverse), dot_nt(rows[1], second_inverse)])
    summed = jnp.sum(pieces, axis=0)
    kept = jnp.where(half == 0, summed[:128], summed[128:])
    got = lax.ppermute(jnp.where(half == 0, summed[128:], summed[:128]), "col", PAIR_SWAP)
    lower = jnp.where(half == 0, kept, got)
    upper = jnp.where(half == 0, got, kept)
    real_part = dot_nt(jnp.concatenate([lower[:, :HALF], upper[:, :HALF]], axis=1), both_inverse)
    imag_part = dot_nt(jnp.concatenate([lower[:, HALF:], upper[:, HALF:]], axis=1), both_inverse)
    power = dot(real_part * real_part + imag_part * imag_part, weights) / jnp.sum(weights)
    return (basis, power**NU)


def solution(mesh):
    in_specs = (
        P("row", "col"),
        P("row", "col"),
        P(None, ("col", "row"), None),
        P(None, "col"),
        P(None, "row"),
        P(),
    )
    out_specs = (P(None, ("col", "row"), None), P(("row", "col")))
    return jax.shard_map(body, mesh=mesh, in_specs=in_specs, out_specs=out_specs, check_vma=False)
```

```python
import jax
import jax.numpy as jnp
from jax import lax
from jax.experimental import pallas as pl
from jax.experimental.pallas import tpu as pltpu
from jax.sharding import PartitionSpec as P

NU = 4
K = 256
MOD = 4093
HIGH = lax.Precision.HIGHEST

Z_GROUPS = [list(range(core, 16, 2)) for core in range(2)]
CORE_SWAP = [(index, index ^ 1) for index in range(16)]

PAIR_SWAP = [(index, index ^ 1) for index in range(16)]
HALF = K // 2
SMEM = pl.BlockSpec(memory_space=pltpu.SMEM)
HBM = pl.BlockSpec(memory_space=pltpu.HBM)
VMEM = pl.BlockSpec(memory_space=pltpu.VMEM)

PANEL = 64
MICRO = 16


def dot(a, b):
    return jnp.dot(a, b, precision=HIGH, preferred_element_type=jnp.float32)


def dot_tn(a, b):
    return lax.dot_general(
        a, b, (((0,), (0,)), ((), ())), precision=HIGH, preferred_element_type=jnp.float32
    )


def dot_nt(a, b):
    return lax.dot_general(
        a, b, (((1,), (1,)), ((), ())), precision=HIGH, preferred_element_type=jnp.float32
    )


def eliminate(work_ref, upper_ref, inverse_ref):
    rows = lax.broadcasted_iota(jnp.int32, (K, K), 0)
    cols = lax.broadcasted_iota(jnp.int32, (K, K), 1)
    work_ref[:, K:] = (rows == cols).astype(jnp.float32)
    panel_row = lax.broadcasted_iota(jnp.int32, (PANEL, 128), 0)
    for start in range(0, K, PANEL):
        low = (start // 128) * 128
        high = K + ((start + PANEL + 127) // 128) * 128
        width = high - low
        offset = start - low
        panel = work_ref[start : start + PANEL, low:high]
        for first in range(0, PANEL, MICRO):
            columns = [
                jnp.broadcast_to(
                    panel[:, offset + first + k : offset + first + k + 1], (PANEL, 128)
                )
                for k in range(MICRO)
            ]
            for k in range(MICRO):
                j = first + k
                scale = jnp.where(panel_row > j, columns[k] * (1.0 / columns[k][j : j + 1, :]), 0.0)
                for later in range(k + 1, MICRO):
                    columns[later] = columns[later] - scale * columns[later][j : j + 1, :]
                panel = (
                    panel
                    - jnp.concatenate([scale] * (width // 128), axis=1) * panel[j : j + 1, :]
                )
        square_row = lax.broadcasted_iota(jnp.int32, (PANEL, PANEL), 0)
        square_col = lax.broadcasted_iota(jnp.int32, (PANEL, PANEL), 1)
        pivots = jnp.sum(
            jnp.where(square_row == square_col, panel[:, offset : offset + PANEL], 0.0),
            axis=1,
            keepdims=True,
        )
        panel = panel * (1.0 / jnp.sqrt(pivots))
        if upper_ref is not None:
            panel_cols = lax.broadcasted_iota(jnp.int32, (PANEL, K - low), 1) + low
            panel_rows = lax.broadcasted_iota(jnp.int32, (PANEL, K - low), 0) + start
            upper_ref[start : start + PANEL, :] = jnp.zeros((PANEL, K), jnp.float32)
            upper_ref[start : start + PANEL, low:K] = jnp.where(
                panel_cols >= panel_rows, panel[:, : K - low], 0.0
            )
        inverse_ref[start : start + PANEL, :] = jnp.zeros((PANEL, K), jnp.float32)
        inverse_ref[start : start + PANEL, : high - K] = panel[:, K - low :]
        after = start + PANEL
        if after < K:
            update = dot_tn(panel[:, after - low : K - low], panel)
            work_ref[after:, low:high] = work_ref[after:, low:high] - update


def first_factor_kernel(mine_ref, other_ref, core_ref, inverse_ref, work_ref):
    own = core_ref[0]
    for z in range(8):
        for core in range(2):
            part = jnp.where(own == core, mine_ref[z, 32:, :], other_ref[z, 32:, :])
            start = (2 * z + core) * 16
            work_ref[start : start + 8, :K] = part[:, :K]
            work_ref[start + 8 : start + 16, :K] = part[:, K:]
    eliminate(work_ref, None, inverse_ref)


def first_factor(mine, other, core):
    return pl.pallas_call(
        first_factor_kernel,
        out_shape=jax.ShapeDtypeStruct((K, K), jnp.float32),
        in_specs=[VMEM, VMEM, SMEM],
        out_specs=VMEM,
        scratch_shapes=[pltpu.VMEM((K, 2 * K), jnp.float32)],
        compiler_params=pltpu.CompilerParams(vmem_limit_bytes=16 * 2**20),
        cost_estimate=pl.CostEstimate(
            flops=4 * K**3, bytes_accessed=12 * K * K, transcendentals=K
        ),
        name="first_factor",
    )(mine, other, core)


def second_factor_kernel(
    gram_ref, first_ref, rows_ref, basis_ref, both_ref, weights_ref, upper_ref, inverse_ref, work_ref
):
    work_ref[:, :K] = gram_ref[...]
    eliminate(work_ref, upper_ref, inverse_ref)
    rows = lax.broadcasted_iota(jnp.int32, (K, K), 0)
    cols = lax.broadcasted_iota(jnp.int32, (K, K), 1)
    diagonal = jnp.sum(jnp.where(rows == cols, upper_ref[...], 0.0), axis=0, keepdims=True)
    weights_ref[...] = jnp.sqrt(jnp.sqrt(diagonal))
    both_ref[...] = dot(inverse_ref[...], first_ref[...])
    raw = jnp.concatenate([rows_ref[:32, :K], rows_ref[:32, K:]], axis=0)
    basis = dot_nt(dot_nt(raw, first_ref[...]), inverse_ref[...])
    basis_ref[0] = basis[:32]
    basis_ref[1] = basis[32:]


def second_factor(gram, first_inverse, rows):
    return pl.pallas_call(
        second_factor_kernel,
        out_shape=(
            jax.ShapeDtypeStruct((2, 32, K), jnp.float32),
            jax.ShapeDtypeStruct((K, K), jnp.float32),
            jax.ShapeDtypeStruct((1, K), jnp.float32),
        ),
        scratch_shapes=[
            pltpu.VMEM((K, K), jnp.float32),
            pltpu.VMEM((K, K), jnp.float32),
            pltpu.VMEM((K, 2 * K), jnp.float32),
        ],
        compiler_params=pltpu.CompilerParams(vmem_limit_bytes=16 * 2**20),
        cost_estimate=pl.CostEstimate(
            flops=6 * K**3, bytes_accessed=16 * K * K, transcendentals=K
        ),
        name="second_factor",
    )(gram, first_inverse, rows)


def finish_kernel(pieces_ref, both_ref, weights_ref, beam_ref):
    lower = pieces_ref[0]
    upper = pieces_ref[1]
    for index in range(2, 16, 2):
        lower = lower + pieces_ref[index]
        upper = upper + pieces_ref[index + 1]
    real_part = jnp.concatenate([lower[:, :HALF], upper[:, :HALF]], axis=1)
    imag_part = jnp.concatenate([lower[:, HALF:], upper[:, HALF:]], axis=1)
    projected = dot_nt(jnp.concatenate([real_part, imag_part], axis=0), both_ref[...])
    square = projected * projected
    weights = weights_ref[...]
    power = dot_nt(weights, square[:128] + square[128:]) / jnp.sum(weights)
    power = power * power
    beam_ref[...] = power * power


def finish(pieces, both, weights):
    return pl.pallas_call(
        finish_kernel,
        out_shape=jax.ShapeDtypeStruct((1, 128), jnp.float32),
        compiler_params=pltpu.CompilerParams(vmem_limit_bytes=16 * 2**20),
        name="finish",
    )(pieces, both, weights)


def turned(block):
    return jnp.concatenate([-block[:, K:], block[:, :K]], axis=1)


def exchange(pieces, axis, groups=None):
    return lax.all_to_all(pieces, axis, 0, 0, tiled=True, axis_index_groups=groups)


def drain(copies):
    for copy in copies:
        copy.start()
    for copy in copies:
        copy.wait()


def spread_kernel(pieces_ref, total_ref, copies_ref, sems):
    total_ref[...] = jnp.sum(pieces_ref[...], axis=0)
    drain(
        [
            pltpu.make_async_copy(total_ref, copies_ref.at[index], sems.at[index])
            for index in range(copies_ref.shape[0])
        ]
    )


def spread(pieces, count):
    piece = pieces.shape[1:]
    return pl.pallas_call(
        spread_kernel,
        out_shape=(
            jax.ShapeDtypeStruct(piece, jnp.float32),
            pltpu.HBM((count,) + piece, jnp.float32),
        ),
        out_specs=(
            pl.BlockSpec(memory_space=pltpu.VMEM),
            pl.BlockSpec(memory_space=pltpu.HBM),
        ),
        scratch_shapes=[pltpu.SemaphoreType.DMA((count,))],
        compiler_params=pltpu.CompilerParams(vmem_limit_bytes=16 * 2**20),
        name="spread",
    )(pieces)


def stage_kernel(*refs):
    terms, out_ref, total_ref, sem = refs[:-3], refs[-3], refs[-2], refs[-1]
    total = terms[0][...]
    for term in terms[1:]:
        total = total + term[...]
    total_ref[...] = total
    drain([pltpu.make_async_copy(total_ref, out_ref, sem)])


def stage(*terms):
    shape = jax.ShapeDtypeStruct(terms[0].shape, jnp.float32)
    return pl.pallas_call(
        stage_kernel,
        out_shape=pltpu.HBM(shape.shape, jnp.float32),
        out_specs=pl.BlockSpec(memory_space=pltpu.HBM),
        scratch_shapes=[pltpu.VMEM(shape.shape, jnp.float32), pltpu.SemaphoreType.DMA],
        compiler_params=pltpu.CompilerParams(vmem_limit_bytes=16 * 2**20),
        name="stage",
    )(*terms)


def order_cores(mine, other, core):
    even = jnp.where(core == 0, mine, other)
    odd = jnp.where(core == 0, other, mine)
    return jnp.stack([even, odd], axis=1).reshape((16,) + mine.shape[1:])


SIN_TERMS = (
    3.1415926535362906,
    -5.167712764624546,
    2.550163318947043,
    -0.5992521978220368,
    0.08205040179571269,
    -0.007028386383306818,
)
COS_TERMS = (
    0.9999999997799041,
    -4.9348021370788295,
    4.058709159556314,
    -1.335212003049894,
    0.23493731381328964,
    -0.024396324346460163,
)


def polynomial(terms, x):
    value = terms[-1]
    for term in terms[-2::-1]:
        value = value * x + term
    return value


def halves(value):
    high = value.astype(jnp.bfloat16)
    return high, (value - high.astype(jnp.float32)).astype(jnp.bfloat16)


def spread_start_kernel(start_ref, copies_ref, total_ref, sems):
    total_ref[:, :K] = start_ref[0]
    total_ref[:, K:] = start_ref[1]
    drain(
        [
            pltpu.make_async_copy(total_ref, copies_ref.at[index], sems.at[index])
            for index in range(8)
        ]
    )


def spread_start(start):
    return pl.pallas_call(
        spread_start_kernel,
        out_shape=pltpu.HBM((8, 32, 2 * K), jnp.float32),
        in_specs=[VMEM],
        out_specs=HBM,
        scratch_shapes=[pltpu.VMEM((32, 2 * K), jnp.float32), pltpu.SemaphoreType.DMA((8,))],
        compiler_params=pltpu.CompilerParams(vmem_limit_bytes=8 * 2**20),
        name="spread_start",
    )(start)


def steering_kernel(grid_ref, mics_ref, *refs):
    index = (
        grid_ref[:, 0:1] * mics_ref[0:1, :] + grid_ref[:, 1:2] * mics_ref[1:2, :]
    )
    turns = (index - jnp.round(index * (1.0 / MOD)) * float(MOD)) * (1.0 / MOD)
    square = turns * turns
    half_sine = turns * polynomial(SIN_TERMS, square)
    half_cosine = polynomial(COS_TERMS, square)
    cosine = 1.0 - 2.0 * half_sine * half_sine
    sine = 2.0 * half_sine * half_cosine
    for value, high_ref, low_ref in ((cosine, refs[-4], refs[-3]), (sine, refs[-2], refs[-1])):
        high_ref[...], low_ref[...] = halves(value)


def steering(grid, mics, first, count, before=()):
    block = pl.BlockSpec((256, 1024), lambda i: (i + first, 0))
    return pl.pallas_call(
        steering_kernel,
        grid=(count,),
        in_specs=[
            pl.BlockSpec((256, 2), lambda i: (i + first, 0)),
            pl.BlockSpec((2, 1024), lambda i: (0, 0)),
        ]
        + [HBM] * len(before),
        out_specs=(block,) * 4,
        out_shape=(pltpu.HBM((2048, 1024), jnp.bfloat16),) * 4,
        input_output_aliases={2 + index: index for index in range(len(before))},
        compiler_params=pltpu.CompilerParams(vmem_limit_bytes=24 * 2**20),
        cost_estimate=pl.CostEstimate(
            flops=45 * 256 * 1024 * count, bytes_accessed=8 * 256 * 1024 * count, transcendentals=0
        ),
        name="steering",
    )(grid, mics, *before)


def second_gram_kernel(mine_ref, other_ref, inverse_ref, row_ref, copies_ref, slice_ref, sems):
    own = pl.multiple_of(row_ref[0] * 16, 16)
    raw = jnp.concatenate(
        [
            ref[:, :32, lanes].reshape(256, K)
            for ref in (mine_ref, other_ref)
            for lanes in (slice(0, K), slice(K, 2 * K))
        ],
        axis=0,
    )
    second = dot_nt(raw, inverse_ref[...])
    turned_slice = dot_nt(inverse_ref[pl.ds(own, 16), :], raw)
    slice_ref[...] = dot(turned_slice, second)
    drain(
        [
            pltpu.make_async_copy(slice_ref, copies_ref.at[index], sems.at[index])
            for index in range(16)
        ]
    )


def second_gram_slice(mine, other, inverse, row):
    return pl.pallas_call(
        second_gram_kernel,
        out_shape=pltpu.HBM((16, 16, K), jnp.float32),
        in_specs=[VMEM, VMEM, VMEM, SMEM],
        out_specs=HBM,
        scratch_shapes=[pltpu.VMEM((16, K), jnp.float32), pltpu.SemaphoreType.DMA((16,))],
        compiler_params=pltpu.CompilerParams(vmem_limit_bytes=24 * 2**20),
        cost_estimate=pl.CostEstimate(
            flops=2 * 1024 * K * (K + 32), bytes_accessed=2**21, transcendentals=0
        ),
        name="second_gram",
    )(mine, other, inverse, row)


def project_kernel(
    mine_ref, other_ref, near_ref, far_ref, half_ref, cos_high, cos_low, sin_high, sin_low,
    out_ref, high_ref, low_ref, slots, sems,
):
    step = pl.program_id(0)

    @pl.when(step == 0)
    def _():
        lower = half_ref[0] == 0
        sources = []
        for ref in (mine_ref, other_ref):
            parts = [ref[:, :32, lane : lane + HALF].reshape(256, HALF) for lane in range(0, 2 * K, HALF)]
            sources.append((jnp.where(lower, parts[0], parts[1]), jnp.where(lower, parts[2], parts[3])))
        for ref in (near_ref, far_ref):
            sources.append((ref[:, :, :HALF].reshape(256, HALF), ref[:, :, HALF:].reshape(256, HALF)))
        for index, (real, imag) in enumerate(sources):
            start, size = index * 256, 256
            for base, value in (
                (0, jnp.concatenate([real, imag], axis=1)),
                (1024, jnp.concatenate([-imag, real], axis=1)),
            ):
                high, low = halves(value)
                high_ref[base + start : base + start + size, :] = high
                low_ref[base + start : base + start + size, :] = low

    high = jnp.concatenate([cos_high[...], sin_high[...]], axis=1)
    low = jnp.concatenate([cos_low[...], sin_low[...]], axis=1)
    product = jnp.dot(high, high_ref[...], preferred_element_type=jnp.float32)
    product += jnp.dot(high, low_ref[...], preferred_element_type=jnp.float32)
    product += jnp.dot(low, high_ref[...], preferred_element_type=jnp.float32)
    slots[pl.ds(2 * step, 2)] = product.reshape(2, 128, 256)

    def copy(index):
        both = pl.ds(2 * index, 2)
        return pltpu.make_async_copy(slots.at[both], out_ref.at[both], sems.at[index])

    copy(step).start()

    @pl.when(step == 7)
    def _():
        for index in range(8):
            copy(index).wait()


def project(mine, other, near, far, half, steered):
    block = pl.BlockSpec((256, 1024), lambda i: (i, 0))
    return pl.pallas_call(
        project_kernel,
        grid=(8,),
        in_specs=[
            pl.BlockSpec((8, 40, 512), lambda i: (0, 0, 0)),
            pl.BlockSpec((8, 40, 512), lambda i: (0, 0, 0)),
            pl.BlockSpec((8, 32, 256), lambda i: (0, 0, 0)),
            pl.BlockSpec((8, 32, 256), lambda i: (0, 0, 0)),
            SMEM,
        ]
        + [block] * 4,
        out_specs=HBM,
        out_shape=pltpu.HBM((16, 128, 256), jnp.float32),
        scratch_shapes=[
            pltpu.VMEM((2048, 256), jnp.bfloat16),
            pltpu.VMEM((2048, 256), jnp.bfloat16),
            pltpu.VMEM((16, 128, 256), jnp.float32),
            pltpu.SemaphoreType.DMA((8,)),
        ],
        compiler_params=pltpu.CompilerParams(vmem_limit_bytes=32 * 2**20),
        cost_estimate=pl.CostEstimate(
            flops=3 * 2 * 2048 * 2048 * 256, bytes_accessed=18 * 2**20, transcendentals=0
        ),
        name="project",
    )(mine, other, near, far, half, *[pltpu.with_memory_space_constraint(x, pltpu.HBM) for x in steered])


def gram_of(block):
    return dot_tn(block[:, :K], block[:, :K]) + dot_tn(block[:, K:], block[:, K:])


def halves_beside(pieces, half):
    lower = jnp.concatenate([pieces[..., :HALF], pieces[..., K : K + HALF]], axis=-1)
    upper = jnp.concatenate([pieces[..., HALF:K], pieces[..., K + HALF :]], axis=-1)
    return jnp.where(half == 0, upper, lower)


def body(csm_real, csm_imag, start_block, mic_coords, grid_coords, bin_index):
    row = lax.axis_index("row")
    core = row % 2
    half = lax.axis_index("col") % 2
    reduced = ((bin_index * grid_coords) % MOD).astype(jnp.float32).T
    beside = lax.ppermute(mic_coords, "col", PAIR_SWAP)
    both = jnp.stack([mic_coords, beside], axis=1).reshape(2, 2, 8, 2, 32)
    even, odd = both[:, :, :, 0], both[:, :, :, 1]
    mics = jnp.stack([jnp.where(core == 0, even, odd), jnp.where(core == 0, odd, even)], axis=2)
    mics = mics.reshape(2, 1024).astype(jnp.float32)

    steered = steering(reduced, mics, 0, 1)
    mine = exchange(spread_start(start_block), "row", Z_GROUPS)
    mine, steered = lax.optimization_barrier((mine, steered))
    other = lax.ppermute(mine, "row", CORE_SWAP)
    start = order_cores(mine, other, core).reshape(512, 2 * K)
    first_partial = stage(dot(csm_real, start) + dot(csm_imag, turned(start)))

    steered = steering(reduced, mics, 1, 2, steered)
    first_pieces = exchange(first_partial.reshape(16, 32, 2 * K), "col")
    first_pieces, steered = lax.optimization_barrier((first_pieces, steered))

    steered = steering(reduced, mics, 3, 2, steered)
    first = exchange(spread(first_pieces, 16)[1], "col").reshape(512, 2 * K)
    first, steered = lax.optimization_barrier((first, steered))
    second_partial = dot_tn(csm_real, first) - dot_tn(csm_imag, turned(first))
    first_gram = gram_of(first).reshape(16, 16, K)
    first_gram = jnp.concatenate([first_gram[:, :8], first_gram[:, 8:]], axis=2)
    both = jnp.concatenate([second_partial.reshape(16, 32, 2 * K), first_gram], axis=1)
    both = both.reshape(8, 2, 40, 2 * K)
    kept = lax.dynamic_index_in_dim(both, core, 1, keepdims=False)
    sent = lax.dynamic_index_in_dim(both, 1 - core, 1, keepdims=False)
    pair = stage(kept, lax.ppermute(sent, "row", CORE_SWAP))

    steered = steering(reduced, mics, 5, 2, steered)
    pieces = exchange(pair, "row", Z_GROUPS)
    pieces, steered = lax.optimization_barrier((pieces, steered))
    own, spread_out = spread(pieces, 8)

    steered = steering(reduced, mics, 7, 1, steered)
    mine = exchange(spread_out, "row", Z_GROUPS)
    mine, steered = lax.optimization_barrier((mine, steered))
    other = lax.ppermute(mine, "row", CORE_SWAP)
    near = lax.ppermute(halves_beside(mine[:, :32], half), "col", PAIR_SWAP)
    far = lax.ppermute(near, "row", CORE_SWAP)
    first_inverse = first_factor(mine, other, core.reshape(1))
    gram_pieces = exchange(second_gram_slice(mine, other, first_inverse, row.reshape(1)), "col")
    part = project(mine, other, near, far, half.reshape(1), steered)
    part, gram_pieces = lax.optimization_barrier((part, gram_pieces))
    pieces = exchange(part, "col")
    second_gram = lax.all_gather(jnp.sum(gram_pieces, axis=0), "row", axis=0, tiled=True)
    basis, both_inverse, weights = second_factor(second_gram, first_inverse, own)
    return (basis, finish(pieces, both_inverse, weights).reshape(128))


def solution(mesh):
    in_specs = (
        P("row", "col"),
        P("row", "col"),
        P(None, ("col", "row"), None),
        P(None, "col"),
        P(None, "row"),
        P(),
    )
    out_specs = (P(None, ("col", "row"), None), P(("row", "col")))
    return jax.shard_map(body, mesh=mesh, in_specs=in_specs, out_specs=out_specs, check_vma=False)
```

```python
import jax
import jax.numpy as jnp
from jax import lax
from jax.experimental import pallas as pl
from jax.experimental.pallas import tpu as pltpu
from jax.sharding import PartitionSpec as P

NU = 4
K = 256
MOD = 4093
HIGH = lax.Precision.HIGHEST

Z_GROUPS = [list(range(core, 16, 2)) for core in range(2)]
CORE_SWAP = [(index, index ^ 1) for index in range(16)]

ALONG_X = [[(index, index ^ flip) for index in range(16)] for flip in range(4)]
POINT_GROUPS = [[index for index in range(16) if index // 2 % 2 == part] for part in range(2)]
HALF = K // 2
SMEM = pl.BlockSpec(memory_space=pltpu.SMEM)
HBM = pl.BlockSpec(memory_space=pltpu.HBM)
VMEM = pl.BlockSpec(memory_space=pltpu.VMEM)

PANEL = 64
MICRO = 16


def dot(a, b):
    return jnp.dot(a, b, precision=HIGH, preferred_element_type=jnp.float32)


def dot_tn(a, b):
    return lax.dot_general(
        a, b, (((0,), (0,)), ((), ())), precision=HIGH, preferred_element_type=jnp.float32
    )


def dot_nt(a, b):
    return lax.dot_general(
        a, b, (((1,), (1,)), ((), ())), precision=HIGH, preferred_element_type=jnp.float32
    )


def eliminate(work_ref, upper_ref, inverse_ref):
    rows = lax.broadcasted_iota(jnp.int32, (K, K), 0)
    cols = lax.broadcasted_iota(jnp.int32, (K, K), 1)
    work_ref[:, K:] = (rows == cols).astype(jnp.float32)
    panel_row = lax.broadcasted_iota(jnp.int32, (PANEL, 128), 0)
    for start in range(0, K, PANEL):
        low = (start // 128) * 128
        high = K + ((start + PANEL + 127) // 128) * 128
        width = high - low
        offset = start - low
        panel = work_ref[start : start + PANEL, low:high]
        for first in range(0, PANEL, MICRO):
            columns = [
                jnp.broadcast_to(
                    panel[:, offset + first + k : offset + first + k + 1], (PANEL, 128)
                )
                for k in range(MICRO)
            ]
            for k in range(MICRO):
                j = first + k
                scale = jnp.where(panel_row > j, columns[k] * (1.0 / columns[k][j : j + 1, :]), 0.0)
                for later in range(k + 1, MICRO):
                    columns[later] = columns[later] - scale * columns[later][j : j + 1, :]
                panel = (
                    panel
                    - jnp.concatenate([scale] * (width // 128), axis=1) * panel[j : j + 1, :]
                )
        square_row = lax.broadcasted_iota(jnp.int32, (PANEL, PANEL), 0)
        square_col = lax.broadcasted_iota(jnp.int32, (PANEL, PANEL), 1)
        pivots = jnp.sum(
            jnp.where(square_row == square_col, panel[:, offset : offset + PANEL], 0.0),
            axis=1,
            keepdims=True,
        )
        panel = panel * (1.0 / jnp.sqrt(pivots))
        if upper_ref is not None:
            panel_cols = lax.broadcasted_iota(jnp.int32, (PANEL, K - low), 1) + low
            panel_rows = lax.broadcasted_iota(jnp.int32, (PANEL, K - low), 0) + start
            upper_ref[start : start + PANEL, :] = jnp.zeros((PANEL, K), jnp.float32)
            upper_ref[start : start + PANEL, low:K] = jnp.where(
                panel_cols >= panel_rows, panel[:, : K - low], 0.0
            )
        inverse_ref[start : start + PANEL, :] = jnp.zeros((PANEL, K), jnp.float32)
        inverse_ref[start : start + PANEL, : high - K] = panel[:, K - low :]
        after = start + PANEL
        if after < K:
            update = dot_tn(panel[:, after - low : K - low], panel)
            work_ref[after:, low:high] = work_ref[after:, low:high] - update


def first_factor_kernel(mine_ref, other_ref, core_ref, inverse_ref, work_ref):
    own = core_ref[0]
    for z in range(8):
        for core in range(2):
            part = jnp.where(own == core, mine_ref[z, 32:, :], other_ref[z, 32:, :])
            start = (2 * z + core) * 16
            work_ref[start : start + 8, :K] = part[:, :K]
            work_ref[start + 8 : start + 16, :K] = part[:, K:]
    eliminate(work_ref, None, inverse_ref)


def first_factor(mine, other, core):
    return pl.pallas_call(
        first_factor_kernel,
        out_shape=jax.ShapeDtypeStruct((K, K), jnp.float32),
        in_specs=[VMEM, VMEM, SMEM],
        out_specs=VMEM,
        scratch_shapes=[pltpu.VMEM((K, 2 * K), jnp.float32)],
        compiler_params=pltpu.CompilerParams(vmem_limit_bytes=16 * 2**20),
        cost_estimate=pl.CostEstimate(
            flops=4 * K**3, bytes_accessed=12 * K * K, transcendentals=K
        ),
        name="first_factor",
    )(mine, other, core)


def second_factor_kernel(
    gram_ref, first_ref, rows_ref, basis_ref, both_ref, weights_ref, upper_ref, inverse_ref, work_ref
):
    work_ref[:, :K] = gram_ref[...]
    eliminate(work_ref, upper_ref, inverse_ref)
    rows = lax.broadcasted_iota(jnp.int32, (K, K), 0)
    cols = lax.broadcasted_iota(jnp.int32, (K, K), 1)
    diagonal = jnp.sum(jnp.where(rows == cols, upper_ref[...], 0.0), axis=0, keepdims=True)
    weights_ref[...] = jnp.sqrt(jnp.sqrt(diagonal))
    both_ref[...] = dot(inverse_ref[...], first_ref[...])
    raw = jnp.concatenate([rows_ref[:32, :K], rows_ref[:32, K:]], axis=0)
    basis = dot_nt(dot_nt(raw, first_ref[...]), inverse_ref[...])
    basis_ref[0] = basis[:32]
    basis_ref[1] = basis[32:]


def second_factor(gram, first_inverse, rows):
    return pl.pallas_call(
        second_factor_kernel,
        out_shape=(
            jax.ShapeDtypeStruct((2, 32, K), jnp.float32),
            jax.ShapeDtypeStruct((K, K), jnp.float32),
            jax.ShapeDtypeStruct((1, K), jnp.float32),
        ),
        scratch_shapes=[
            pltpu.VMEM((K, K), jnp.float32),
            pltpu.VMEM((K, K), jnp.float32),
            pltpu.VMEM((K, 2 * K), jnp.float32),
        ],
        compiler_params=pltpu.CompilerParams(vmem_limit_bytes=16 * 2**20),
        cost_estimate=pl.CostEstimate(
            flops=6 * K**3, bytes_accessed=16 * K * K, transcendentals=K
        ),
        name="second_factor",
    )(gram, first_inverse, rows)


def finish_kernel(pieces_ref, both_ref, weights_ref, beam_ref):
    lower = pieces_ref[0]
    upper = pieces_ref[1]
    for index in range(2, 8, 2):
        lower = lower + pieces_ref[index]
        upper = upper + pieces_ref[index + 1]
    real_part = jnp.concatenate([lower[:, :HALF], upper[:, :HALF]], axis=1)
    imag_part = jnp.concatenate([lower[:, HALF:], upper[:, HALF:]], axis=1)
    projected = dot_nt(jnp.concatenate([real_part, imag_part], axis=0), both_ref[...])
    square = projected * projected
    weights = weights_ref[...]
    power = dot_nt(weights, square[:128] + square[128:]) / jnp.sum(weights)
    power = power * power
    beam_ref[...] = power * power


def finish(pieces, both, weights):
    return pl.pallas_call(
        finish_kernel,
        out_shape=jax.ShapeDtypeStruct((1, 128), jnp.float32),
        compiler_params=pltpu.CompilerParams(vmem_limit_bytes=16 * 2**20),
        name="finish",
    )(pieces, both, weights)


def turned(block):
    return jnp.concatenate([-block[:, K:], block[:, :K]], axis=1)


def exchange(pieces, axis, groups=None):
    return lax.all_to_all(pieces, axis, 0, 0, tiled=True, axis_index_groups=groups)


def drain(copies):
    for copy in copies:
        copy.start()
    for copy in copies:
        copy.wait()


def spread_kernel(pieces_ref, total_ref, copies_ref, sems):
    total_ref[...] = jnp.sum(pieces_ref[...], axis=0)
    drain(
        [
            pltpu.make_async_copy(total_ref, copies_ref.at[index], sems.at[index])
            for index in range(copies_ref.shape[0])
        ]
    )


def spread(pieces, count):
    piece = pieces.shape[1:]
    return pl.pallas_call(
        spread_kernel,
        out_shape=(
            jax.ShapeDtypeStruct(piece, jnp.float32),
            pltpu.HBM((count,) + piece, jnp.float32),
        ),
        out_specs=(
            pl.BlockSpec(memory_space=pltpu.VMEM),
            pl.BlockSpec(memory_space=pltpu.HBM),
        ),
        scratch_shapes=[pltpu.SemaphoreType.DMA((count,))],
        compiler_params=pltpu.CompilerParams(vmem_limit_bytes=16 * 2**20),
        name="spread",
    )(pieces)


def stage_kernel(*refs):
    terms, out_ref, total_ref, sem = refs[:-3], refs[-3], refs[-2], refs[-1]
    total = terms[0][...]
    for term in terms[1:]:
        total = total + term[...]
    total_ref[...] = total
    drain([pltpu.make_async_copy(total_ref, out_ref, sem)])


def stage(*terms):
    shape = jax.ShapeDtypeStruct(terms[0].shape, jnp.float32)
    return pl.pallas_call(
        stage_kernel,
        out_shape=pltpu.HBM(shape.shape, jnp.float32),
        out_specs=pl.BlockSpec(memory_space=pltpu.HBM),
        scratch_shapes=[pltpu.VMEM(shape.shape, jnp.float32), pltpu.SemaphoreType.DMA],
        compiler_params=pltpu.CompilerParams(vmem_limit_bytes=16 * 2**20),
        name="stage",
    )(*terms)


def order_cores(mine, other, core):
    even = jnp.where(core == 0, mine, other)
    odd = jnp.where(core == 0, other, mine)
    return jnp.stack([even, odd], axis=1).reshape((16,) + mine.shape[1:])


SIN_TERMS = (
    3.1415926535362906,
    -5.167712764624546,
    2.550163318947043,
    -0.5992521978220368,
    0.08205040179571269,
    -0.007028386383306818,
)
COS_TERMS = (
    0.9999999997799041,
    -4.9348021370788295,
    4.058709159556314,
    -1.335212003049894,
    0.23493731381328964,
    -0.024396324346460163,
)


def polynomial(terms, x):
    value = terms[-1]
    for term in terms[-2::-1]:
        value = value * x + term
    return value


def halves(value):
    high = value.astype(jnp.bfloat16)
    return high, (value - high.astype(jnp.float32)).astype(jnp.bfloat16)


def spread_start_kernel(start_ref, copies_ref, total_ref, sems):
    total_ref[:, :K] = start_ref[0]
    total_ref[:, K:] = start_ref[1]
    drain(
        [
            pltpu.make_async_copy(total_ref, copies_ref.at[index], sems.at[index])
            for index in range(8)
        ]
    )


def spread_start(start):
    return pl.pallas_call(
        spread_start_kernel,
        out_shape=pltpu.HBM((8, 32, 2 * K), jnp.float32),
        in_specs=[VMEM],
        out_specs=HBM,
        scratch_shapes=[pltpu.VMEM((32, 2 * K), jnp.float32), pltpu.SemaphoreType.DMA((8,))],
        compiler_params=pltpu.CompilerParams(vmem_limit_bytes=8 * 2**20),
        name="spread_start",
    )(start)


def steering_kernel(grid_ref, mics_ref, *refs):
    index = (
        grid_ref[:, 0:1] * mics_ref[0:1, :] + grid_ref[:, 1:2] * mics_ref[1:2, :]
    )
    turns = (index - jnp.round(index * (1.0 / MOD)) * float(MOD)) * (1.0 / MOD)
    square = turns * turns
    half_sine = turns * polynomial(SIN_TERMS, square)
    half_cosine = polynomial(COS_TERMS, square)
    cosine = 1.0 - 2.0 * half_sine * half_sine
    sine = 2.0 * half_sine * half_cosine
    for value, high_ref, low_ref in ((cosine, refs[-4], refs[-3]), (sine, refs[-2], refs[-1])):
        high_ref[...], low_ref[...] = halves(value)


def steering(grid, mics, first, count, before=()):
    block = pl.BlockSpec((256, 1024), lambda i: ((i + first) // 2, (i + first) % 2))
    return pl.pallas_call(
        steering_kernel,
        grid=(count,),
        in_specs=[
            pl.BlockSpec((256, 2), lambda i: ((i + first) // 2, 0)),
            pl.BlockSpec((2, 1024), lambda i: (0, (i + first) % 2)),
        ]
        + [HBM] * len(before),
        out_specs=(block,) * 4,
        out_shape=(pltpu.HBM((1024, 2048), jnp.bfloat16),) * 4,
        input_output_aliases={2 + index: index for index in range(len(before))},
        compiler_params=pltpu.CompilerParams(vmem_limit_bytes=24 * 2**20),
        cost_estimate=pl.CostEstimate(
            flops=45 * 256 * 1024 * count, bytes_accessed=8 * 256 * 1024 * count, transcendentals=0
        ),
        name="steering",
    )(grid, mics, *before)


def second_gram_kernel(mine_ref, other_ref, inverse_ref, row_ref, copies_ref, slice_ref, sems):
    own = pl.multiple_of(row_ref[0] * 16, 16)
    raw = jnp.concatenate(
        [
            ref[:, :32, lanes].reshape(256, K)
            for ref in (mine_ref, other_ref)
            for lanes in (slice(0, K), slice(K, 2 * K))
        ],
        axis=0,
    )
    second = dot_nt(raw, inverse_ref[...])
    turned_slice = dot_nt(inverse_ref[pl.ds(own, 16), :], raw)
    slice_ref[...] = dot(turned_slice, second)
    drain(
        [
            pltpu.make_async_copy(slice_ref, copies_ref.at[index], sems.at[index])
            for index in range(16)
        ]
    )


def second_gram_slice(mine, other, inverse, row):
    return pl.pallas_call(
        second_gram_kernel,
        out_shape=pltpu.HBM((16, 16, K), jnp.float32),
        in_specs=[VMEM, VMEM, VMEM, SMEM],
        out_specs=HBM,
        scratch_shapes=[pltpu.VMEM((16, K), jnp.float32), pltpu.SemaphoreType.DMA((16,))],
        compiler_params=pltpu.CompilerParams(vmem_limit_bytes=24 * 2**20),
        cost_estimate=pl.CostEstimate(
            flops=2 * 1024 * K * (K + 32), bytes_accessed=2**21, transcendentals=0
        ),
        name="second_gram",
    )(mine, other, inverse, row)


def project_kernel(half_ref, *refs):
    raw_refs, beside_refs = refs[:2], refs[2:8]
    cos_high, cos_low, sin_high, sin_low = refs[8:12]
    out_ref, high_ref, low_ref, slots, sems = refs[12:]
    step = pl.program_id(0)

    @pl.when(step == 0)
    def _():
        lower = half_ref[0] == 0
        sources = []
        for ref in raw_refs:
            parts = [
                ref[:, :32, lane : lane + HALF].reshape(256, HALF) for lane in range(0, 2 * K, HALF)
            ]
            sources.append(
                (jnp.where(lower, parts[0], parts[1]), jnp.where(lower, parts[2], parts[3]))
            )
        for ref in beside_refs:
            sources.append((ref[:, :, :HALF].reshape(256, HALF), ref[:, :, HALF:].reshape(256, HALF)))
        for index, (real, imag) in enumerate(sources):
            start = index * 256
            for base, value in (
                (0, jnp.concatenate([real, imag], axis=1)),
                (2048, jnp.concatenate([-imag, real], axis=1)),
            ):
                high, low = halves(value)
                high_ref[base + start : base + start + 256, :] = high
                low_ref[base + start : base + start + 256, :] = low

    high = jnp.concatenate([cos_high[...], sin_high[...]], axis=1)
    low = jnp.concatenate([cos_low[...], sin_low[...]], axis=1)
    product = jnp.dot(high, high_ref[...], preferred_element_type=jnp.float32)
    product += jnp.dot(high, low_ref[...], preferred_element_type=jnp.float32)
    product += jnp.dot(low, high_ref[...], preferred_element_type=jnp.float32)
    slots[pl.ds(2 * step, 2)] = product.reshape(2, 128, 256)

    def copy(index):
        both = pl.ds(2 * index, 2)
        return pltpu.make_async_copy(slots.at[both], out_ref.at[both], sems.at[index])

    copy(step).start()

    @pl.when(step == 3)
    def _():
        for index in range(4):
            copy(index).wait()


def project(half, raw, beside, steered):
    block = pl.BlockSpec((256, 2048), lambda i: (i, 0))
    return pl.pallas_call(
        project_kernel,
        grid=(4,),
        in_specs=[SMEM]
        + [pl.BlockSpec((8, 40, 512), lambda i: (0, 0, 0))] * 2
        + [pl.BlockSpec((8, 32, 256), lambda i: (0, 0, 0))] * 6
        + [block] * 4,
        out_specs=HBM,
        out_shape=pltpu.HBM((8, 128, 256), jnp.float32),
        scratch_shapes=[
            pltpu.VMEM((4096, 256), jnp.bfloat16),
            pltpu.VMEM((4096, 256), jnp.bfloat16),
            pltpu.VMEM((8, 128, 256), jnp.float32),
            pltpu.SemaphoreType.DMA((4,)),
        ],
        compiler_params=pltpu.CompilerParams(vmem_limit_bytes=40 * 2**20),
        cost_estimate=pl.CostEstimate(
            flops=3 * 2 * 1024 * 4096 * 256, bytes_accessed=18 * 2**20, transcendentals=0
        ),
        name="project",
    )(half, *raw, *beside, *[pltpu.with_memory_space_constraint(x, pltpu.HBM) for x in steered])


def gram_of(block):
    return dot_tn(block[:, :K], block[:, :K]) + dot_tn(block[:, K:], block[:, K:])


def half_of_vectors(pieces, half):
    lower = jnp.concatenate([pieces[..., :HALF], pieces[..., K : K + HALF]], axis=-1)
    upper = jnp.concatenate([pieces[..., HALF:K], pieces[..., K + HALF :]], axis=-1)
    return jnp.where(half == 0, lower, upper)


def body(csm_real, csm_imag, start_block, mic_coords, grid_coords, bin_index):
    row = lax.axis_index("row")
    core = row % 2
    col = lax.axis_index("col")
    half = col % 2
    points = grid_coords.reshape(2, 4, 2, 256)
    points = jnp.where(col // 2 % 2 == 0, points[:, :, 0], points[:, :, 1]).reshape(2, 1024)
    reduced = ((bin_index * points) % MOD).astype(jnp.float32).T
    places = [mic_coords] + [lax.ppermute(mic_coords, "col", ALONG_X[flip]) for flip in (1, 2, 3)]
    places = jnp.stack(places, axis=1).reshape(2, 4, 8, 2, 32)
    even, odd = places[:, :, :, 0], places[:, :, :, 1]
    mics = jnp.stack([jnp.where(core == 0, even, odd), jnp.where(core == 0, odd, even)], axis=2)
    mics = mics.reshape(2, 2048).astype(jnp.float32)

    steered = steering(reduced, mics, 0, 1)
    mine = exchange(spread_start(start_block), "row", Z_GROUPS)
    mine, steered = lax.optimization_barrier((mine, steered))
    other = lax.ppermute(mine, "row", CORE_SWAP)
    start = order_cores(mine, other, core).reshape(512, 2 * K)
    first_partial = stage(dot(csm_real, start) + dot(csm_imag, turned(start)))

    steered = steering(reduced, mics, 1, 2, steered)
    first_pieces = exchange(first_partial.reshape(16, 32, 2 * K), "col")
    first_pieces, steered = lax.optimization_barrier((first_pieces, steered))

    steered = steering(reduced, mics, 3, 2, steered)
    first = exchange(spread(first_pieces, 16)[1], "col").reshape(512, 2 * K)
    first, steered = lax.optimization_barrier((first, steered))
    second_partial = dot_tn(csm_real, first) - dot_tn(csm_imag, turned(first))
    first_gram = gram_of(first).reshape(16, 16, K)
    first_gram = jnp.concatenate([first_gram[:, :8], first_gram[:, 8:]], axis=2)
    both = jnp.concatenate([second_partial.reshape(16, 32, 2 * K), first_gram], axis=1)
    both = both.reshape(8, 2, 40, 2 * K)
    kept = lax.dynamic_index_in_dim(both, core, 1, keepdims=False)
    sent = lax.dynamic_index_in_dim(both, 1 - core, 1, keepdims=False)
    pair = stage(kept, lax.ppermute(sent, "row", CORE_SWAP))

    steered = steering(reduced, mics, 5, 2, steered)
    pieces = exchange(pair, "row", Z_GROUPS)
    pieces, steered = lax.optimization_barrier((pieces, steered))
    own, spread_out = spread(pieces, 8)

    steered = steering(reduced, mics, 7, 1, steered)
    mine = exchange(spread_out, "row", Z_GROUPS)
    mine, steered = lax.optimization_barrier((mine, steered))
    other = lax.ppermute(mine, "row", CORE_SWAP)
    taken = half_of_vectors(mine[:, :32], half)
    given = half_of_vectors(mine[:, :32], 1 - half)
    near = [
        lax.ppermute(taken if flip == 2 else given, "col", ALONG_X[flip]) for flip in (1, 2, 3)
    ]
    first_inverse = first_factor(mine, other, core.reshape(1))
    near, first_inverse = lax.optimization_barrier((near, first_inverse))
    far = [lax.ppermute(block, "row", CORE_SWAP) for block in near]
    beside = [block for both in zip(near, far) for block in both]
    gram_pieces = exchange(second_gram_slice(mine, other, first_inverse, row.reshape(1)), "col")
    part = project(half.reshape(1), (mine, other), beside, steered)
    part, gram_pieces = lax.optimization_barrier((part, gram_pieces))
    pieces = exchange(part, "col", POINT_GROUPS)
    second_gram = lax.all_gather(jnp.sum(gram_pieces, axis=0), "row", axis=0, tiled=True)
    basis, both_inverse, weights = second_factor(second_gram, first_inverse, own)
    return (basis, finish(pieces, both_inverse, weights).reshape(128))


def solution(mesh):
    in_specs = (
        P("row", "col"),
        P("row", "col"),
        P(None, ("col", "row"), None),
        P(None, "col"),
        P(None, "row"),
        P(),
    )
    out_specs = (P(None, ("col", "row"), None), P(("row", "col")))
    return jax.shard_map(body, mesh=mesh, in_specs=in_specs, out_specs=out_specs, check_vma=False)
```

```python
import jax
import jax.numpy as jnp
from jax import lax
from jax.experimental import pallas as pl
from jax.experimental.pallas import tpu as pltpu
from jax.sharding import PartitionSpec as P

NU = 4
K = 256
MOD = 4093
HIGH = lax.Precision.HIGHEST

Z_GROUPS = [list(range(core, 16, 2)) for core in range(2)]
CORE_SWAP = [(index, index ^ 1) for index in range(16)]

ALONG_X = [[(index, index ^ flip) for index in range(16)] for flip in range(4)]
POINT_GROUPS = [[index for index in range(16) if index // 2 % 2 == part] for part in range(2)]
HALF = K // 2
SMEM = pl.BlockSpec(memory_space=pltpu.SMEM)
HBM = pl.BlockSpec(memory_space=pltpu.HBM)
VMEM = pl.BlockSpec(memory_space=pltpu.VMEM)

PANEL = 64
MICRO = 16


def dot(a, b):
    return jnp.dot(a, b, precision=HIGH, preferred_element_type=jnp.float32)


def dot_tn(a, b):
    return lax.dot_general(
        a, b, (((0,), (0,)), ((), ())), precision=HIGH, preferred_element_type=jnp.float32
    )


def dot_nt(a, b):
    return lax.dot_general(
        a, b, (((1,), (1,)), ((), ())), precision=HIGH, preferred_element_type=jnp.float32
    )


def eliminate(work_ref, upper_ref, inverse_ref):
    rows = lax.broadcasted_iota(jnp.int32, (K, K), 0)
    cols = lax.broadcasted_iota(jnp.int32, (K, K), 1)
    work_ref[:, K:] = (rows == cols).astype(jnp.float32)
    chunk_row = lax.broadcasted_iota(jnp.int32, (8, 128), 0)
    for start in range(0, K, PANEL):
        low = (start // 128) * 128
        high = K + ((start + PANEL + 127) // 128) * 128
        width = high - low
        offset = start - low
        chunks = [work_ref[at : at + 8, low:high] for at in range(start, start + PANEL, 8)]
        for first in range(0, PANEL, MICRO):
            columns = [
                {
                    at: jnp.broadcast_to(
                        chunks[at][:, offset + first + k : offset + first + k + 1], (8, 128)
                    )
                    for at in range(first // 8, PANEL // 8)
                }
                for k in range(MICRO)
            ]
            for k in range(MICRO):
                j = first + k
                own, line = j // 8, j % 8
                reciprocal = 1.0 / columns[k][own][line : line + 1, :]
                pivot_row = chunks[own][line : line + 1, :]
                entries = [columns[later][own][line : line + 1, :] for later in range(MICRO)]
                for at in range(own, PANEL // 8):
                    scale = columns[k][at] * reciprocal
                    if at == own:
                        scale = jnp.where(chunk_row > line, scale, 0.0)
                    for later in range(k + 1, MICRO):
                        columns[later][at] = columns[later][at] - scale * entries[later]
                    chunks[at] = (
                        chunks[at] - jnp.concatenate([scale] * (width // 128), axis=1) * pivot_row
                    )
        panel = jnp.concatenate(chunks, axis=0)
        square_row = lax.broadcasted_iota(jnp.int32, (PANEL, PANEL), 0)
        square_col = lax.broadcasted_iota(jnp.int32, (PANEL, PANEL), 1)
        pivots = jnp.sum(
            jnp.where(square_row == square_col, panel[:, offset : offset + PANEL], 0.0),
            axis=1,
            keepdims=True,
        )
        panel = panel * (1.0 / jnp.sqrt(pivots))
        if upper_ref is not None:
            panel_cols = lax.broadcasted_iota(jnp.int32, (PANEL, K - low), 1) + low
            panel_rows = lax.broadcasted_iota(jnp.int32, (PANEL, K - low), 0) + start
            upper_ref[start : start + PANEL, :] = jnp.zeros((PANEL, K), jnp.float32)
            upper_ref[start : start + PANEL, low:K] = jnp.where(
                panel_cols >= panel_rows, panel[:, : K - low], 0.0
            )
        inverse_ref[start : start + PANEL, :] = jnp.zeros((PANEL, K), jnp.float32)
        inverse_ref[start : start + PANEL, : high - K] = panel[:, K - low :]
        after = start + PANEL
        if after < K:
            update = dot_tn(panel[:, after - low : K - low], panel)
            work_ref[after:, low:high] = work_ref[after:, low:high] - update


def first_factor_kernel(mine_ref, other_ref, core_ref, inverse_ref, work_ref):
    own = core_ref[0]
    for z in range(8):
        for core in range(2):
            part = jnp.where(own == core, mine_ref[z, 32:, :], other_ref[z, 32:, :])
            start = (2 * z + core) * 16
            work_ref[start : start + 8, :K] = part[:, :K]
            work_ref[start + 8 : start + 16, :K] = part[:, K:]
    eliminate(work_ref, None, inverse_ref)


def first_factor(mine, other, core):
    return pl.pallas_call(
        first_factor_kernel,
        out_shape=jax.ShapeDtypeStruct((K, K), jnp.float32),
        in_specs=[VMEM, VMEM, SMEM],
        out_specs=VMEM,
        scratch_shapes=[pltpu.VMEM((K, 2 * K), jnp.float32)],
        compiler_params=pltpu.CompilerParams(vmem_limit_bytes=16 * 2**20),
        cost_estimate=pl.CostEstimate(
            flops=4 * K**3, bytes_accessed=12 * K * K, transcendentals=K
        ),
        name="first_factor",
    )(mine, other, core)


def second_factor_kernel(
    gram_ref, first_ref, rows_ref, basis_ref, both_ref, weights_ref, upper_ref, inverse_ref, work_ref
):
    work_ref[:, :K] = gram_ref[...]
    eliminate(work_ref, upper_ref, inverse_ref)
    rows = lax.broadcasted_iota(jnp.int32, (K, K), 0)
    cols = lax.broadcasted_iota(jnp.int32, (K, K), 1)
    diagonal = jnp.sum(jnp.where(rows == cols, upper_ref[...], 0.0), axis=0, keepdims=True)
    weights_ref[...] = jnp.sqrt(jnp.sqrt(diagonal))
    both_ref[...] = dot(inverse_ref[...], first_ref[...])
    raw = jnp.concatenate([rows_ref[:32, :K], rows_ref[:32, K:]], axis=0)
    basis = dot_nt(dot_nt(raw, first_ref[...]), inverse_ref[...])
    basis_ref[0] = basis[:32]
    basis_ref[1] = basis[32:]


def second_factor(gram, first_inverse, rows):
    return pl.pallas_call(
        second_factor_kernel,
        out_shape=(
            jax.ShapeDtypeStruct((2, 32, K), jnp.float32),
            jax.ShapeDtypeStruct((K, K), jnp.float32),
            jax.ShapeDtypeStruct((1, K), jnp.float32),
        ),
        scratch_shapes=[
            pltpu.VMEM((K, K), jnp.float32),
            pltpu.VMEM((K, K), jnp.float32),
            pltpu.VMEM((K, 2 * K), jnp.float32),
        ],
        compiler_params=pltpu.CompilerParams(vmem_limit_bytes=16 * 2**20),
        cost_estimate=pl.CostEstimate(
            flops=6 * K**3, bytes_accessed=16 * K * K, transcendentals=K
        ),
        name="second_factor",
    )(gram, first_inverse, rows)


def finish_kernel(pieces_ref, both_ref, weights_ref, beam_ref):
    lower = pieces_ref[0]
    upper = pieces_ref[1]
    for index in range(2, 8, 2):
        lower = lower + pieces_ref[index]
        upper = upper + pieces_ref[index + 1]
    real_part = jnp.concatenate([lower[:, :HALF], upper[:, :HALF]], axis=1)
    imag_part = jnp.concatenate([lower[:, HALF:], upper[:, HALF:]], axis=1)
    projected = dot_nt(jnp.concatenate([real_part, imag_part], axis=0), both_ref[...])
    square = projected * projected
    weights = weights_ref[...]
    power = dot_nt(weights, square[:128] + square[128:]) / jnp.sum(weights)
    power = power * power
    beam_ref[...] = power * power


def finish(pieces, both, weights):
    return pl.pallas_call(
        finish_kernel,
        out_shape=jax.ShapeDtypeStruct((1, 128), jnp.float32),
        compiler_params=pltpu.CompilerParams(vmem_limit_bytes=16 * 2**20),
        name="finish",
    )(pieces, both, weights)


def turned(block):
    return jnp.concatenate([-block[:, K:], block[:, :K]], axis=1)


def exchange(pieces, axis, groups=None):
    return lax.all_to_all(pieces, axis, 0, 0, tiled=True, axis_index_groups=groups)


def drain(copies):
    for copy in copies:
        copy.start()
    for copy in copies:
        copy.wait()


def spread_kernel(pieces_ref, total_ref, copies_ref, sems):
    total_ref[...] = jnp.sum(pieces_ref[...], axis=0)
    drain(
        [
            pltpu.make_async_copy(total_ref, copies_ref.at[index], sems.at[index])
            for index in range(copies_ref.shape[0])
        ]
    )


def spread(pieces, count):
    piece = pieces.shape[1:]
    return pl.pallas_call(
        spread_kernel,
        out_shape=(
            jax.ShapeDtypeStruct(piece, jnp.float32),
            pltpu.HBM((count,) + piece, jnp.float32),
        ),
        out_specs=(
            pl.BlockSpec(memory_space=pltpu.VMEM),
            pl.BlockSpec(memory_space=pltpu.HBM),
        ),
        scratch_shapes=[pltpu.SemaphoreType.DMA((count,))],
        compiler_params=pltpu.CompilerParams(vmem_limit_bytes=16 * 2**20),
        name="spread",
    )(pieces)


def thirds(value):
    high = value.astype(jnp.bfloat16)
    rest = value - high.astype(jnp.float32)
    middle = rest.astype(jnp.bfloat16)
    return high, middle, (rest - middle.astype(jnp.float32)).astype(jnp.bfloat16)


def full_dot(left, parts):
    high, middle, low = thirds(left)
    terms = (
        (low, parts[0]), (high, parts[2]), (middle, parts[1]),
        (middle, parts[0]), (high, parts[1]), (high, parts[0]),
    )
    total = None
    for one, other in terms:
        term = jnp.dot(one, other, preferred_element_type=jnp.float32)
        total = term if total is None else total + term
    return total


def first_product_kernel(
    real_ref, imag_ref, mine_ref, other_ref, core_ref, out_ref, start_ref, parts_ref, rows_ref, sems
):
    core = core_ref[0]
    for z in range(8):
        start_ref[2 * z + core] = mine_ref[z]
        start_ref[2 * z + 1 - core] = other_ref[z]
    start = start_ref[...].reshape(512, 2 * K)
    for base, value in ((0, start), (512, turned(start))):
        for index, part in enumerate(thirds(value)):
            parts_ref[index, base : base + 512, :] = part
    parts = [parts_ref[index] for index in range(3)]
    copies = []
    for block in range(4):
        at = block * 128
        tile = jnp.concatenate([real_ref[at : at + 128, :], imag_ref[at : at + 128, :]], axis=1)
        rows_ref[block * 4 : block * 4 + 4] = full_dot(tile, parts).reshape(4, 32, 2 * K)
        copies.append(
            pltpu.make_async_copy(
                rows_ref.at[block * 4 : block * 4 + 4],
                out_ref.at[block * 4 : block * 4 + 4],
                sems.at[block],
            )
        )
        copies[-1].start()
    for copy in copies:
        copy.wait()


def first_product(real, imag, mine, other, core):
    return pl.pallas_call(
        first_product_kernel,
        out_shape=pltpu.HBM((16, 32, 2 * K), jnp.float32),
        in_specs=[VMEM] * 4 + [SMEM],
        out_specs=HBM,
        scratch_shapes=[
            pltpu.VMEM((16, 32, 2 * K), jnp.float32),
            pltpu.VMEM((3, 1024, 2 * K), jnp.bfloat16),
            pltpu.VMEM((16, 32, 2 * K), jnp.float32),
            pltpu.SemaphoreType.DMA((4,)),
        ],
        compiler_params=pltpu.CompilerParams(vmem_limit_bytes=32 * 2**20),
        cost_estimate=pl.CostEstimate(
            flops=12 * 512 * 1024 * 512, bytes_accessed=5 * 2**20, transcendentals=0
        ),
        name="first_product",
    )(real, imag, mine, other, core)


def sent_product_kernel(
    real_ref, imag_ref, first_ref, core_ref, out_ref, kept_ref, parts_out, parts_ref, gram_ref
):
    first = first_ref[...].reshape(512, 2 * K)
    for base, value in ((0, first), (512, -turned(first))):
        for index, part in enumerate(thirds(value)):
            parts_ref[index, base : base + 512, :] = part
    parts_out[...] = parts_ref[...]
    rows = jnp.concatenate([first[:, :K], first[:, K:]], axis=0)
    gram_ref[...] = dot_tn(rows, rows)
    core = core_ref[0]
    for z in range(8):
        for which, target, at in ((core, kept_ref, 0), (1 - core, out_ref, 32)):
            start = pl.multiple_of(z * 32 + which * 16, 16)
            target[z, at : at + 8, :K] = gram_ref[pl.ds(start, 8), :]
            target[z, at : at + 8, K:] = gram_ref[pl.ds(start + 8, 8), :]
    parts = [parts_ref[index] for index in range(3)]
    for block in range(2):
        at = slice(block * 4, block * 4 + 4)
        tile = jnp.concatenate(
            [real_ref[at].reshape(128, 512), imag_ref[at].reshape(128, 512)], axis=1
        )
        out_ref[at, :32, :] = full_dot(tile, parts).reshape(4, 32, 2 * K)


def sent_product(real, imag, first, core):
    return pl.pallas_call(
        sent_product_kernel,
        out_shape=(
            jax.ShapeDtypeStruct((8, 40, 2 * K), jnp.float32),
            jax.ShapeDtypeStruct((8, 8, 2 * K), jnp.float32),
            jax.ShapeDtypeStruct((3, 1024, 2 * K), jnp.bfloat16),
        ),
        in_specs=[VMEM] * 3 + [SMEM],
        out_specs=(VMEM,) * 3,
        scratch_shapes=[
            pltpu.VMEM((3, 1024, 2 * K), jnp.bfloat16),
            pltpu.VMEM((K, K), jnp.float32),
        ],
        compiler_params=pltpu.CompilerParams(vmem_limit_bytes=32 * 2**20),
        cost_estimate=pl.CostEstimate(
            flops=12 * 256 * 1024 * 512, bytes_accessed=5 * 2**20, transcendentals=0
        ),
        name="sent_product",
    )(real, imag, first, core)


def kept_product_kernel(real_ref, imag_ref, parts_ref, gram_ref, out_ref):
    out_ref[:, 32:, :] = gram_ref[...]
    parts = [parts_ref[index] for index in range(3)]
    for block in range(2):
        at = slice(block * 4, block * 4 + 4)
        tile = jnp.concatenate(
            [real_ref[at].reshape(128, 512), imag_ref[at].reshape(128, 512)], axis=1
        )
        out_ref[at, :32, :] = full_dot(tile, parts).reshape(4, 32, 2 * K)


def kept_product(real, imag, parts, gram):
    return pl.pallas_call(
        kept_product_kernel,
        out_shape=jax.ShapeDtypeStruct((8, 40, 2 * K), jnp.float32),
        in_specs=[VMEM] * 4,
        out_specs=VMEM,
        compiler_params=pltpu.CompilerParams(vmem_limit_bytes=32 * 2**20),
        cost_estimate=pl.CostEstimate(
            flops=12 * 256 * 1024 * 512, bytes_accessed=5 * 2**20, transcendentals=0
        ),
        name="kept_product",
    )(real, imag, parts, gram)


def stage_kernel(*refs):
    terms, out_ref, total_ref, sem = refs[:-3], refs[-3], refs[-2], refs[-1]
    total = terms[0][...]
    for term in terms[1:]:
        total = total + term[...]
    total_ref[...] = total
    drain([pltpu.make_async_copy(total_ref, out_ref, sem)])


def stage(*terms):
    shape = jax.ShapeDtypeStruct(terms[0].shape, jnp.float32)
    return pl.pallas_call(
        stage_kernel,
        out_shape=pltpu.HBM(shape.shape, jnp.float32),
        out_specs=pl.BlockSpec(memory_space=pltpu.HBM),
        scratch_shapes=[pltpu.VMEM(shape.shape, jnp.float32), pltpu.SemaphoreType.DMA],
        compiler_params=pltpu.CompilerParams(vmem_limit_bytes=16 * 2**20),
        name="stage",
    )(*terms)


SIN_TERMS = (
    3.1415926535362906,
    -5.167712764624546,
    2.550163318947043,
    -0.5992521978220368,
    0.08205040179571269,
    -0.007028386383306818,
)
COS_TERMS = (
    0.9999999997799041,
    -4.9348021370788295,
    4.058709159556314,
    -1.335212003049894,
    0.23493731381328964,
    -0.024396324346460163,
)


def polynomial(terms, x):
    value = terms[-1]
    for term in terms[-2::-1]:
        value = value * x + term
    return value


def halves(value):
    high = value.astype(jnp.bfloat16)
    return high, (value - high.astype(jnp.float32)).astype(jnp.bfloat16)


def spread_start_kernel(start_ref, copies_ref, total_ref, sems):
    total_ref[:, :K] = start_ref[0]
    total_ref[:, K:] = start_ref[1]
    drain(
        [
            pltpu.make_async_copy(total_ref, copies_ref.at[index], sems.at[index])
            for index in range(8)
        ]
    )


def spread_start(start):
    return pl.pallas_call(
        spread_start_kernel,
        out_shape=pltpu.HBM((8, 32, 2 * K), jnp.float32),
        in_specs=[VMEM],
        out_specs=HBM,
        scratch_shapes=[pltpu.VMEM((32, 2 * K), jnp.float32), pltpu.SemaphoreType.DMA((8,))],
        compiler_params=pltpu.CompilerParams(vmem_limit_bytes=8 * 2**20),
        name="spread_start",
    )(start)


def steering_kernel(grid_ref, mics_ref, *refs):
    index = (
        grid_ref[:, 0:1] * mics_ref[0:1, :] + grid_ref[:, 1:2] * mics_ref[1:2, :]
    )
    turns = (index - jnp.round(index * (1.0 / MOD)) * float(MOD)) * (1.0 / MOD)
    square = turns * turns
    half_sine = turns * polynomial(SIN_TERMS, square)
    half_cosine = polynomial(COS_TERMS, square)
    cosine = 1.0 - 2.0 * half_sine * half_sine
    sine = 2.0 * half_sine * half_cosine
    for value, high_ref, low_ref in ((cosine, refs[-4], refs[-3]), (sine, refs[-2], refs[-1])):
        high_ref[...], low_ref[...] = halves(value)


def steering(grid, mics, first, count, before=()):
    block = pl.BlockSpec((256, 1024), lambda i: ((i + first) // 2, (i + first) % 2))
    return pl.pallas_call(
        steering_kernel,
        grid=(count,),
        in_specs=[
            pl.BlockSpec((256, 2), lambda i: ((i + first) // 2, 0)),
            pl.BlockSpec((2, 1024), lambda i: (0, (i + first) % 2)),
        ]
        + [HBM] * len(before),
        out_specs=(block,) * 4,
        out_shape=(pltpu.HBM((1024, 2048), jnp.bfloat16),) * 4,
        input_output_aliases={2 + index: index for index in range(len(before))},
        compiler_params=pltpu.CompilerParams(vmem_limit_bytes=24 * 2**20),
        cost_estimate=pl.CostEstimate(
            flops=45 * 256 * 1024 * count, bytes_accessed=8 * 256 * 1024 * count, transcendentals=0
        ),
        name="steering",
    )(grid, mics, *before)


def second_gram_kernel(mine_ref, other_ref, inverse_ref, row_ref, copies_ref, slice_ref, sems):
    own = pl.multiple_of(row_ref[0] * 16, 16)
    raw = jnp.concatenate(
        [
            ref[:, :32, lanes].reshape(256, K)
            for ref in (mine_ref, other_ref)
            for lanes in (slice(0, K), slice(K, 2 * K))
        ],
        axis=0,
    )
    second = dot_nt(raw, inverse_ref[...])
    turned_slice = dot_nt(inverse_ref[pl.ds(own, 16), :], raw)
    slice_ref[...] = dot(turned_slice, second)
    drain(
        [
            pltpu.make_async_copy(slice_ref, copies_ref.at[index], sems.at[index])
            for index in range(16)
        ]
    )


def second_gram_slice(mine, other, inverse, row):
    return pl.pallas_call(
        second_gram_kernel,
        out_shape=pltpu.HBM((16, 16, K), jnp.float32),
        in_specs=[VMEM, VMEM, VMEM, SMEM],
        out_specs=HBM,
        scratch_shapes=[pltpu.VMEM((16, K), jnp.float32), pltpu.SemaphoreType.DMA((16,))],
        compiler_params=pltpu.CompilerParams(vmem_limit_bytes=24 * 2**20),
        cost_estimate=pl.CostEstimate(
            flops=2 * 1024 * K * (K + 32), bytes_accessed=2**21, transcendentals=0
        ),
        name="second_gram",
    )(mine, other, inverse, row)


def project_kernel(half_ref, *refs):
    raw_refs, beside_refs = refs[:2], refs[2:8]
    cos_high, cos_low, sin_high, sin_low = refs[8:12]
    out_ref, high_ref, low_ref, slots, sems = refs[12:]
    step = pl.program_id(0)

    @pl.when(step == 0)
    def _():
        lower = half_ref[0] == 0
        sources = []
        for ref in raw_refs:
            parts = [
                ref[:, :32, lane : lane + HALF].reshape(256, HALF) for lane in range(0, 2 * K, HALF)
            ]
            sources.append(
                (jnp.where(lower, parts[0], parts[1]), jnp.where(lower, parts[2], parts[3]))
            )
        for ref in beside_refs:
            sources.append((ref[:, :, :HALF].reshape(256, HALF), ref[:, :, HALF:].reshape(256, HALF)))
        for index, (real, imag) in enumerate(sources):
            start = index * 256
            for base, value in (
                (0, jnp.concatenate([real, imag], axis=1)),
                (2048, jnp.concatenate([-imag, real], axis=1)),
            ):
                high, low = halves(value)
                high_ref[base + start : base + start + 256, :] = high
                low_ref[base + start : base + start + 256, :] = low

    high = jnp.concatenate([cos_high[...], sin_high[...]], axis=1)
    low = jnp.concatenate([cos_low[...], sin_low[...]], axis=1)
    product = jnp.dot(high, high_ref[...], preferred_element_type=jnp.float32)
    product += jnp.dot(high, low_ref[...], preferred_element_type=jnp.float32)
    product += jnp.dot(low, high_ref[...], preferred_element_type=jnp.float32)
    slots[pl.ds(2 * step, 2)] = product.reshape(2, 128, 256)

    def copy(index):
        both = pl.ds(2 * index, 2)
        return pltpu.make_async_copy(slots.at[both], out_ref.at[both], sems.at[index])

    copy(step).start()

    @pl.when(step == 3)
    def _():
        for index in range(4):
            copy(index).wait()


def project(half, raw, beside, steered):
    block = pl.BlockSpec((256, 2048), lambda i: (i, 0))
    return pl.pallas_call(
        project_kernel,
        grid=(4,),
        in_specs=[SMEM]
        + [pl.BlockSpec((8, 40, 512), lambda i: (0, 0, 0))] * 2
        + [pl.BlockSpec((8, 32, 256), lambda i: (0, 0, 0))] * 6
        + [block] * 4,
        out_specs=HBM,
        out_shape=pltpu.HBM((8, 128, 256), jnp.float32),
        scratch_shapes=[
            pltpu.VMEM((4096, 256), jnp.bfloat16),
            pltpu.VMEM((4096, 256), jnp.bfloat16),
            pltpu.VMEM((8, 128, 256), jnp.float32),
            pltpu.SemaphoreType.DMA((4,)),
        ],
        compiler_params=pltpu.CompilerParams(vmem_limit_bytes=40 * 2**20),
        cost_estimate=pl.CostEstimate(
            flops=3 * 2 * 1024 * 4096 * 256, bytes_accessed=18 * 2**20, transcendentals=0
        ),
        name="project",
    )(half, *raw, *beside, *[pltpu.with_memory_space_constraint(x, pltpu.HBM) for x in steered])


def half_of_vectors(pieces, half):
    lower = jnp.concatenate([pieces[..., :HALF], pieces[..., K : K + HALF]], axis=-1)
    upper = jnp.concatenate([pieces[..., HALF:K], pieces[..., K + HALF :]], axis=-1)
    return jnp.where(half == 0, lower, upper)


def by_core(tile, core):
    rows = tile.T.reshape(8, 2, 32, 512)
    return (
        jnp.where(core == 0, rows[:, 0], rows[:, 1]),
        jnp.where(core == 0, rows[:, 1], rows[:, 0]),
    )


def body(csm_real, csm_imag, start_block, mic_coords, grid_coords, bin_index):
    row = lax.axis_index("row")
    core = row % 2
    own_core = core.reshape(1)
    col = lax.axis_index("col")
    half = col % 2
    points = grid_coords.reshape(2, 4, 2, 256)
    points = jnp.where(col // 2 % 2 == 0, points[:, :, 0], points[:, :, 1]).reshape(2, 1024)
    reduced = ((bin_index * points) % MOD).astype(jnp.float32).T

    start, mic_coords = lax.optimization_barrier((spread_start(start_block), mic_coords))
    mine = exchange(start, "row", Z_GROUPS)
    places = [mic_coords] + [lax.ppermute(mic_coords, "col", ALONG_X[flip]) for flip in (1, 2, 3)]
    places = jnp.stack(places, axis=1).reshape(2, 4, 8, 2, 32)
    even, odd = places[:, :, :, 0], places[:, :, :, 1]
    mics = jnp.stack([jnp.where(core == 0, even, odd), jnp.where(core == 0, odd, even)], axis=2)
    mics = mics.reshape(2, 2048).astype(jnp.float32)
    kept_real, sent_real = by_core(csm_real, core)
    kept_imag, sent_imag = by_core(csm_imag, core)
    mine, mics, kept_real, kept_imag, sent_real, sent_imag = lax.optimization_barrier(
        (mine, mics, kept_real, kept_imag, sent_real, sent_imag)
    )
    other = lax.ppermute(mine, "row", CORE_SWAP)
    first_partial = first_product(csm_real, csm_imag, mine, other, own_core)

    steered = steering(reduced, mics, 0, 3)
    first_pieces = exchange(first_partial, "col")
    first_pieces, steered = lax.optimization_barrier((first_pieces, steered))

    steered = steering(reduced, mics, 3, 2, steered)
    first = exchange(spread(first_pieces, 16)[1], "col")
    first, steered = lax.optimization_barrier((first, steered))
    sent, gram_rows, parts = sent_product(sent_real, sent_imag, first, own_core)
    got = lax.ppermute(sent, "row", CORE_SWAP)
    kept = kept_product(kept_real, kept_imag, parts, gram_rows)
    pair = stage(kept, got)

    steered = steering(reduced, mics, 5, 2, steered)
    pieces = exchange(pair, "row", Z_GROUPS)
    pieces, steered = lax.optimization_barrier((pieces, steered))
    own, spread_out = spread(pieces, 8)

    steered = steering(reduced, mics, 7, 1, steered)
    mine = exchange(spread_out, "row", Z_GROUPS)
    mine, steered = lax.optimization_barrier((mine, steered))
    other = lax.ppermute(mine, "row", CORE_SWAP)
    taken = half_of_vectors(mine[:, :32], half)
    given = half_of_vectors(mine[:, :32], 1 - half)
    near = [
        lax.ppermute(taken if flip == 2 else given, "col", ALONG_X[flip]) for flip in (1, 2, 3)
    ]
    first_inverse = first_factor(mine, other, own_core)
    gram_copies = second_gram_slice(mine, other, first_inverse, row.reshape(1))
    near, gram_copies = lax.optimization_barrier((near, gram_copies))
    far = [lax.ppermute(block, "row", CORE_SWAP) for block in near]
    beside = [block for both in zip(near, far) for block in both]
    gram_pieces = exchange(gram_copies, "col")
    part = project(half.reshape(1), (mine, other), beside, steered)
    part, gram_pieces = lax.optimization_barrier((part, gram_pieces))
    pieces = exchange(part, "col", POINT_GROUPS)
    second_gram = lax.all_gather(jnp.sum(gram_pieces, axis=0), "row", axis=0, tiled=True)
    basis, both_inverse, weights = second_factor(second_gram, first_inverse, own)
    return (basis, finish(pieces, both_inverse, weights).reshape(128))


def solution(mesh):
    in_specs = (
        P("row", "col"),
        P("row", "col"),
        P(None, ("col", "row"), None),
        P(None, "col"),
        P(None, "row"),
        P(),
    )
    out_specs = (P(None, ("col", "row"), None), P(("row", "col")))
    return jax.shard_map(body, mesh=mesh, in_specs=in_specs, out_specs=out_specs, check_vma=False)
```

```python
import jax
import jax.numpy as jnp
from jax import lax
from jax.experimental import pallas as pl
from jax.experimental.pallas import tpu as pltpu
from jax.sharding import PartitionSpec as P

NU = 4
K = 256
MOD = 4093
HIGH = lax.Precision.HIGHEST

Z_GROUPS = [list(range(core, 16, 2)) for core in range(2)]
CORE_SWAP = [(index, index ^ 1) for index in range(16)]

ALONG_X = [[(index, index ^ flip) for index in range(16)] for flip in range(4)]
POINT_GROUPS = [[index for index in range(16) if index // 2 % 2 == part] for part in range(2)]
HALF = K // 2
SMEM = pl.BlockSpec(memory_space=pltpu.SMEM)
HBM = pl.BlockSpec(memory_space=pltpu.HBM)
VMEM = pl.BlockSpec(memory_space=pltpu.VMEM)

PANEL = 64
MICRO = 16


def dot(a, b):
    return jnp.dot(a, b, precision=HIGH, preferred_element_type=jnp.float32)


def dot_tn(a, b):
    return lax.dot_general(
        a, b, (((0,), (0,)), ((), ())), precision=HIGH, preferred_element_type=jnp.float32
    )


def dot_nt(a, b):
    return lax.dot_general(
        a, b, (((1,), (1,)), ((), ())), precision=HIGH, preferred_element_type=jnp.float32
    )


def eliminate(work_ref, upper_ref, inverse_ref):
    rows = lax.broadcasted_iota(jnp.int32, (K, K), 0)
    cols = lax.broadcasted_iota(jnp.int32, (K, K), 1)
    work_ref[:, K:] = (rows == cols).astype(jnp.float32)
    panel_row = lax.broadcasted_iota(jnp.int32, (PANEL, 128), 0)
    for start in range(0, K, PANEL):
        low = (start // 128) * 128
        high = K + ((start + PANEL + 127) // 128) * 128
        width = high - low
        offset = start - low
        panel = work_ref[start : start + PANEL, low:high]
        for first in range(0, PANEL, MICRO):
            columns = [
                jnp.broadcast_to(
                    panel[:, offset + first + k : offset + first + k + 1], (PANEL, 128)
                )
                for k in range(MICRO)
            ]
            for k in range(MICRO):
                j = first + k
                scale = jnp.where(panel_row > j, columns[k] * (1.0 / columns[k][j : j + 1, :]), 0.0)
                for later in range(k + 1, MICRO):
                    columns[later] = columns[later] - scale * columns[later][j : j + 1, :]
                panel = (
                    panel
                    - jnp.concatenate([scale] * (width // 128), axis=1) * panel[j : j + 1, :]
                )
        square_row = lax.broadcasted_iota(jnp.int32, (PANEL, PANEL), 0)
        square_col = lax.broadcasted_iota(jnp.int32, (PANEL, PANEL), 1)
        pivots = jnp.sum(
            jnp.where(square_row == square_col, panel[:, offset : offset + PANEL], 0.0),
            axis=1,
            keepdims=True,
        )
        panel = panel * (1.0 / jnp.sqrt(pivots))
        if upper_ref is not None:
            panel_cols = lax.broadcasted_iota(jnp.int32, (PANEL, K - low), 1) + low
            panel_rows = lax.broadcasted_iota(jnp.int32, (PANEL, K - low), 0) + start
            upper_ref[start : start + PANEL, :] = jnp.zeros((PANEL, K), jnp.float32)
            upper_ref[start : start + PANEL, low:K] = jnp.where(
                panel_cols >= panel_rows, panel[:, : K - low], 0.0
            )
        inverse_ref[start : start + PANEL, :] = jnp.zeros((PANEL, K), jnp.float32)
        inverse_ref[start : start + PANEL, : high - K] = panel[:, K - low :]
        after = start + PANEL
        if after < K:
            update = dot_tn(panel[:, after - low : K - low], panel)
            work_ref[after:, low:high] = work_ref[after:, low:high] - update


def first_factor_kernel(mine_ref, other_ref, core_ref, inverse_ref, work_ref):
    own = core_ref[0]
    for z in range(8):
        for core in range(2):
            part = jnp.where(own == core, mine_ref[z, 32:, :], other_ref[z, 32:, :])
            start = (2 * z + core) * 16
            work_ref[start : start + 8, :K] = part[:, :K]
            work_ref[start + 8 : start + 16, :K] = part[:, K:]
    eliminate(work_ref, None, inverse_ref)


def first_factor(mine, other, core):
    return pl.pallas_call(
        first_factor_kernel,
        out_shape=jax.ShapeDtypeStruct((K, K), jnp.float32),
        in_specs=[VMEM, VMEM, SMEM],
        out_specs=VMEM,
        scratch_shapes=[pltpu.VMEM((K, 2 * K), jnp.float32)],
        compiler_params=pltpu.CompilerParams(vmem_limit_bytes=16 * 2**20),
        cost_estimate=pl.CostEstimate(
            flops=4 * K**3, bytes_accessed=12 * K * K, transcendentals=K
        ),
        name="first_factor",
    )(mine, other, core)


def second_factor_kernel(
    gram_ref, first_ref, rows_ref, basis_ref, both_ref, weights_ref, upper_ref, inverse_ref, work_ref
):
    work_ref[:, :K] = gram_ref[...]
    eliminate(work_ref, upper_ref, inverse_ref)
    rows = lax.broadcasted_iota(jnp.int32, (K, K), 0)
    cols = lax.broadcasted_iota(jnp.int32, (K, K), 1)
    diagonal = jnp.sum(jnp.where(rows == cols, upper_ref[...], 0.0), axis=0, keepdims=True)
    weights_ref[...] = jnp.sqrt(jnp.sqrt(diagonal))
    both_ref[...] = dot(inverse_ref[...], first_ref[...])
    raw = jnp.concatenate([rows_ref[:32, :K], rows_ref[:32, K:]], axis=0)
    basis = dot_nt(dot_nt(raw, first_ref[...]), inverse_ref[...])
    basis_ref[0] = basis[:32]
    basis_ref[1] = basis[32:]


def second_factor(gram, first_inverse, rows):
    return pl.pallas_call(
        second_factor_kernel,
        out_shape=(
            jax.ShapeDtypeStruct((2, 32, K), jnp.float32),
            jax.ShapeDtypeStruct((K, K), jnp.float32),
            jax.ShapeDtypeStruct((1, K), jnp.float32),
        ),
        scratch_shapes=[
            pltpu.VMEM((K, K), jnp.float32),
            pltpu.VMEM((K, K), jnp.float32),
            pltpu.VMEM((K, 2 * K), jnp.float32),
        ],
        compiler_params=pltpu.CompilerParams(vmem_limit_bytes=16 * 2**20),
        cost_estimate=pl.CostEstimate(
            flops=6 * K**3, bytes_accessed=16 * K * K, transcendentals=K
        ),
        name="second_factor",
    )(gram, first_inverse, rows)


def finish_kernel(pieces_ref, both_ref, weights_ref, beam_ref):
    lower = pieces_ref[0]
    upper = pieces_ref[1]
    for index in range(2, 8, 2):
        lower = lower + pieces_ref[index]
        upper = upper + pieces_ref[index + 1]
    real_part = jnp.concatenate([lower[:, :HALF], upper[:, :HALF]], axis=1)
    imag_part = jnp.concatenate([lower[:, HALF:], upper[:, HALF:]], axis=1)
    projected = dot_nt(jnp.concatenate([real_part, imag_part], axis=0), both_ref[...])
    square = projected * projected
    weights = weights_ref[...]
    power = dot_nt(weights, square[:128] + square[128:]) / jnp.sum(weights)
    power = power * power
    beam_ref[...] = power * power


def finish(pieces, both, weights):
    return pl.pallas_call(
        finish_kernel,
        out_shape=jax.ShapeDtypeStruct((1, 128), jnp.float32),
        compiler_params=pltpu.CompilerParams(vmem_limit_bytes=16 * 2**20),
        name="finish",
    )(pieces, both, weights)


def turned(block):
    return jnp.concatenate([-block[:, K:], block[:, :K]], axis=1)


def exchange(pieces, axis, groups=None):
    return lax.all_to_all(pieces, axis, 0, 0, tiled=True, axis_index_groups=groups)


def drain(copies):
    for copy in copies:
        copy.start()
    for copy in copies:
        copy.wait()


def spread_kernel(pieces_ref, total_ref, copies_ref, sems):
    total_ref[...] = jnp.sum(pieces_ref[...], axis=0)
    drain(
        [
            pltpu.make_async_copy(total_ref, copies_ref.at[index], sems.at[index])
            for index in range(copies_ref.shape[0])
        ]
    )


def spread(pieces, count):
    piece = pieces.shape[1:]
    return pl.pallas_call(
        spread_kernel,
        out_shape=(
            jax.ShapeDtypeStruct(piece, jnp.float32),
            pltpu.HBM((count,) + piece, jnp.float32),
        ),
        out_specs=(
            pl.BlockSpec(memory_space=pltpu.VMEM),
            pl.BlockSpec(memory_space=pltpu.HBM),
        ),
        scratch_shapes=[pltpu.SemaphoreType.DMA((count,))],
        compiler_params=pltpu.CompilerParams(vmem_limit_bytes=16 * 2**20),
        name="spread",
    )(pieces)


def halves(value):
    high = value.astype(jnp.bfloat16)
    return high, (value - high.astype(jnp.float32)).astype(jnp.bfloat16)


def split_dot(left, parts):
    high, low = halves(left)
    total = jnp.dot(low, parts[0], preferred_element_type=jnp.float32)
    total += jnp.dot(high, parts[1], preferred_element_type=jnp.float32)
    return total + jnp.dot(high, parts[0], preferred_element_type=jnp.float32)


def first_product_kernel(
    real_ref, imag_ref, mine_ref, other_ref, core_ref, out_ref, start_ref, parts_ref, rows_ref, sems
):
    core = core_ref[0]
    for z in range(8):
        start_ref[2 * z + core] = mine_ref[z]
        start_ref[2 * z + 1 - core] = other_ref[z]
    start = start_ref[...].reshape(512, 2 * K)
    for base, value in ((0, start), (512, turned(start))):
        for index, part in enumerate(halves(value)):
            parts_ref[index, base : base + 512, :] = part
    parts = [parts_ref[index] for index in range(2)]
    copies = []
    for block in range(4):
        at = block * 128
        tile = jnp.concatenate([real_ref[at : at + 128, :], imag_ref[at : at + 128, :]], axis=1)
        rows_ref[block * 4 : block * 4 + 4] = split_dot(tile, parts).reshape(4, 32, 2 * K)
        copies.append(
            pltpu.make_async_copy(
                rows_ref.at[block * 4 : block * 4 + 4],
                out_ref.at[block * 4 : block * 4 + 4],
                sems.at[block],
            )
        )
        copies[-1].start()
    for copy in copies:
        copy.wait()


def first_product(real, imag, mine, other, core):
    return pl.pallas_call(
        first_product_kernel,
        out_shape=pltpu.HBM((16, 32, 2 * K), jnp.float32),
        in_specs=[VMEM] * 4 + [SMEM],
        out_specs=HBM,
        scratch_shapes=[
            pltpu.VMEM((16, 32, 2 * K), jnp.float32),
            pltpu.VMEM((2, 1024, 2 * K), jnp.bfloat16),
            pltpu.VMEM((16, 32, 2 * K), jnp.float32),
            pltpu.SemaphoreType.DMA((4,)),
        ],
        compiler_params=pltpu.CompilerParams(vmem_limit_bytes=32 * 2**20),
        cost_estimate=pl.CostEstimate(
            flops=6 * 512 * 1024 * 512, bytes_accessed=5 * 2**20, transcendentals=0
        ),
        name="first_product",
    )(real, imag, mine, other, core)


def sent_product_kernel(
    real_ref, imag_ref, first_ref, core_ref, out_ref, kept_ref, parts_out, parts_ref, gram_ref
):
    first = first_ref[...].reshape(512, 2 * K)
    for base, value in ((0, first), (512, -turned(first))):
        for index, part in enumerate(halves(value)):
            parts_ref[index, base : base + 512, :] = part
    parts_out[...] = parts_ref[...]
    rows = jnp.concatenate([first[:, :K], first[:, K:]], axis=0)
    gram_ref[...] = dot_tn(rows, rows)
    core = core_ref[0]
    for z in range(8):
        for which, target, at in ((core, kept_ref, 0), (1 - core, out_ref, 32)):
            start = pl.multiple_of(z * 32 + which * 16, 16)
            target[z, at : at + 8, :K] = gram_ref[pl.ds(start, 8), :]
            target[z, at : at + 8, K:] = gram_ref[pl.ds(start + 8, 8), :]
    parts = [parts_ref[index] for index in range(2)]
    for block in range(2):
        at = slice(block * 4, block * 4 + 4)
        tile = jnp.concatenate(
            [real_ref[at].reshape(128, 512), imag_ref[at].reshape(128, 512)], axis=1
        )
        out_ref[at, :32, :] = split_dot(tile, parts).reshape(4, 32, 2 * K)


def sent_product(real, imag, first, core):
    return pl.pallas_call(
        sent_product_kernel,
        out_shape=(
            jax.ShapeDtypeStruct((8, 40, 2 * K), jnp.float32),
            jax.ShapeDtypeStruct((8, 8, 2 * K), jnp.float32),
            jax.ShapeDtypeStruct((2, 1024, 2 * K), jnp.bfloat16),
        ),
        in_specs=[VMEM] * 3 + [SMEM],
        out_specs=(VMEM,) * 3,
        scratch_shapes=[
            pltpu.VMEM((2, 1024, 2 * K), jnp.bfloat16),
            pltpu.VMEM((K, K), jnp.float32),
        ],
        compiler_params=pltpu.CompilerParams(vmem_limit_bytes=32 * 2**20),
        cost_estimate=pl.CostEstimate(
            flops=6 * 256 * 1024 * 512, bytes_accessed=5 * 2**20, transcendentals=0
        ),
        name="sent_product",
    )(real, imag, first, core)


def kept_product_kernel(real_ref, imag_ref, parts_ref, gram_ref, out_ref):
    out_ref[:, 32:, :] = gram_ref[...]
    parts = [parts_ref[index] for index in range(2)]
    for block in range(2):
        at = slice(block * 4, block * 4 + 4)
        tile = jnp.concatenate(
            [real_ref[at].reshape(128, 512), imag_ref[at].reshape(128, 512)], axis=1
        )
        out_ref[at, :32, :] = split_dot(tile, parts).reshape(4, 32, 2 * K)


def kept_product(real, imag, parts, gram):
    return pl.pallas_call(
        kept_product_kernel,
        out_shape=jax.ShapeDtypeStruct((8, 40, 2 * K), jnp.float32),
        in_specs=[VMEM] * 4,
        out_specs=VMEM,
        compiler_params=pltpu.CompilerParams(vmem_limit_bytes=32 * 2**20),
        cost_estimate=pl.CostEstimate(
            flops=6 * 256 * 1024 * 512, bytes_accessed=5 * 2**20, transcendentals=0
        ),
        name="kept_product",
    )(real, imag, parts, gram)


def stage_kernel(*refs):
    terms, out_ref, total_ref, sem = refs[:-3], refs[-3], refs[-2], refs[-1]
    total = terms[0][...]
    for term in terms[1:]:
        total = total + term[...]
    total_ref[...] = total
    drain([pltpu.make_async_copy(total_ref, out_ref, sem)])


def stage(*terms):
    shape = jax.ShapeDtypeStruct(terms[0].shape, jnp.float32)
    return pl.pallas_call(
        stage_kernel,
        out_shape=pltpu.HBM(shape.shape, jnp.float32),
        out_specs=pl.BlockSpec(memory_space=pltpu.HBM),
        scratch_shapes=[pltpu.VMEM(shape.shape, jnp.float32), pltpu.SemaphoreType.DMA],
        compiler_params=pltpu.CompilerParams(vmem_limit_bytes=16 * 2**20),
        name="stage",
    )(*terms)


SIN_TERMS = (
    3.1415926535362906,
    -5.167712764624546,
    2.550163318947043,
    -0.5992521978220368,
    0.08205040179571269,
    -0.007028386383306818,
)
COS_TERMS = (
    0.9999999997799041,
    -4.9348021370788295,
    4.058709159556314,
    -1.335212003049894,
    0.23493731381328964,
    -0.024396324346460163,
)


def polynomial(terms, x):
    value = terms[-1]
    for term in terms[-2::-1]:
        value = value * x + term
    return value


def spread_start_kernel(start_ref, copies_ref, total_ref, sems):
    total_ref[:, :K] = start_ref[0]
    total_ref[:, K:] = start_ref[1]
    drain(
        [
            pltpu.make_async_copy(total_ref, copies_ref.at[index], sems.at[index])
            for index in range(8)
        ]
    )


def spread_start(start):
    return pl.pallas_call(
        spread_start_kernel,
        out_shape=pltpu.HBM((8, 32, 2 * K), jnp.float32),
        in_specs=[VMEM],
        out_specs=HBM,
        scratch_shapes=[pltpu.VMEM((32, 2 * K), jnp.float32), pltpu.SemaphoreType.DMA((8,))],
        compiler_params=pltpu.CompilerParams(vmem_limit_bytes=8 * 2**20),
        name="spread_start",
    )(start)


def steering_kernel(grid_ref, mics_ref, *refs):
    index = (
        grid_ref[:, 0:1] * mics_ref[0:1, :] + grid_ref[:, 1:2] * mics_ref[1:2, :]
    )
    turns = (index - jnp.round(index * (1.0 / MOD)) * float(MOD)) * (1.0 / MOD)
    square = turns * turns
    half_sine = turns * polynomial(SIN_TERMS, square)
    half_cosine = polynomial(COS_TERMS, square)
    cosine = 1.0 - 2.0 * half_sine * half_sine
    sine = 2.0 * half_sine * half_cosine
    for value, high_ref, low_ref in ((cosine, refs[-4], refs[-3]), (sine, refs[-2], refs[-1])):
        high_ref[...], low_ref[...] = halves(value)


def steering(grid, mics, first, count, before=()):
    block = pl.BlockSpec((256, 1024), lambda i: ((i + first) // 2, (i + first) % 2))
    return pl.pallas_call(
        steering_kernel,
        grid=(count,),
        in_specs=[
            pl.BlockSpec((256, 2), lambda i: ((i + first) // 2, 0)),
            pl.BlockSpec((2, 1024), lambda i: (0, (i + first) % 2)),
        ]
        + [HBM] * len(before),
        out_specs=(block,) * 4,
        out_shape=(pltpu.HBM((1024, 2048), jnp.bfloat16),) * 4,
        input_output_aliases={2 + index: index for index in range(len(before))},
        compiler_params=pltpu.CompilerParams(vmem_limit_bytes=24 * 2**20),
        cost_estimate=pl.CostEstimate(
            flops=45 * 256 * 1024 * count, bytes_accessed=8 * 256 * 1024 * count, transcendentals=0
        ),
        name="steering",
    )(grid, mics, *before)


def second_gram_kernel(mine_ref, other_ref, inverse_ref, row_ref, copies_ref, slice_ref, sems):
    own = pl.multiple_of(row_ref[0] * 16, 16)
    raw = jnp.concatenate(
        [
            ref[:, :32, lanes].reshape(256, K)
            for ref in (mine_ref, other_ref)
            for lanes in (slice(0, K), slice(K, 2 * K))
        ],
        axis=0,
    )
    second = dot_nt(raw, inverse_ref[...])
    turned_slice = dot_nt(inverse_ref[pl.ds(own, 16), :], raw)
    slice_ref[...] = dot(turned_slice, second)
    drain(
        [
            pltpu.make_async_copy(slice_ref, copies_ref.at[index], sems.at[index])
            for index in range(16)
        ]
    )


def second_gram_slice(mine, other, inverse, row):
    return pl.pallas_call(
        second_gram_kernel,
        out_shape=pltpu.HBM((16, 16, K), jnp.float32),
        in_specs=[VMEM, VMEM, VMEM, SMEM],
        out_specs=HBM,
        scratch_shapes=[pltpu.VMEM((16, K), jnp.float32), pltpu.SemaphoreType.DMA((16,))],
        compiler_params=pltpu.CompilerParams(vmem_limit_bytes=24 * 2**20),
        cost_estimate=pl.CostEstimate(
            flops=2 * 1024 * K * (K + 32), bytes_accessed=2**21, transcendentals=0
        ),
        name="second_gram",
    )(mine, other, inverse, row)


def project_kernel(half_ref, *refs):
    raw_refs, beside_refs = refs[:2], refs[2:8]
    cos_high, cos_low, sin_high, sin_low = refs[8:12]
    out_ref, high_ref, low_ref, slots, sems = refs[12:]
    step = pl.program_id(0)

    @pl.when(step == 0)
    def _():
        lower = half_ref[0] == 0
        sources = []
        for ref in raw_refs:
            parts = [
                ref[:, :32, lane : lane + HALF].reshape(256, HALF) for lane in range(0, 2 * K, HALF)
            ]
            sources.append(
                (jnp.where(lower, parts[0], parts[1]), jnp.where(lower, parts[2], parts[3]))
            )
        for ref in beside_refs:
            sources.append((ref[:, :, :HALF].reshape(256, HALF), ref[:, :, HALF:].reshape(256, HALF)))
        for index, (real, imag) in enumerate(sources):
            start = index * 256
            for base, value in (
                (0, jnp.concatenate([real, imag], axis=1)),
                (2048, jnp.concatenate([-imag, real], axis=1)),
            ):
                high, low = halves(value)
                high_ref[base + start : base + start + 256, :] = high
                low_ref[base + start : base + start + 256, :] = low

    high = jnp.concatenate([cos_high[...], sin_high[...]], axis=1)
    low = jnp.concatenate([cos_low[...], sin_low[...]], axis=1)
    product = jnp.dot(high, high_ref[...], preferred_element_type=jnp.float32)
    product += jnp.dot(high, low_ref[...], preferred_element_type=jnp.float32)
    product += jnp.dot(low, high_ref[...], preferred_element_type=jnp.float32)
    slots[pl.ds(2 * step, 2)] = product.reshape(2, 128, 256)

    def copy(index):
        both = pl.ds(2 * index, 2)
        return pltpu.make_async_copy(slots.at[both], out_ref.at[both], sems.at[index])

    copy(step).start()

    @pl.when(step == 3)
    def _():
        for index in range(4):
            copy(index).wait()


def project(half, raw, beside, steered):
    block = pl.BlockSpec((256, 2048), lambda i: (i, 0))
    return pl.pallas_call(
        project_kernel,
        grid=(4,),
        in_specs=[SMEM]
        + [pl.BlockSpec((8, 40, 512), lambda i: (0, 0, 0))] * 2
        + [pl.BlockSpec((8, 32, 256), lambda i: (0, 0, 0))] * 6
        + [block] * 4,
        out_specs=HBM,
        out_shape=pltpu.HBM((8, 128, 256), jnp.float32),
        scratch_shapes=[
            pltpu.VMEM((4096, 256), jnp.bfloat16),
            pltpu.VMEM((4096, 256), jnp.bfloat16),
            pltpu.VMEM((8, 128, 256), jnp.float32),
            pltpu.SemaphoreType.DMA((4,)),
        ],
        compiler_params=pltpu.CompilerParams(vmem_limit_bytes=40 * 2**20),
        cost_estimate=pl.CostEstimate(
            flops=3 * 2 * 1024 * 4096 * 256, bytes_accessed=18 * 2**20, transcendentals=0
        ),
        name="project",
    )(half, *raw, *beside, *[pltpu.with_memory_space_constraint(x, pltpu.HBM) for x in steered])


def half_of_vectors(pieces, half):
    lower = jnp.concatenate([pieces[..., :HALF], pieces[..., K : K + HALF]], axis=-1)
    upper = jnp.concatenate([pieces[..., HALF:K], pieces[..., K + HALF :]], axis=-1)
    return jnp.where(half == 0, lower, upper)


def by_core(tile, core):
    rows = tile.T.reshape(8, 2, 32, 512)
    return (
        jnp.where(core == 0, rows[:, 0], rows[:, 1]),
        jnp.where(core == 0, rows[:, 1], rows[:, 0]),
    )


def body(csm_real, csm_imag, start_block, mic_coords, grid_coords, bin_index):
    row = lax.axis_index("row")
    core = row % 2
    own_core = core.reshape(1)
    col = lax.axis_index("col")
    half = col % 2
    points = grid_coords.reshape(2, 4, 2, 256)
    points = jnp.where(col // 2 % 2 == 0, points[:, :, 0], points[:, :, 1]).reshape(2, 1024)
    reduced = ((bin_index * points) % MOD).astype(jnp.float32).T

    mine = exchange(spread_start(start_block), "row", Z_GROUPS)
    kept_real, sent_real = by_core(csm_real, core)
    kept_imag, sent_imag = by_core(csm_imag, core)
    mine, kept_real, kept_imag, sent_real, sent_imag, mic_coords = lax.optimization_barrier(
        (mine, kept_real, kept_imag, sent_real, sent_imag, mic_coords)
    )
    other = lax.ppermute(mine, "row", CORE_SWAP)
    first_partial = first_product(csm_real, csm_imag, mine, other, own_core)

    places = [mic_coords] + [lax.ppermute(mic_coords, "col", ALONG_X[flip]) for flip in (1, 2, 3)]
    places = jnp.stack(places, axis=1).reshape(2, 4, 8, 2, 32)
    even, odd = places[:, :, :, 0], places[:, :, :, 1]
    mics = jnp.stack([jnp.where(core == 0, even, odd), jnp.where(core == 0, odd, even)], axis=2)
    mics = mics.reshape(2, 2048).astype(jnp.float32)
    steered = steering(reduced, mics, 0, 3)
    first_pieces = exchange(first_partial, "col")
    first_pieces, steered = lax.optimization_barrier((first_pieces, steered))

    steered = steering(reduced, mics, 3, 2, steered)
    first = exchange(spread(first_pieces, 16)[1], "col")
    first, steered = lax.optimization_barrier((first, steered))
    sent, gram_rows, parts = sent_product(sent_real, sent_imag, first, own_core)
    got = lax.ppermute(sent, "row", CORE_SWAP)
    kept = kept_product(kept_real, kept_imag, parts, gram_rows)
    pair = stage(kept, got)

    steered = steering(reduced, mics, 5, 2, steered)
    pieces = exchange(pair, "row", Z_GROUPS)
    pieces, steered = lax.optimization_barrier((pieces, steered))
    own, spread_out = spread(pieces, 8)

    steered = steering(reduced, mics, 7, 1, steered)
    mine = exchange(spread_out, "row", Z_GROUPS)
    mine, steered = lax.optimization_barrier((mine, steered))
    other = lax.ppermute(mine, "row", CORE_SWAP)
    taken = half_of_vectors(mine[:, :32], half)
    given = half_of_vectors(mine[:, :32], 1 - half)
    near = [
        lax.ppermute(taken if flip == 2 else given, "col", ALONG_X[flip]) for flip in (1, 2, 3)
    ]
    first_inverse = first_factor(mine, other, own_core)
    gram_copies = second_gram_slice(mine, other, first_inverse, row.reshape(1))
    near, gram_copies = lax.optimization_barrier((near, gram_copies))
    far = [lax.ppermute(block, "row", CORE_SWAP) for block in near]
    beside = [block for both in zip(near, far) for block in both]
    gram_pieces = exchange(gram_copies, "col")
    part = project(half.reshape(1), (mine, other), beside, steered)
    part, gram_pieces = lax.optimization_barrier((part, gram_pieces))
    pieces = exchange(part, "col", POINT_GROUPS)
    second_gram = lax.all_gather(jnp.sum(gram_pieces, axis=0), "row", axis=0, tiled=True)
    basis, both_inverse, weights = second_factor(second_gram, first_inverse, own)
    return (basis, finish(pieces, both_inverse, weights).reshape(128))


def solution(mesh):
    in_specs = (
        P("row", "col"),
        P("row", "col"),
        P(None, ("col", "row"), None),
        P(None, "col"),
        P(None, "row"),
        P(),
    )
    out_specs = (P(None, ("col", "row"), None), P(("row", "col")))
    return jax.shard_map(body, mesh=mesh, in_specs=in_specs, out_specs=out_specs, check_vma=False)
```

```python
import jax
import jax.numpy as jnp
from jax import lax
from jax.experimental import pallas as pl
from jax.experimental.pallas import tpu as pltpu
from jax.sharding import PartitionSpec as P

NU = 4
K = 256
MOD = 4093
HIGH = lax.Precision.HIGHEST

Z_GROUPS = [list(range(core, 16, 2)) for core in range(2)]
CORE_SWAP = [(index, index ^ 1) for index in range(16)]

ALONG_X = [[(index, index ^ flip) for index in range(16)] for flip in range(4)]
POINT_GROUPS = [[index for index in range(16) if index // 2 % 2 == part] for part in range(2)]
HALF = K // 2
SMEM = pl.BlockSpec(memory_space=pltpu.SMEM)
HBM = pl.BlockSpec(memory_space=pltpu.HBM)
VMEM = pl.BlockSpec(memory_space=pltpu.VMEM)

PANEL = 64
MICRO = 16


def dot(a, b):
    return jnp.dot(a, b, precision=HIGH, preferred_element_type=jnp.float32)


def dot_tn(a, b):
    return lax.dot_general(
        a, b, (((0,), (0,)), ((), ())), precision=HIGH, preferred_element_type=jnp.float32
    )


def dot_nt(a, b):
    return lax.dot_general(
        a, b, (((1,), (1,)), ((), ())), precision=HIGH, preferred_element_type=jnp.float32
    )


def eliminate(work_ref, upper_ref, inverse_ref):
    rows = lax.broadcasted_iota(jnp.int32, (K, K), 0)
    cols = lax.broadcasted_iota(jnp.int32, (K, K), 1)
    work_ref[:, K:] = (rows == cols).astype(jnp.float32)
    panel_row = lax.broadcasted_iota(jnp.int32, (PANEL, 128), 0)
    for start in range(0, K, PANEL):
        low = (start // 128) * 128
        high = K + ((start + PANEL + 127) // 128) * 128
        width = high - low
        offset = start - low
        panel = work_ref[start : start + PANEL, low:high]
        for first in range(0, PANEL, MICRO):
            columns = [
                jnp.broadcast_to(
                    panel[:, offset + first + k : offset + first + k + 1], (PANEL, 128)
                )
                for k in range(MICRO)
            ]
            for k in range(MICRO):
                j = first + k
                scale = jnp.where(panel_row > j, columns[k] * (1.0 / columns[k][j : j + 1, :]), 0.0)
                for later in range(k + 1, MICRO):
                    columns[later] = columns[later] - scale * columns[later][j : j + 1, :]
                panel = (
                    panel
                    - jnp.concatenate([scale] * (width // 128), axis=1) * panel[j : j + 1, :]
                )
        square_row = lax.broadcasted_iota(jnp.int32, (PANEL, PANEL), 0)
        square_col = lax.broadcasted_iota(jnp.int32, (PANEL, PANEL), 1)
        pivots = jnp.sum(
            jnp.where(square_row == square_col, panel[:, offset : offset + PANEL], 0.0),
            axis=1,
            keepdims=True,
        )
        panel = panel * (1.0 / jnp.sqrt(pivots))
        if upper_ref is not None:
            panel_cols = lax.broadcasted_iota(jnp.int32, (PANEL, K - low), 1) + low
            panel_rows = lax.broadcasted_iota(jnp.int32, (PANEL, K - low), 0) + start
            upper_ref[start : start + PANEL, :] = jnp.zeros((PANEL, K), jnp.float32)
            upper_ref[start : start + PANEL, low:K] = jnp.where(
                panel_cols >= panel_rows, panel[:, : K - low], 0.0
            )
        inverse_ref[start : start + PANEL, :] = jnp.zeros((PANEL, K), jnp.float32)
        inverse_ref[start : start + PANEL, : high - K] = panel[:, K - low :]
        after = start + PANEL
        if after < K:
            update = dot_tn(panel[:, after - low : K - low], panel)
            work_ref[after:, low:high] = work_ref[after:, low:high] - update


def first_factor_kernel(mine_ref, other_ref, core_ref, inverse_ref, work_ref):
    own = core_ref[0]
    for z in range(8):
        for core in range(2):
            part = jnp.where(own == core, mine_ref[z, 32:, :], other_ref[z, 32:, :])
            start = (2 * z + core) * 16
            work_ref[start : start + 8, :K] = part[:, :K]
            work_ref[start + 8 : start + 16, :K] = part[:, K:]
    eliminate(work_ref, None, inverse_ref)


def first_factor(mine, other, core):
    return pl.pallas_call(
        first_factor_kernel,
        out_shape=jax.ShapeDtypeStruct((K, K), jnp.float32),
        in_specs=[VMEM, VMEM, SMEM],
        out_specs=VMEM,
        scratch_shapes=[pltpu.VMEM((K, 2 * K), jnp.float32)],
        compiler_params=pltpu.CompilerParams(vmem_limit_bytes=16 * 2**20),
        cost_estimate=pl.CostEstimate(
            flops=4 * K**3, bytes_accessed=12 * K * K, transcendentals=K
        ),
        name="first_factor",
    )(mine, other, core)


def second_factor_kernel(
    gram_ref, first_ref, rows_ref, basis_ref, both_ref, weights_ref, upper_ref, inverse_ref, work_ref
):
    work_ref[:, :K] = gram_ref[...]
    eliminate(work_ref, upper_ref, inverse_ref)
    rows = lax.broadcasted_iota(jnp.int32, (K, K), 0)
    cols = lax.broadcasted_iota(jnp.int32, (K, K), 1)
    diagonal = jnp.sum(jnp.where(rows == cols, upper_ref[...], 0.0), axis=0, keepdims=True)
    weights_ref[...] = jnp.sqrt(jnp.sqrt(diagonal))
    both_ref[...] = dot(inverse_ref[...], first_ref[...])
    raw = jnp.concatenate([rows_ref[:32, :K], rows_ref[:32, K:]], axis=0)
    basis = dot_nt(dot_nt(raw, first_ref[...]), inverse_ref[...])
    basis_ref[0] = basis[:32]
    basis_ref[1] = basis[32:]


def second_factor(gram, first_inverse, rows):
    return pl.pallas_call(
        second_factor_kernel,
        out_shape=(
            jax.ShapeDtypeStruct((2, 32, K), jnp.float32),
            jax.ShapeDtypeStruct((K, K), jnp.float32),
            jax.ShapeDtypeStruct((1, K), jnp.float32),
        ),
        scratch_shapes=[
            pltpu.VMEM((K, K), jnp.float32),
            pltpu.VMEM((K, K), jnp.float32),
            pltpu.VMEM((K, 2 * K), jnp.float32),
        ],
        compiler_params=pltpu.CompilerParams(vmem_limit_bytes=16 * 2**20),
        cost_estimate=pl.CostEstimate(
            flops=6 * K**3, bytes_accessed=16 * K * K, transcendentals=K
        ),
        name="second_factor",
    )(gram, first_inverse, rows)


def finish_kernel(pieces_ref, both_ref, weights_ref, beam_ref):
    lower = pieces_ref[0]
    upper = pieces_ref[1]
    for index in range(2, 8, 2):
        lower = lower + pieces_ref[index]
        upper = upper + pieces_ref[index + 1]
    real_part = jnp.concatenate([lower[:, :HALF], upper[:, :HALF]], axis=1)
    imag_part = jnp.concatenate([lower[:, HALF:], upper[:, HALF:]], axis=1)
    projected = dot_nt(jnp.concatenate([real_part, imag_part], axis=0), both_ref[...])
    square = projected * projected
    weights = weights_ref[...]
    power = dot_nt(weights, square[:128] + square[128:]) / jnp.sum(weights)
    power = power * power
    beam_ref[...] = power * power


def finish(pieces, both, weights):
    return pl.pallas_call(
        finish_kernel,
        out_shape=jax.ShapeDtypeStruct((1, 128), jnp.float32),
        compiler_params=pltpu.CompilerParams(vmem_limit_bytes=16 * 2**20),
        name="finish",
    )(pieces, both, weights)


def turned(block):
    return jnp.concatenate([-block[:, K:], block[:, :K]], axis=1)


def exchange(pieces, axis, groups=None):
    return lax.all_to_all(pieces, axis, 0, 0, tiled=True, axis_index_groups=groups)


def drain(copies):
    for copy in copies:
        copy.start()
    for copy in copies:
        copy.wait()


def spread_kernel(pieces_ref, total_ref, copies_ref, sems):
    total_ref[...] = jnp.sum(pieces_ref[...], axis=0)
    drain(
        [
            pltpu.make_async_copy(total_ref, copies_ref.at[index], sems.at[index])
            for index in range(copies_ref.shape[0])
        ]
    )


def spread(pieces, count):
    piece = pieces.shape[1:]
    return pl.pallas_call(
        spread_kernel,
        out_shape=(
            jax.ShapeDtypeStruct(piece, jnp.float32),
            pltpu.HBM((count,) + piece, jnp.float32),
        ),
        out_specs=(
            pl.BlockSpec(memory_space=pltpu.VMEM),
            pl.BlockSpec(memory_space=pltpu.HBM),
        ),
        scratch_shapes=[pltpu.SemaphoreType.DMA((count,))],
        compiler_params=pltpu.CompilerParams(vmem_limit_bytes=16 * 2**20),
        name="spread",
    )(pieces)


def halves(value):
    high = value.astype(jnp.bfloat16)
    return high, (value - high.astype(jnp.float32)).astype(jnp.bfloat16)


def split_dot(left, parts):
    high, low = halves(left)
    total = jnp.dot(low, parts[0], preferred_element_type=jnp.float32)
    total += jnp.dot(high, parts[1], preferred_element_type=jnp.float32)
    return total + jnp.dot(high, parts[0], preferred_element_type=jnp.float32)


def first_product_kernel(
    real_ref, imag_ref, mine_ref, other_ref, core_ref, out_ref, start_ref, parts_ref, rows_ref, sems
):
    core = core_ref[0]
    for z in range(8):
        start_ref[2 * z + core] = mine_ref[z]
        start_ref[2 * z + 1 - core] = other_ref[z]
    start = start_ref[...].reshape(512, 2 * K)
    for base, value in ((0, start), (512, turned(start))):
        for index, part in enumerate(halves(value)):
            parts_ref[index, base : base + 512, :] = part
    parts = [parts_ref[index] for index in range(2)]
    copies = []
    for block in range(4):
        at = block * 128
        tile = jnp.concatenate([real_ref[at : at + 128, :], imag_ref[at : at + 128, :]], axis=1)
        rows_ref[block * 4 : block * 4 + 4] = split_dot(tile, parts).reshape(4, 32, 2 * K)
        copies.append(
            pltpu.make_async_copy(
                rows_ref.at[block * 4 : block * 4 + 4],
                out_ref.at[block * 4 : block * 4 + 4],
                sems.at[block],
            )
        )
        copies[-1].start()
    for copy in copies:
        copy.wait()


def first_product(real, imag, mine, other, core):
    return pl.pallas_call(
        first_product_kernel,
        out_shape=pltpu.HBM((16, 32, 2 * K), jnp.float32),
        in_specs=[VMEM] * 4 + [SMEM],
        out_specs=HBM,
        scratch_shapes=[
            pltpu.VMEM((16, 32, 2 * K), jnp.float32),
            pltpu.VMEM((2, 1024, 2 * K), jnp.bfloat16),
            pltpu.VMEM((16, 32, 2 * K), jnp.float32),
            pltpu.SemaphoreType.DMA((4,)),
        ],
        compiler_params=pltpu.CompilerParams(vmem_limit_bytes=32 * 2**20),
        cost_estimate=pl.CostEstimate(
            flops=6 * 512 * 1024 * 512, bytes_accessed=5 * 2**20, transcendentals=0
        ),
        name="first_product",
    )(real, imag, mine, other, core)


def sent_product_kernel(
    real_ref, imag_ref, first_ref, core_ref, out_ref, kept_ref, parts_out, parts_ref, gram_ref
):
    first = first_ref[...].reshape(512, 2 * K)
    for base, value in ((0, first), (512, -turned(first))):
        for index, part in enumerate(halves(value)):
            parts_ref[index, base : base + 512, :] = part
    parts_out[...] = parts_ref[...]
    rows = jnp.concatenate([first[:, :K], first[:, K:]], axis=0)
    gram_ref[...] = dot_tn(rows, rows)
    core = core_ref[0]
    for z in range(8):
        for which, target, at in ((core, kept_ref, 0), (1 - core, out_ref, 32)):
            start = pl.multiple_of(z * 32 + which * 16, 16)
            target[z, at : at + 8, :K] = gram_ref[pl.ds(start, 8), :]
            target[z, at : at + 8, K:] = gram_ref[pl.ds(start + 8, 8), :]
    parts = [parts_ref[index] for index in range(2)]
    for block in range(2):
        at = slice(block * 4, block * 4 + 4)
        tile = jnp.concatenate(
            [real_ref[at].reshape(128, 512), imag_ref[at].reshape(128, 512)], axis=1
        )
        out_ref[at, :32, :] = split_dot(tile, parts).reshape(4, 32, 2 * K)


def sent_product(real, imag, first, core):
    return pl.pallas_call(
        sent_product_kernel,
        out_shape=(
            jax.ShapeDtypeStruct((8, 40, 2 * K), jnp.float32),
            jax.ShapeDtypeStruct((8, 8, 2 * K), jnp.float32),
            jax.ShapeDtypeStruct((2, 1024, 2 * K), jnp.bfloat16),
        ),
        in_specs=[VMEM] * 3 + [SMEM],
        out_specs=(VMEM,) * 3,
        scratch_shapes=[
            pltpu.VMEM((2, 1024, 2 * K), jnp.bfloat16),
            pltpu.VMEM((K, K), jnp.float32),
        ],
        compiler_params=pltpu.CompilerParams(vmem_limit_bytes=32 * 2**20),
        cost_estimate=pl.CostEstimate(
            flops=6 * 256 * 1024 * 512, bytes_accessed=5 * 2**20, transcendentals=0
        ),
        name="sent_product",
    )(real, imag, first, core)


def kept_product_kernel(real_ref, imag_ref, parts_ref, gram_ref, out_ref):
    out_ref[:, 32:, :] = gram_ref[...]
    parts = [parts_ref[index] for index in range(2)]
    for block in range(2):
        at = slice(block * 4, block * 4 + 4)
        tile = jnp.concatenate(
            [real_ref[at].reshape(128, 512), imag_ref[at].reshape(128, 512)], axis=1
        )
        out_ref[at, :32, :] = split_dot(tile, parts).reshape(4, 32, 2 * K)


def kept_product(real, imag, parts, gram):
    return pl.pallas_call(
        kept_product_kernel,
        out_shape=jax.ShapeDtypeStruct((8, 40, 2 * K), jnp.float32),
        in_specs=[VMEM] * 4,
        out_specs=VMEM,
        compiler_params=pltpu.CompilerParams(vmem_limit_bytes=32 * 2**20),
        cost_estimate=pl.CostEstimate(
            flops=6 * 256 * 1024 * 512, bytes_accessed=5 * 2**20, transcendentals=0
        ),
        name="kept_product",
    )(real, imag, parts, gram)


def stage_kernel(*refs):
    terms, out_ref, total_ref, sem = refs[:-3], refs[-3], refs[-2], refs[-1]
    total = terms[0][...]
    for term in terms[1:]:
        total = total + term[...]
    total_ref[...] = total
    drain([pltpu.make_async_copy(total_ref, out_ref, sem)])


def stage(*terms):
    shape = jax.ShapeDtypeStruct(terms[0].shape, jnp.float32)
    return pl.pallas_call(
        stage_kernel,
        out_shape=pltpu.HBM(shape.shape, jnp.float32),
        out_specs=pl.BlockSpec(memory_space=pltpu.HBM),
        scratch_shapes=[pltpu.VMEM(shape.shape, jnp.float32), pltpu.SemaphoreType.DMA],
        compiler_params=pltpu.CompilerParams(vmem_limit_bytes=16 * 2**20),
        name="stage",
    )(*terms)


SIN_TERMS = (
    3.1415926535362906,
    -5.167712764624546,
    2.550163318947043,
    -0.5992521978220368,
    0.08205040179571269,
    -0.007028386383306818,
)
COS_TERMS = (
    0.9999999997799041,
    -4.9348021370788295,
    4.058709159556314,
    -1.335212003049894,
    0.23493731381328964,
    -0.024396324346460163,
)


def polynomial(terms, x):
    value = terms[-1]
    for term in terms[-2::-1]:
        value = value * x + term
    return value


def spread_start_kernel(start_ref, copies_ref, sems):
    drain(
        [
            pltpu.make_async_copy(
                start_ref.at[part],
                copies_ref.at[index, :, pl.ds(part * K, K)],
                sems.at[2 * index + part],
            )
            for index in range(8)
            for part in range(2)
        ]
    )


def spread_start(start):
    return pl.pallas_call(
        spread_start_kernel,
        out_shape=pltpu.HBM((8, 32, 2 * K), jnp.float32),
        in_specs=[HBM],
        out_specs=HBM,
        scratch_shapes=[pltpu.SemaphoreType.DMA((16,))],
        compiler_params=pltpu.CompilerParams(vmem_limit_bytes=8 * 2**20),
        name="spread_start",
    )(pltpu.with_memory_space_constraint(start, pltpu.HBM))


def steering_kernel(grid_ref, mics_ref, *refs):
    index = (
        grid_ref[:, 0:1] * mics_ref[0:1, :] + grid_ref[:, 1:2] * mics_ref[1:2, :]
    )
    turns = (index - jnp.round(index * (1.0 / MOD)) * float(MOD)) * (1.0 / MOD)
    square = turns * turns
    half_sine = turns * polynomial(SIN_TERMS, square)
    half_cosine = polynomial(COS_TERMS, square)
    cosine = 1.0 - 2.0 * half_sine * half_sine
    sine = 2.0 * half_sine * half_cosine
    for value, high_ref, low_ref in ((cosine, refs[-4], refs[-3]), (sine, refs[-2], refs[-1])):
        high_ref[...], low_ref[...] = halves(value)


def steering(grid, mics, first, count, before=()):
    block = pl.BlockSpec((256, 1024), lambda i: ((i + first) // 2, (i + first) % 2))
    return pl.pallas_call(
        steering_kernel,
        grid=(count,),
        in_specs=[
            pl.BlockSpec((256, 2), lambda i: ((i + first) // 2, 0)),
            pl.BlockSpec((2, 1024), lambda i: (0, (i + first) % 2)),
        ]
        + [HBM] * len(before),
        out_specs=(block,) * 4,
        out_shape=(pltpu.HBM((1024, 2048), jnp.bfloat16),) * 4,
        input_output_aliases={2 + index: index for index in range(len(before))},
        compiler_params=pltpu.CompilerParams(vmem_limit_bytes=24 * 2**20),
        cost_estimate=pl.CostEstimate(
            flops=45 * 256 * 1024 * count, bytes_accessed=8 * 256 * 1024 * count, transcendentals=0
        ),
        name="steering",
    )(grid, mics, *before)


def second_gram_kernel(mine_ref, other_ref, inverse_ref, row_ref, copies_ref, slice_ref, sems):
    own = pl.multiple_of(row_ref[0] * 16, 16)
    raw = jnp.concatenate(
        [
            ref[:, :32, lanes].reshape(256, K)
            for ref in (mine_ref, other_ref)
            for lanes in (slice(0, K), slice(K, 2 * K))
        ],
        axis=0,
    )
    second = dot_nt(raw, inverse_ref[...])
    turned_slice = dot_nt(inverse_ref[pl.ds(own, 16), :], raw)
    slice_ref[...] = dot(turned_slice, second)
    drain(
        [
            pltpu.make_async_copy(slice_ref, copies_ref.at[index], sems.at[index])
            for index in range(16)
        ]
    )


def second_gram_slice(mine, other, inverse, row):
    return pl.pallas_call(
        second_gram_kernel,
        out_shape=pltpu.HBM((16, 16, K), jnp.float32),
        in_specs=[VMEM, VMEM, VMEM, SMEM],
        out_specs=HBM,
        scratch_shapes=[pltpu.VMEM((16, K), jnp.float32), pltpu.SemaphoreType.DMA((16,))],
        compiler_params=pltpu.CompilerParams(vmem_limit_bytes=24 * 2**20),
        cost_estimate=pl.CostEstimate(
            flops=2 * 1024 * K * (K + 32), bytes_accessed=2**21, transcendentals=0
        ),
        name="second_gram",
    )(mine, other, inverse, row)


def project_kernel(half_ref, *refs):
    raw_refs, beside_refs = refs[:2], refs[2:8]
    cos_high, cos_low, sin_high, sin_low = refs[8:12]
    out_ref, high_ref, low_ref, slots, sems = refs[12:]
    step = pl.program_id(0)

    @pl.when(step == 0)
    def _():
        lower = half_ref[0] == 0
        sources = []
        for ref in raw_refs:
            parts = [
                ref[:, :32, lane : lane + HALF].reshape(256, HALF) for lane in range(0, 2 * K, HALF)
            ]
            sources.append(
                (jnp.where(lower, parts[0], parts[1]), jnp.where(lower, parts[2], parts[3]))
            )
        for ref in beside_refs:
            sources.append((ref[:, :, :HALF].reshape(256, HALF), ref[:, :, HALF:].reshape(256, HALF)))
        for index, (real, imag) in enumerate(sources):
            start = index * 256
            for base, value in (
                (0, jnp.concatenate([real, imag], axis=1)),
                (2048, jnp.concatenate([-imag, real], axis=1)),
            ):
                high, low = halves(value)
                high_ref[base + start : base + start + 256, :] = high
                low_ref[base + start : base + start + 256, :] = low

    high = jnp.concatenate([cos_high[...], sin_high[...]], axis=1)
    low = jnp.concatenate([cos_low[...], sin_low[...]], axis=1)
    product = jnp.dot(high, high_ref[...], preferred_element_type=jnp.float32)
    product += jnp.dot(high, low_ref[...], preferred_element_type=jnp.float32)
    product += jnp.dot(low, high_ref[...], preferred_element_type=jnp.float32)
    slots[pl.ds(2 * step, 2)] = product.reshape(2, 128, 256)

    def copy(index):
        both = pl.ds(2 * index, 2)
        return pltpu.make_async_copy(slots.at[both], out_ref.at[both], sems.at[index])

    copy(step).start()

    @pl.when(step == 3)
    def _():
        for index in range(4):
            copy(index).wait()


def project(half, raw, beside, steered):
    block = pl.BlockSpec((256, 2048), lambda i: (i, 0))
    return pl.pallas_call(
        project_kernel,
        grid=(4,),
        in_specs=[SMEM]
        + [pl.BlockSpec((8, 40, 512), lambda i: (0, 0, 0))] * 2
        + [pl.BlockSpec((8, 32, 256), lambda i: (0, 0, 0))] * 6
        + [block] * 4,
        out_specs=HBM,
        out_shape=pltpu.HBM((8, 128, 256), jnp.float32),
        scratch_shapes=[
            pltpu.VMEM((4096, 256), jnp.bfloat16),
            pltpu.VMEM((4096, 256), jnp.bfloat16),
            pltpu.VMEM((8, 128, 256), jnp.float32),
            pltpu.SemaphoreType.DMA((4,)),
        ],
        compiler_params=pltpu.CompilerParams(vmem_limit_bytes=40 * 2**20),
        cost_estimate=pl.CostEstimate(
            flops=3 * 2 * 1024 * 4096 * 256, bytes_accessed=18 * 2**20, transcendentals=0
        ),
        name="project",
    )(half, *raw, *beside, *[pltpu.with_memory_space_constraint(x, pltpu.HBM) for x in steered])


def half_of_vectors(pieces, half):
    lower = jnp.concatenate([pieces[..., :HALF], pieces[..., K : K + HALF]], axis=-1)
    upper = jnp.concatenate([pieces[..., HALF:K], pieces[..., K + HALF :]], axis=-1)
    return jnp.where(half == 0, lower, upper)


def by_core(tile, core):
    rows = tile.T.reshape(8, 2, 32, 512)
    return (
        jnp.where(core == 0, rows[:, 0], rows[:, 1]),
        jnp.where(core == 0, rows[:, 1], rows[:, 0]),
    )


def body(csm_real, csm_imag, start_block, mic_coords, grid_coords, bin_index):
    row = lax.axis_index("row")
    core = row % 2
    own_core = core.reshape(1)
    col = lax.axis_index("col")
    half = col % 2
    points = grid_coords.reshape(2, 4, 2, 256)
    points = jnp.where(col // 2 % 2 == 0, points[:, :, 0], points[:, :, 1]).reshape(2, 1024)
    reduced = ((bin_index * points) % MOD).astype(jnp.float32).T

    mine = exchange(spread_start(start_block), "row", Z_GROUPS)
    kept_real, sent_real = by_core(csm_real, core)
    kept_imag, sent_imag = by_core(csm_imag, core)
    kept_real, kept_imag, sent_real, sent_imag, mic_coords = lax.optimization_barrier(
        (kept_real, kept_imag, sent_real, sent_imag, mic_coords)
    )
    places = [mic_coords] + [lax.ppermute(mic_coords, "col", ALONG_X[flip]) for flip in (1, 2, 3)]
    mine, *places = lax.optimization_barrier((mine, *places))
    other = lax.ppermute(mine, "row", CORE_SWAP)
    first_partial = first_product(csm_real, csm_imag, mine, other, own_core)

    places = jnp.stack(places, axis=1).reshape(2, 4, 8, 2, 32)
    even, odd = places[:, :, :, 0], places[:, :, :, 1]
    mics = jnp.stack([jnp.where(core == 0, even, odd), jnp.where(core == 0, odd, even)], axis=2)
    mics = mics.reshape(2, 2048).astype(jnp.float32)
    steered = steering(reduced, mics, 0, 3)
    first_pieces = exchange(first_partial, "col")
    first_pieces, steered = lax.optimization_barrier((first_pieces, steered))

    steered = steering(reduced, mics, 3, 2, steered)
    first = exchange(spread(first_pieces, 16)[1], "col")
    first, steered = lax.optimization_barrier((first, steered))
    sent, gram_rows, parts = sent_product(sent_real, sent_imag, first, own_core)
    got = lax.ppermute(sent, "row", CORE_SWAP)
    kept = kept_product(kept_real, kept_imag, parts, gram_rows)
    pair = stage(kept, got)

    steered = steering(reduced, mics, 5, 2, steered)
    pieces = exchange(pair, "row", Z_GROUPS)
    pieces, steered = lax.optimization_barrier((pieces, steered))
    own, spread_out = spread(pieces, 8)

    steered = steering(reduced, mics, 7, 1, steered)
    mine = exchange(spread_out, "row", Z_GROUPS)
    mine, steered = lax.optimization_barrier((mine, steered))
    other = lax.ppermute(mine, "row", CORE_SWAP)
    taken = half_of_vectors(mine[:, :32], half)
    given = half_of_vectors(mine[:, :32], 1 - half)
    near = [
        lax.ppermute(taken if flip == 2 else given, "col", ALONG_X[flip]) for flip in (1, 2, 3)
    ]
    first_inverse = first_factor(mine, other, own_core)
    gram_copies = second_gram_slice(mine, other, first_inverse, row.reshape(1))
    near, gram_copies = lax.optimization_barrier((near, gram_copies))
    far = [lax.ppermute(block, "row", CORE_SWAP) for block in near]
    beside = [block for both in zip(near, far) for block in both]
    gram_pieces = exchange(gram_copies, "col")
    part = project(half.reshape(1), (mine, other), beside, steered)
    part, gram_pieces = lax.optimization_barrier((part, gram_pieces))
    pieces = exchange(part, "col", POINT_GROUPS)
    second_gram = lax.all_gather(jnp.sum(gram_pieces, axis=0), "row", axis=0, tiled=True)
    basis, both_inverse, weights = second_factor(second_gram, first_inverse, own)
    return (basis, finish(pieces, both_inverse, weights).reshape(128))


def solution(mesh):
    in_specs = (
        P("row", "col"),
        P("row", "col"),
        P(None, ("col", "row"), None),
        P(None, "col"),
        P(None, "row"),
        P(),
    )
    out_specs = (P(None, ("col", "row"), None), P(("row", "col")))
    return jax.shard_map(body, mesh=mesh, in_specs=in_specs, out_specs=out_specs, check_vma=False)
```

```python
import jax
import jax.numpy as jnp
from jax import lax
from jax.experimental import pallas as pl
from jax.experimental.pallas import tpu as pltpu
from jax.sharding import PartitionSpec as P

NU = 4
K = 256
MOD = 4093
HIGH = lax.Precision.HIGHEST

Z_GROUPS = [list(range(core, 16, 2)) for core in range(2)]
CORE_SWAP = [(index, index ^ 1) for index in range(16)]

ALONG_X = [[(index, index ^ flip) for index in range(16)] for flip in range(4)]
POINT_GROUPS = [[index for index in range(16) if index // 2 % 2 == part] for part in range(2)]
HALF = K // 2
SMEM = pl.BlockSpec(memory_space=pltpu.SMEM)
HBM = pl.BlockSpec(memory_space=pltpu.HBM)
VMEM = pl.BlockSpec(memory_space=pltpu.VMEM)

PANEL = 64
MICRO = 16


def dot(a, b):
    return jnp.dot(a, b, precision=HIGH, preferred_element_type=jnp.float32)


def dot_tn(a, b):
    return lax.dot_general(
        a, b, (((0,), (0,)), ((), ())), precision=HIGH, preferred_element_type=jnp.float32
    )


def dot_nt(a, b):
    return lax.dot_general(
        a, b, (((1,), (1,)), ((), ())), precision=HIGH, preferred_element_type=jnp.float32
    )


def eliminate(work_ref, upper_ref, inverse_ref):
    rows = lax.broadcasted_iota(jnp.int32, (K, K), 0)
    cols = lax.broadcasted_iota(jnp.int32, (K, K), 1)
    work_ref[:, K:] = (rows == cols).astype(jnp.float32)
    panel_row = lax.broadcasted_iota(jnp.int32, (PANEL, 128), 0)
    for start in range(0, K, PANEL):
        low = (start // 128) * 128
        high = K + ((start + PANEL + 127) // 128) * 128
        width = high - low
        offset = start - low
        panel = work_ref[start : start + PANEL, low:high]
        for first in range(0, PANEL, MICRO):
            columns = [
                jnp.broadcast_to(
                    panel[:, offset + first + k : offset + first + k + 1], (PANEL, 128)
                )
                for k in range(MICRO)
            ]
            for k in range(MICRO):
                j = first + k
                scale = jnp.where(panel_row > j, columns[k] * (1.0 / columns[k][j : j + 1, :]), 0.0)
                for later in range(k + 1, MICRO):
                    columns[later] = columns[later] - scale * columns[later][j : j + 1, :]
                panel = (
                    panel
                    - jnp.concatenate([scale] * (width // 128), axis=1) * panel[j : j + 1, :]
                )
        square_row = lax.broadcasted_iota(jnp.int32, (PANEL, PANEL), 0)
        square_col = lax.broadcasted_iota(jnp.int32, (PANEL, PANEL), 1)
        pivots = jnp.sum(
            jnp.where(square_row == square_col, panel[:, offset : offset + PANEL], 0.0),
            axis=1,
            keepdims=True,
        )
        panel = panel * (1.0 / jnp.sqrt(pivots))
        if upper_ref is not None:
            panel_cols = lax.broadcasted_iota(jnp.int32, (PANEL, K - low), 1) + low
            panel_rows = lax.broadcasted_iota(jnp.int32, (PANEL, K - low), 0) + start
            upper_ref[start : start + PANEL, :] = jnp.zeros((PANEL, K), jnp.float32)
            upper_ref[start : start + PANEL, low:K] = jnp.where(
                panel_cols >= panel_rows, panel[:, : K - low], 0.0
            )
        inverse_ref[start : start + PANEL, :] = jnp.zeros((PANEL, K), jnp.float32)
        inverse_ref[start : start + PANEL, : high - K] = panel[:, K - low :]
        after = start + PANEL
        if after < K:
            update = dot_tn(panel[:, after - low : K - low], panel)
            work_ref[after:, low:high] = work_ref[after:, low:high] - update


def first_factor_kernel(mine_ref, other_ref, core_ref, inverse_ref, work_ref):
    own = core_ref[0]
    for z in range(8):
        for core in range(2):
            part = jnp.where(own == core, mine_ref[z, 32:, :], other_ref[z, 32:, :])
            start = (2 * z + core) * 16
            work_ref[start : start + 8, :K] = part[:, :K]
            work_ref[start + 8 : start + 16, :K] = part[:, K:]
    eliminate(work_ref, None, inverse_ref)


def first_factor(mine, other, core):
    return pl.pallas_call(
        first_factor_kernel,
        out_shape=jax.ShapeDtypeStruct((K, K), jnp.float32),
        in_specs=[VMEM, VMEM, SMEM],
        out_specs=VMEM,
        scratch_shapes=[pltpu.VMEM((K, 2 * K), jnp.float32)],
        compiler_params=pltpu.CompilerParams(vmem_limit_bytes=16 * 2**20),
        cost_estimate=pl.CostEstimate(
            flops=4 * K**3, bytes_accessed=12 * K * K, transcendentals=K
        ),
        name="first_factor",
    )(mine, other, core)


def second_factor_kernel(
    gram_ref, first_ref, rows_ref, basis_ref, both_ref, weights_ref, upper_ref, inverse_ref, work_ref
):
    work_ref[:, :K] = gram_ref[...]
    eliminate(work_ref, upper_ref, inverse_ref)
    rows = lax.broadcasted_iota(jnp.int32, (K, K), 0)
    cols = lax.broadcasted_iota(jnp.int32, (K, K), 1)
    diagonal = jnp.sum(jnp.where(rows == cols, upper_ref[...], 0.0), axis=0, keepdims=True)
    weights_ref[...] = jnp.sqrt(jnp.sqrt(diagonal))
    both_ref[...] = dot(inverse_ref[...], first_ref[...])
    raw = jnp.concatenate([rows_ref[:32, :K], rows_ref[:32, K:]], axis=0)
    basis = dot_nt(dot_nt(raw, first_ref[...]), inverse_ref[...])
    basis_ref[0] = basis[:32]
    basis_ref[1] = basis[32:]


def second_factor(gram, first_inverse, rows):
    return pl.pallas_call(
        second_factor_kernel,
        out_shape=(
            jax.ShapeDtypeStruct((2, 32, K), jnp.float32),
            jax.ShapeDtypeStruct((K, K), jnp.float32),
            jax.ShapeDtypeStruct((1, K), jnp.float32),
        ),
        scratch_shapes=[
            pltpu.VMEM((K, K), jnp.float32),
            pltpu.VMEM((K, K), jnp.float32),
            pltpu.VMEM((K, 2 * K), jnp.float32),
        ],
        compiler_params=pltpu.CompilerParams(vmem_limit_bytes=16 * 2**20),
        cost_estimate=pl.CostEstimate(
            flops=6 * K**3, bytes_accessed=16 * K * K, transcendentals=K
        ),
        name="second_factor",
    )(gram, first_inverse, rows)


def finish_kernel(pieces_ref, both_ref, weights_ref, beam_ref):
    lower = pieces_ref[0]
    upper = pieces_ref[1]
    for index in range(2, 8, 2):
        lower = lower + pieces_ref[index]
        upper = upper + pieces_ref[index + 1]
    real_part = jnp.concatenate([lower[:, :HALF], upper[:, :HALF]], axis=1)
    imag_part = jnp.concatenate([lower[:, HALF:], upper[:, HALF:]], axis=1)
    projected = dot_nt(jnp.concatenate([real_part, imag_part], axis=0), both_ref[...])
    square = projected * projected
    weights = weights_ref[...]
    power = dot_nt(weights, square[:128] + square[128:]) / jnp.sum(weights)
    power = power * power
    beam_ref[...] = power * power


def finish(pieces, both, weights):
    return pl.pallas_call(
        finish_kernel,
        out_shape=jax.ShapeDtypeStruct((1, 128), jnp.float32),
        compiler_params=pltpu.CompilerParams(vmem_limit_bytes=16 * 2**20),
        name="finish",
    )(pieces, both, weights)


def turned(block):
    return jnp.concatenate([-block[:, K:], block[:, :K]], axis=1)


def exchange(pieces, axis, groups=None):
    return lax.all_to_all(pieces, axis, 0, 0, tiled=True, axis_index_groups=groups)


def drain(copies):
    for copy in copies:
        copy.start()
    for copy in copies:
        copy.wait()


def spread_kernel(pieces_ref, total_ref, copies_ref, sems):
    total_ref[...] = jnp.sum(pieces_ref[...], axis=0)
    drain(
        [
            pltpu.make_async_copy(total_ref, copies_ref.at[index], sems.at[index])
            for index in range(copies_ref.shape[0])
        ]
    )


def spread(pieces, count):
    piece = pieces.shape[1:]
    return pl.pallas_call(
        spread_kernel,
        out_shape=(
            jax.ShapeDtypeStruct(piece, jnp.float32),
            pltpu.HBM((count,) + piece, jnp.float32),
        ),
        out_specs=(
            pl.BlockSpec(memory_space=pltpu.VMEM),
            pl.BlockSpec(memory_space=pltpu.HBM),
        ),
        scratch_shapes=[pltpu.SemaphoreType.DMA((count,))],
        compiler_params=pltpu.CompilerParams(vmem_limit_bytes=16 * 2**20),
        name="spread",
    )(pieces)


def halves(value):
    high = value.astype(jnp.bfloat16)
    return high, (value - high.astype(jnp.float32)).astype(jnp.bfloat16)


def split_dot(high, low, parts):
    total = jnp.dot(low, parts[0], preferred_element_type=jnp.float32)
    total += jnp.dot(high, parts[1], preferred_element_type=jnp.float32)
    return total + jnp.dot(high, parts[0], preferred_element_type=jnp.float32)


def prepare_kernel(
    real_ref, imag_ref, core_ref, tile_high, tile_low, kept_high, kept_low, sent_high, sent_low
):
    first_core = core_ref[0] == 0
    for base, ref in ((0, real_ref), (512, imag_ref)):
        lanes = slice(base, base + 512)
        value = ref[...]
        tile_high[:, lanes], tile_low[:, lanes] = halves(value)
        rows = value.T.reshape(8, 2, 32, 512)
        kept = jnp.where(first_core, rows[:, 0], rows[:, 1]).reshape(256, 512)
        sent = jnp.where(first_core, rows[:, 1], rows[:, 0]).reshape(256, 512)
        kept_high[:, lanes], kept_low[:, lanes] = halves(kept)
        sent_high[:, lanes], sent_low[:, lanes] = halves(sent)


def prepare(real, imag, core):
    shapes = [(512, 1024)] * 2 + [(256, 1024)] * 4
    return pl.pallas_call(
        prepare_kernel,
        out_shape=tuple(pltpu.VMEM(shape, jnp.bfloat16) for shape in shapes),
        in_specs=[VMEM, VMEM, SMEM],
        out_specs=(VMEM,) * 6,
        compiler_params=pltpu.CompilerParams(vmem_limit_bytes=24 * 2**20),
        cost_estimate=pl.CostEstimate(
            flops=20 * 512 * 1024, bytes_accessed=8 * 2**20, transcendentals=0
        ),
        name="prepare",
    )(real, imag, core)


def first_product_kernel(
    high_ref, low_ref, mine_ref, other_ref, core_ref, out_ref, start_ref, parts_ref, rows_ref, sems
):
    core = core_ref[0]
    for z in range(8):
        start_ref[2 * z + core] = mine_ref[z]
        start_ref[2 * z + 1 - core] = other_ref[z]
    start = start_ref[...].reshape(512, 2 * K)
    for base, value in ((0, start), (512, turned(start))):
        for index, part in enumerate(halves(value)):
            parts_ref[index, base : base + 512, :] = part
    parts = [parts_ref[index] for index in range(2)]
    copies = []
    for block in range(4):
        at = slice(block * 128, block * 128 + 128)
        product = split_dot(high_ref[at, :], low_ref[at, :], parts)
        four = pl.ds(block * 4, 4)
        rows_ref[four] = product.reshape(4, 32, 2 * K)
        copies.append(
            pltpu.make_async_copy(rows_ref.at[four], out_ref.at[four], sems.at[block])
        )
        copies[-1].start()
    for copy in copies:
        copy.wait()


def first_product(high, low, mine, other, core):
    return pl.pallas_call(
        first_product_kernel,
        out_shape=pltpu.HBM((16, 32, 2 * K), jnp.float32),
        in_specs=[VMEM] * 4 + [SMEM],
        out_specs=HBM,
        scratch_shapes=[
            pltpu.VMEM((16, 32, 2 * K), jnp.float32),
            pltpu.VMEM((2, 1024, 2 * K), jnp.bfloat16),
            pltpu.VMEM((16, 32, 2 * K), jnp.float32),
            pltpu.SemaphoreType.DMA((4,)),
        ],
        compiler_params=pltpu.CompilerParams(vmem_limit_bytes=24 * 2**20),
        cost_estimate=pl.CostEstimate(
            flops=6 * 512 * 1024 * 512, bytes_accessed=5 * 2**20, transcendentals=0
        ),
        name="first_product",
    )(high, low, mine, other, core)


def sent_product_kernel(
    high_ref, low_ref, first_ref, core_ref, out_ref, kept_ref, parts_ref, gram_ref
):
    first = first_ref[...].reshape(512, 2 * K)
    for base, value in ((0, first), (512, -turned(first))):
        for index, part in enumerate(halves(value)):
            parts_ref[index, base : base + 512, :] = part
    rows = jnp.concatenate([first[:, :K], first[:, K:]], axis=0)
    gram_ref[...] = dot_tn(rows, rows)
    core = core_ref[0]
    for z in range(8):
        for which, target, at in ((core, kept_ref, 0), (1 - core, out_ref, 32)):
            start = pl.multiple_of(z * 32 + which * 16, 16)
            target[z, at : at + 8, :K] = gram_ref[pl.ds(start, 8), :]
            target[z, at : at + 8, K:] = gram_ref[pl.ds(start + 8, 8), :]
    share(high_ref, low_ref, parts_ref, out_ref)


def share(high_ref, low_ref, parts_ref, out_ref):
    parts = [parts_ref[index] for index in range(2)]
    for block in range(2):
        at = slice(block * 128, block * 128 + 128)
        product = split_dot(high_ref[at, :], low_ref[at, :], parts)
        out_ref[block * 4 : block * 4 + 4, :32, :] = product.reshape(4, 32, 2 * K)


def sent_product(high, low, first, core):
    return pl.pallas_call(
        sent_product_kernel,
        out_shape=(
            jax.ShapeDtypeStruct((8, 40, 2 * K), jnp.float32),
            jax.ShapeDtypeStruct((8, 8, 2 * K), jnp.float32),
            jax.ShapeDtypeStruct((2, 1024, 2 * K), jnp.bfloat16),
        ),
        in_specs=[VMEM] * 3 + [SMEM],
        out_specs=(VMEM,) * 3,
        scratch_shapes=[pltpu.VMEM((K, K), jnp.float32)],
        compiler_params=pltpu.CompilerParams(vmem_limit_bytes=24 * 2**20),
        cost_estimate=pl.CostEstimate(
            flops=6 * 256 * 1024 * 512, bytes_accessed=5 * 2**20, transcendentals=0
        ),
        name="sent_product",
    )(high, low, first, core)


def kept_product_kernel(high_ref, low_ref, parts_ref, gram_ref, out_ref):
    out_ref[:, 32:, :] = gram_ref[...]
    share(high_ref, low_ref, parts_ref, out_ref)


def kept_product(high, low, parts, gram):
    return pl.pallas_call(
        kept_product_kernel,
        out_shape=jax.ShapeDtypeStruct((8, 40, 2 * K), jnp.float32),
        in_specs=[VMEM] * 4,
        out_specs=VMEM,
        compiler_params=pltpu.CompilerParams(vmem_limit_bytes=24 * 2**20),
        cost_estimate=pl.CostEstimate(
            flops=6 * 256 * 1024 * 512, bytes_accessed=5 * 2**20, transcendentals=0
        ),
        name="kept_product",
    )(high, low, parts, gram)


def stage_kernel(*refs):
    terms, out_ref, total_ref, sem = refs[:-3], refs[-3], refs[-2], refs[-1]
    total = terms[0][...]
    for term in terms[1:]:
        total = total + term[...]
    total_ref[...] = total
    drain([pltpu.make_async_copy(total_ref, out_ref, sem)])


def stage(*terms):
    shape = jax.ShapeDtypeStruct(terms[0].shape, jnp.float32)
    return pl.pallas_call(
        stage_kernel,
        out_shape=pltpu.HBM(shape.shape, jnp.float32),
        out_specs=pl.BlockSpec(memory_space=pltpu.HBM),
        scratch_shapes=[pltpu.VMEM(shape.shape, jnp.float32), pltpu.SemaphoreType.DMA],
        compiler_params=pltpu.CompilerParams(vmem_limit_bytes=16 * 2**20),
        name="stage",
    )(*terms)


SIN_TERMS = (
    3.1415926535362906,
    -5.167712764624546,
    2.550163318947043,
    -0.5992521978220368,
    0.08205040179571269,
    -0.007028386383306818,
)
COS_TERMS = (
    0.9999999997799041,
    -4.9348021370788295,
    4.058709159556314,
    -1.335212003049894,
    0.23493731381328964,
    -0.024396324346460163,
)


def polynomial(terms, x):
    value = terms[-1]
    for term in terms[-2::-1]:
        value = value * x + term
    return value


def spread_start_kernel(start_ref, copies_ref, total_ref, sems):
    total_ref[:, :K] = start_ref[0]
    total_ref[:, K:] = start_ref[1]
    drain(
        [
            pltpu.make_async_copy(total_ref, copies_ref.at[index], sems.at[index])
            for index in range(8)
        ]
    )


def spread_start(start):
    return pl.pallas_call(
        spread_start_kernel,
        out_shape=pltpu.HBM((8, 32, 2 * K), jnp.float32),
        in_specs=[VMEM],
        out_specs=HBM,
        scratch_shapes=[pltpu.VMEM((32, 2 * K), jnp.float32), pltpu.SemaphoreType.DMA((8,))],
        compiler_params=pltpu.CompilerParams(vmem_limit_bytes=8 * 2**20),
        name="spread_start",
    )(start)


def steering_kernel(grid_ref, mics_ref, *refs):
    index = (
        grid_ref[:, 0:1] * mics_ref[0:1, :] + grid_ref[:, 1:2] * mics_ref[1:2, :]
    )
    turns = (index - jnp.round(index * (1.0 / MOD)) * float(MOD)) * (1.0 / MOD)
    square = turns * turns
    half_sine = turns * polynomial(SIN_TERMS, square)
    half_cosine = polynomial(COS_TERMS, square)
    cosine = 1.0 - 2.0 * half_sine * half_sine
    sine = 2.0 * half_sine * half_cosine
    for value, high_ref, low_ref in ((cosine, refs[-4], refs[-3]), (sine, refs[-2], refs[-1])):
        high_ref[...], low_ref[...] = halves(value)


def steering(grid, mics, first, count, before=()):
    block = pl.BlockSpec((256, 1024), lambda i: ((i + first) // 2, (i + first) % 2))
    return pl.pallas_call(
        steering_kernel,
        grid=(count,),
        in_specs=[
            pl.BlockSpec((256, 2), lambda i: ((i + first) // 2, 0)),
            pl.BlockSpec((2, 1024), lambda i: (0, (i + first) % 2)),
        ]
        + [HBM] * len(before),
        out_specs=(block,) * 4,
        out_shape=(pltpu.HBM((1024, 2048), jnp.bfloat16),) * 4,
        input_output_aliases={2 + index: index for index in range(len(before))},
        compiler_params=pltpu.CompilerParams(vmem_limit_bytes=24 * 2**20),
        cost_estimate=pl.CostEstimate(
            flops=45 * 256 * 1024 * count, bytes_accessed=8 * 256 * 1024 * count, transcendentals=0
        ),
        name="steering",
    )(grid, mics, *before)


def second_gram_kernel(mine_ref, other_ref, inverse_ref, row_ref, copies_ref, slice_ref, sems):
    own = pl.multiple_of(row_ref[0] * 16, 16)
    raw = jnp.concatenate(
        [
            ref[:, :32, lanes].reshape(256, K)
            for ref in (mine_ref, other_ref)
            for lanes in (slice(0, K), slice(K, 2 * K))
        ],
        axis=0,
    )
    second = dot_nt(raw, inverse_ref[...])
    turned_slice = dot_nt(inverse_ref[pl.ds(own, 16), :], raw)
    slice_ref[...] = dot(turned_slice, second)
    drain(
        [
            pltpu.make_async_copy(slice_ref, copies_ref.at[index], sems.at[index])
            for index in range(16)
        ]
    )


def second_gram_slice(mine, other, inverse, row):
    return pl.pallas_call(
        second_gram_kernel,
        out_shape=pltpu.HBM((16, 16, K), jnp.float32),
        in_specs=[VMEM, VMEM, VMEM, SMEM],
        out_specs=HBM,
        scratch_shapes=[pltpu.VMEM((16, K), jnp.float32), pltpu.SemaphoreType.DMA((16,))],
        compiler_params=pltpu.CompilerParams(vmem_limit_bytes=24 * 2**20),
        cost_estimate=pl.CostEstimate(
            flops=2 * 1024 * K * (K + 32), bytes_accessed=2**21, transcendentals=0
        ),
        name="second_gram",
    )(mine, other, inverse, row)


def project_kernel(half_ref, *refs):
    raw_refs, beside_refs = refs[:2], refs[2:8]
    cos_high, cos_low, sin_high, sin_low = refs[8:12]
    out_ref, high_ref, low_ref, slots, sems = refs[12:]
    step = pl.program_id(0)

    @pl.when(step == 0)
    def _():
        lower = half_ref[0] == 0
        sources = []
        for ref in raw_refs:
            parts = [
                ref[:, :32, lane : lane + HALF].reshape(256, HALF) for lane in range(0, 2 * K, HALF)
            ]
            sources.append(
                (jnp.where(lower, parts[0], parts[1]), jnp.where(lower, parts[2], parts[3]))
            )
        for ref in beside_refs:
            sources.append((ref[:, :, :HALF].reshape(256, HALF), ref[:, :, HALF:].reshape(256, HALF)))
        for index, (real, imag) in enumerate(sources):
            start = index * 256
            for base, value in (
                (0, jnp.concatenate([real, imag], axis=1)),
                (2048, jnp.concatenate([-imag, real], axis=1)),
            ):
                high, low = halves(value)
                high_ref[base + start : base + start + 256, :] = high
                low_ref[base + start : base + start + 256, :] = low

    high = jnp.concatenate([cos_high[...], sin_high[...]], axis=1)
    low = jnp.concatenate([cos_low[...], sin_low[...]], axis=1)
    product = jnp.dot(high, high_ref[...], preferred_element_type=jnp.float32)
    product += jnp.dot(high, low_ref[...], preferred_element_type=jnp.float32)
    product += jnp.dot(low, high_ref[...], preferred_element_type=jnp.float32)
    slots[pl.ds(2 * step, 2)] = product.reshape(2, 128, 256)

    def copy(index):
        both = pl.ds(2 * index, 2)
        return pltpu.make_async_copy(slots.at[both], out_ref.at[both], sems.at[index])

    copy(step).start()

    @pl.when(step == 3)
    def _():
        for index in range(4):
            copy(index).wait()


def project(half, raw, beside, steered):
    block = pl.BlockSpec((256, 2048), lambda i: (i, 0))
    return pl.pallas_call(
        project_kernel,
        grid=(4,),
        in_specs=[SMEM]
        + [pl.BlockSpec((8, 40, 512), lambda i: (0, 0, 0))] * 2
        + [pl.BlockSpec((8, 32, 256), lambda i: (0, 0, 0))] * 6
        + [block] * 4,
        out_specs=HBM,
        out_shape=pltpu.HBM((8, 128, 256), jnp.float32),
        scratch_shapes=[
            pltpu.VMEM((4096, 256), jnp.bfloat16),
            pltpu.VMEM((4096, 256), jnp.bfloat16),
            pltpu.VMEM((8, 128, 256), jnp.float32),
            pltpu.SemaphoreType.DMA((4,)),
        ],
        compiler_params=pltpu.CompilerParams(vmem_limit_bytes=40 * 2**20),
        cost_estimate=pl.CostEstimate(
            flops=3 * 2 * 1024 * 4096 * 256, bytes_accessed=18 * 2**20, transcendentals=0
        ),
        name="project",
    )(half, *raw, *beside, *[pltpu.with_memory_space_constraint(x, pltpu.HBM) for x in steered])


def half_of_vectors(pieces, half):
    lower = jnp.concatenate([pieces[..., :HALF], pieces[..., K : K + HALF]], axis=-1)
    upper = jnp.concatenate([pieces[..., HALF:K], pieces[..., K + HALF :]], axis=-1)
    return jnp.where(half == 0, lower, upper)


def body(csm_real, csm_imag, start_block, mic_coords, grid_coords, bin_index):
    row = lax.axis_index("row")
    core = row % 2
    own_core = core.reshape(1)
    col = lax.axis_index("col")
    half = col % 2
    points = grid_coords.reshape(2, 4, 2, 256)
    points = jnp.where(col // 2 % 2 == 0, points[:, :, 0], points[:, :, 1]).reshape(2, 1024)
    reduced = ((bin_index * points) % MOD).astype(jnp.float32).T

    mine = exchange(spread_start(start_block), "row", Z_GROUPS)
    *tiles, mic_coords = lax.optimization_barrier(
        (*prepare(csm_real, csm_imag, own_core), mic_coords)
    )
    places = [mic_coords] + [lax.ppermute(mic_coords, "col", ALONG_X[flip]) for flip in (1, 2, 3)]
    mine, *places = lax.optimization_barrier((mine, *places, *tiles))
    places, tiles = places[:4], places[4:]
    other = lax.ppermute(mine, "row", CORE_SWAP)
    first_partial = first_product(*tiles[:2], mine, other, own_core)

    places = jnp.stack(places, axis=1).reshape(2, 4, 8, 2, 32)
    even, odd = places[:, :, :, 0], places[:, :, :, 1]
    mics = jnp.stack([jnp.where(core == 0, even, odd), jnp.where(core == 0, odd, even)], axis=2)
    mics = mics.reshape(2, 2048).astype(jnp.float32)
    steered = steering(reduced, mics, 0, 3)
    first_pieces = exchange(first_partial, "col")
    first_pieces, steered = lax.optimization_barrier((first_pieces, steered))

    steered = steering(reduced, mics, 3, 2, steered)
    first = exchange(spread(first_pieces, 16)[1], "col")
    first, steered = lax.optimization_barrier((first, steered))
    sent, gram_rows, parts = sent_product(*tiles[4:], first, own_core)
    got = lax.ppermute(sent, "row", CORE_SWAP)
    kept = kept_product(*tiles[2:4], parts, gram_rows)
    pair = stage(kept, got)

    steered = steering(reduced, mics, 5, 2, steered)
    pieces = exchange(pair, "row", Z_GROUPS)
    pieces, steered = lax.optimization_barrier((pieces, steered))
    own, spread_out = spread(pieces, 8)

    steered = steering(reduced, mics, 7, 1, steered)
    mine = exchange(spread_out, "row", Z_GROUPS)
    mine, steered = lax.optimization_barrier((mine, steered))
    other = lax.ppermute(mine, "row", CORE_SWAP)
    taken = half_of_vectors(mine[:, :32], half)
    given = half_of_vectors(mine[:, :32], 1 - half)
    near = [
        lax.ppermute(taken if flip == 2 else given, "col", ALONG_X[flip]) for flip in (1, 2, 3)
    ]
    first_inverse = first_factor(mine, other, own_core)
    gram_copies = second_gram_slice(mine, other, first_inverse, row.reshape(1))
    near, gram_copies = lax.optimization_barrier((near, gram_copies))
    far = [lax.ppermute(block, "row", CORE_SWAP) for block in near]
    beside = [block for both in zip(near, far) for block in both]
    gram_pieces = exchange(gram_copies, "col")
    part = project(half.reshape(1), (mine, other), beside, steered)
    part, gram_pieces = lax.optimization_barrier((part, gram_pieces))
    pieces = exchange(part, "col", POINT_GROUPS)
    second_gram = lax.all_gather(jnp.sum(gram_pieces, axis=0), "row", axis=0, tiled=True)
    basis, both_inverse, weights = second_factor(second_gram, first_inverse, own)
    return (basis, finish(pieces, both_inverse, weights).reshape(128))


def solution(mesh):
    in_specs = (
        P("row", "col"),
        P("row", "col"),
        P(None, ("col", "row"), None),
        P(None, "col"),
        P(None, "row"),
        P(),
    )
    out_specs = (P(None, ("col", "row"), None), P(("row", "col")))
    return jax.shard_map(body, mesh=mesh, in_specs=in_specs, out_specs=out_specs, check_vma=False)
```

```python
import jax
import jax.numpy as jnp
from jax import lax
from jax.experimental import pallas as pl
from jax.experimental.pallas import tpu as pltpu
from jax.sharding import PartitionSpec as P

NU = 4
K = 256
MOD = 4093
HIGH = lax.Precision.HIGHEST

Z_GROUPS = [list(range(core, 16, 2)) for core in range(2)]
CORE_SWAP = [(index, index ^ 1) for index in range(16)]

ALONG_X = [[(index, index ^ flip) for index in range(16)] for flip in range(4)]
POINT_GROUPS = [[index for index in range(16) if index // 2 % 2 == part] for part in range(2)]
HALF = K // 2
SMEM = pl.BlockSpec(memory_space=pltpu.SMEM)
HBM = pl.BlockSpec(memory_space=pltpu.HBM)
VMEM = pl.BlockSpec(memory_space=pltpu.VMEM)

PANEL = 64
MICRO = 16


def dot(a, b):
    return jnp.dot(a, b, precision=HIGH, preferred_element_type=jnp.float32)


def dot_tn(a, b):
    return lax.dot_general(
        a, b, (((0,), (0,)), ((), ())), precision=HIGH, preferred_element_type=jnp.float32
    )


def dot_nt(a, b):
    return lax.dot_general(
        a, b, (((1,), (1,)), ((), ())), precision=HIGH, preferred_element_type=jnp.float32
    )


def eliminate(work_ref, upper_ref, inverse_ref):
    rows = lax.broadcasted_iota(jnp.int32, (K, K), 0)
    cols = lax.broadcasted_iota(jnp.int32, (K, K), 1)
    work_ref[:, K:] = (rows == cols).astype(jnp.float32)
    panel_row = lax.broadcasted_iota(jnp.int32, (PANEL, 128), 0)
    for start in range(0, K, PANEL):
        low = (start // 128) * 128
        high = K + ((start + PANEL + 127) // 128) * 128
        width = high - low
        offset = start - low
        panel = work_ref[start : start + PANEL, low:high]
        for first in range(0, PANEL, MICRO):
            columns = [
                jnp.broadcast_to(
                    panel[:, offset + first + k : offset + first + k + 1], (PANEL, 128)
                )
                for k in range(MICRO)
            ]
            for k in range(MICRO):
                j = first + k
                scale = jnp.where(panel_row > j, columns[k] * (1.0 / columns[k][j : j + 1, :]), 0.0)
                for later in range(k + 1, MICRO):
                    columns[later] = columns[later] - scale * columns[later][j : j + 1, :]
                panel = (
                    panel
                    - jnp.concatenate([scale] * (width // 128), axis=1) * panel[j : j + 1, :]
                )
        square_row = lax.broadcasted_iota(jnp.int32, (PANEL, PANEL), 0)
        square_col = lax.broadcasted_iota(jnp.int32, (PANEL, PANEL), 1)
        pivots = jnp.sum(
            jnp.where(square_row == square_col, panel[:, offset : offset + PANEL], 0.0),
            axis=1,
            keepdims=True,
        )
        panel = panel * (1.0 / jnp.sqrt(pivots))
        if upper_ref is not None:
            panel_cols = lax.broadcasted_iota(jnp.int32, (PANEL, K - low), 1) + low
            panel_rows = lax.broadcasted_iota(jnp.int32, (PANEL, K - low), 0) + start
            upper_ref[start : start + PANEL, :] = jnp.zeros((PANEL, K), jnp.float32)
            upper_ref[start : start + PANEL, low:K] = jnp.where(
                panel_cols >= panel_rows, panel[:, : K - low], 0.0
            )
        inverse_ref[start : start + PANEL, :] = jnp.zeros((PANEL, K), jnp.float32)
        inverse_ref[start : start + PANEL, : high - K] = panel[:, K - low :]
        after = start + PANEL
        if after < K:
            update = dot_tn(panel[:, after - low : K - low], panel)
            work_ref[after:, low:high] = work_ref[after:, low:high] - update


def first_factor_kernel(mine_ref, other_ref, core_ref, inverse_ref, work_ref):
    own = core_ref[0]
    for z in range(8):
        for core in range(2):
            part = jnp.where(own == core, mine_ref[z, 32:, :], other_ref[z, 32:, :])
            start = (2 * z + core) * 16
            work_ref[start : start + 8, :K] = part[:, :K]
            work_ref[start + 8 : start + 16, :K] = part[:, K:]
    eliminate(work_ref, None, inverse_ref)


def first_factor(mine, other, core):
    return pl.pallas_call(
        first_factor_kernel,
        out_shape=jax.ShapeDtypeStruct((K, K), jnp.float32),
        in_specs=[VMEM, VMEM, SMEM],
        out_specs=VMEM,
        scratch_shapes=[pltpu.VMEM((K, 2 * K), jnp.float32)],
        compiler_params=pltpu.CompilerParams(vmem_limit_bytes=16 * 2**20),
        cost_estimate=pl.CostEstimate(
            flops=4 * K**3, bytes_accessed=12 * K * K, transcendentals=K
        ),
        name="first_factor",
    )(mine, other, core)


def second_factor_kernel(
    gram_ref, first_ref, rows_ref, basis_ref, both_ref, weights_ref, upper_ref, inverse_ref, work_ref
):
    work_ref[:, :K] = gram_ref[...]
    eliminate(work_ref, upper_ref, inverse_ref)
    rows = lax.broadcasted_iota(jnp.int32, (K, K), 0)
    cols = lax.broadcasted_iota(jnp.int32, (K, K), 1)
    diagonal = jnp.sum(jnp.where(rows == cols, upper_ref[...], 0.0), axis=0, keepdims=True)
    weights_ref[...] = jnp.sqrt(jnp.sqrt(diagonal))
    both_ref[...] = dot(inverse_ref[...], first_ref[...])
    raw = jnp.concatenate([rows_ref[:32, :K], rows_ref[:32, K:]], axis=0)
    basis = dot_nt(dot_nt(raw, first_ref[...]), inverse_ref[...])
    basis_ref[0] = basis[:32]
    basis_ref[1] = basis[32:]


def second_factor(gram, first_inverse, rows):
    return pl.pallas_call(
        second_factor_kernel,
        out_shape=(
            jax.ShapeDtypeStruct((2, 32, K), jnp.float32),
            jax.ShapeDtypeStruct((K, K), jnp.float32),
            jax.ShapeDtypeStruct((1, K), jnp.float32),
        ),
        scratch_shapes=[
            pltpu.VMEM((K, K), jnp.float32),
            pltpu.VMEM((K, K), jnp.float32),
            pltpu.VMEM((K, 2 * K), jnp.float32),
        ],
        compiler_params=pltpu.CompilerParams(vmem_limit_bytes=16 * 2**20),
        cost_estimate=pl.CostEstimate(
            flops=6 * K**3, bytes_accessed=16 * K * K, transcendentals=K
        ),
        name="second_factor",
    )(gram, first_inverse, rows)


def finish_kernel(pieces_ref, both_ref, weights_ref, beam_ref):
    lower = pieces_ref[0]
    upper = pieces_ref[1]
    for index in range(2, 8, 2):
        lower = lower + pieces_ref[index]
        upper = upper + pieces_ref[index + 1]
    real_part = jnp.concatenate([lower[:, :HALF], upper[:, :HALF]], axis=1)
    imag_part = jnp.concatenate([lower[:, HALF:], upper[:, HALF:]], axis=1)
    projected = dot_nt(jnp.concatenate([real_part, imag_part], axis=0), both_ref[...])
    square = projected * projected
    weights = weights_ref[...]
    power = dot_nt(weights, square[:128] + square[128:]) / jnp.sum(weights)
    power = power * power
    beam_ref[...] = power * power


def finish(pieces, both, weights):
    return pl.pallas_call(
        finish_kernel,
        out_shape=jax.ShapeDtypeStruct((1, 128), jnp.float32),
        compiler_params=pltpu.CompilerParams(vmem_limit_bytes=16 * 2**20),
        name="finish",
    )(pieces, both, weights)


def turned(block):
    return jnp.concatenate([-block[:, K:], block[:, :K]], axis=1)


def exchange(pieces, axis, groups=None):
    return lax.all_to_all(pieces, axis, 0, 0, tiled=True, axis_index_groups=groups)


def drain(copies):
    for copy in copies:
        copy.start()
    for copy in copies:
        copy.wait()


def spread_kernel(pieces_ref, total_ref, copies_ref, sems):
    total_ref[...] = jnp.sum(pieces_ref[...], axis=0)
    drain(
        [
            pltpu.make_async_copy(total_ref, copies_ref.at[index], sems.at[index])
            for index in range(copies_ref.shape[0])
        ]
    )


def spread(pieces, count):
    piece = pieces.shape[1:]
    return pl.pallas_call(
        spread_kernel,
        out_shape=(
            jax.ShapeDtypeStruct(piece, jnp.float32),
            pltpu.HBM((count,) + piece, jnp.float32),
        ),
        out_specs=(
            pl.BlockSpec(memory_space=pltpu.VMEM),
            pl.BlockSpec(memory_space=pltpu.HBM),
        ),
        scratch_shapes=[pltpu.SemaphoreType.DMA((count,))],
        compiler_params=pltpu.CompilerParams(vmem_limit_bytes=16 * 2**20),
        name="spread",
    )(pieces)


def halves(value):
    high = value.astype(jnp.bfloat16)
    return high, (value - high.astype(jnp.float32)).astype(jnp.bfloat16)


def split_dot(high, low, parts):
    total = jnp.dot(low, parts[0], preferred_element_type=jnp.float32)
    total += jnp.dot(high, parts[1], preferred_element_type=jnp.float32)
    return total + jnp.dot(high, parts[0], preferred_element_type=jnp.float32)


def in_vmem(value):
    return pltpu.with_memory_space_constraint(value, pltpu.VMEM)


def prepare_kernel(
    real_ref, imag_ref, core_ref, tile_high, tile_low, kept_high, kept_low, sent_high, sent_low
):
    first_core = core_ref[0] == 0
    for base, ref in ((0, real_ref), (512, imag_ref)):
        lanes = slice(base, base + 512)
        value = ref[...]
        tile_high[:, lanes], tile_low[:, lanes] = halves(value)
        rows = value.T.reshape(8, 2, 32, 512)
        kept = jnp.where(first_core, rows[:, 0], rows[:, 1]).reshape(256, 512)
        sent = jnp.where(first_core, rows[:, 1], rows[:, 0]).reshape(256, 512)
        kept_high[:, lanes], kept_low[:, lanes] = halves(kept)
        sent_high[:, lanes], sent_low[:, lanes] = halves(sent)


def prepare(real, imag, core):
    shapes = [(512, 1024)] * 2 + [(256, 1024)] * 4
    return pl.pallas_call(
        prepare_kernel,
        out_shape=tuple(pltpu.VMEM(shape, jnp.bfloat16) for shape in shapes),
        in_specs=[VMEM, VMEM, SMEM],
        out_specs=(VMEM,) * 6,
        compiler_params=pltpu.CompilerParams(vmem_limit_bytes=24 * 2**20),
        cost_estimate=pl.CostEstimate(
            flops=20 * 512 * 1024, bytes_accessed=8 * 2**20, transcendentals=0
        ),
        name="prepare",
    )(real, imag, core)


def first_product_kernel(
    high_ref, low_ref, mine_ref, other_ref, core_ref, out_ref, start_ref, parts_ref, rows_ref, sems
):
    core = core_ref[0]
    for z in range(8):
        start_ref[2 * z + core] = mine_ref[z]
        start_ref[2 * z + 1 - core] = other_ref[z]
    start = start_ref[...].reshape(512, 2 * K)
    for base, value in ((0, start), (512, turned(start))):
        for index, part in enumerate(halves(value)):
            parts_ref[index, base : base + 512, :] = part
    parts = [parts_ref[index] for index in range(2)]
    copies = []
    for block in range(4):
        at = slice(block * 128, block * 128 + 128)
        product = split_dot(high_ref[at, :], low_ref[at, :], parts)
        four = pl.ds(block * 4, 4)
        rows_ref[four] = product.reshape(4, 32, 2 * K)
        copies.append(
            pltpu.make_async_copy(rows_ref.at[four], out_ref.at[four], sems.at[block])
        )
        copies[-1].start()
    for copy in copies:
        copy.wait()


def first_product(high, low, mine, other, core):
    return pl.pallas_call(
        first_product_kernel,
        out_shape=pltpu.HBM((16, 32, 2 * K), jnp.float32),
        in_specs=[VMEM] * 4 + [SMEM],
        out_specs=HBM,
        scratch_shapes=[
            pltpu.VMEM((16, 32, 2 * K), jnp.float32),
            pltpu.VMEM((2, 1024, 2 * K), jnp.bfloat16),
            pltpu.VMEM((16, 32, 2 * K), jnp.float32),
            pltpu.SemaphoreType.DMA((4,)),
        ],
        compiler_params=pltpu.CompilerParams(vmem_limit_bytes=24 * 2**20),
        cost_estimate=pl.CostEstimate(
            flops=6 * 512 * 1024 * 512, bytes_accessed=5 * 2**20, transcendentals=0
        ),
        name="first_product",
    )(in_vmem(high), in_vmem(low), mine, other, core)


def sent_product_kernel(
    high_ref, low_ref, first_ref, core_ref, out_ref, kept_ref, parts_ref, gram_ref
):
    first = first_ref[...].reshape(512, 2 * K)
    for base, value in ((0, first), (512, -turned(first))):
        for index, part in enumerate(halves(value)):
            parts_ref[index, base : base + 512, :] = part
    rows = jnp.concatenate([first[:, :K], first[:, K:]], axis=0)
    gram_ref[...] = dot_tn(rows, rows)
    core = core_ref[0]
    for z in range(8):
        for which, target, at in ((core, kept_ref, 0), (1 - core, out_ref, 32)):
            start = pl.multiple_of(z * 32 + which * 16, 16)
            target[z, at : at + 8, :K] = gram_ref[pl.ds(start, 8), :]
            target[z, at : at + 8, K:] = gram_ref[pl.ds(start + 8, 8), :]
    share(high_ref, low_ref, parts_ref, out_ref)


def share(high_ref, low_ref, parts_ref, out_ref):
    parts = [parts_ref[index] for index in range(2)]
    for block in range(2):
        at = slice(block * 128, block * 128 + 128)
        product = split_dot(high_ref[at, :], low_ref[at, :], parts)
        out_ref[block * 4 : block * 4 + 4, :32, :] = product.reshape(4, 32, 2 * K)


def sent_product(high, low, first, core):
    return pl.pallas_call(
        sent_product_kernel,
        out_shape=(
            jax.ShapeDtypeStruct((8, 40, 2 * K), jnp.float32),
            jax.ShapeDtypeStruct((8, 8, 2 * K), jnp.float32),
            jax.ShapeDtypeStruct((2, 1024, 2 * K), jnp.bfloat16),
        ),
        in_specs=[VMEM] * 3 + [SMEM],
        out_specs=(VMEM,) * 3,
        scratch_shapes=[pltpu.VMEM((K, K), jnp.float32)],
        compiler_params=pltpu.CompilerParams(vmem_limit_bytes=24 * 2**20),
        cost_estimate=pl.CostEstimate(
            flops=6 * 256 * 1024 * 512, bytes_accessed=5 * 2**20, transcendentals=0
        ),
        name="sent_product",
    )(in_vmem(high), in_vmem(low), first, core)


def kept_product_kernel(high_ref, low_ref, parts_ref, gram_ref, out_ref):
    out_ref[:, 32:, :] = gram_ref[...]
    share(high_ref, low_ref, parts_ref, out_ref)


def kept_product(high, low, parts, gram):
    return pl.pallas_call(
        kept_product_kernel,
        out_shape=jax.ShapeDtypeStruct((8, 40, 2 * K), jnp.float32),
        in_specs=[VMEM] * 4,
        out_specs=VMEM,
        compiler_params=pltpu.CompilerParams(vmem_limit_bytes=24 * 2**20),
        cost_estimate=pl.CostEstimate(
            flops=6 * 256 * 1024 * 512, bytes_accessed=5 * 2**20, transcendentals=0
        ),
        name="kept_product",
    )(in_vmem(high), in_vmem(low), parts, gram)


def stage_kernel(*refs):
    terms, out_ref, total_ref, sem = refs[:-3], refs[-3], refs[-2], refs[-1]
    total = terms[0][...]
    for term in terms[1:]:
        total = total + term[...]
    total_ref[...] = total
    drain([pltpu.make_async_copy(total_ref, out_ref, sem)])


def stage(*terms):
    shape = jax.ShapeDtypeStruct(terms[0].shape, jnp.float32)
    return pl.pallas_call(
        stage_kernel,
        out_shape=pltpu.HBM(shape.shape, jnp.float32),
        out_specs=pl.BlockSpec(memory_space=pltpu.HBM),
        scratch_shapes=[pltpu.VMEM(shape.shape, jnp.float32), pltpu.SemaphoreType.DMA],
        compiler_params=pltpu.CompilerParams(vmem_limit_bytes=16 * 2**20),
        name="stage",
    )(*terms)


SIN_TERMS = (
    3.1415926535362906,
    -5.167712764624546,
    2.550163318947043,
    -0.5992521978220368,
    0.08205040179571269,
    -0.007028386383306818,
)
COS_TERMS = (
    0.9999999997799041,
    -4.9348021370788295,
    4.058709159556314,
    -1.335212003049894,
    0.23493731381328964,
    -0.024396324346460163,
)


def polynomial(terms, x):
    value = terms[-1]
    for term in terms[-2::-1]:
        value = value * x + term
    return value


def spread_start_kernel(start_ref, copies_ref, total_ref, sems):
    total_ref[:, :K] = start_ref[0]
    total_ref[:, K:] = start_ref[1]
    drain(
        [
            pltpu.make_async_copy(total_ref, copies_ref.at[index], sems.at[index])
            for index in range(8)
        ]
    )


def spread_start(start):
    return pl.pallas_call(
        spread_start_kernel,
        out_shape=pltpu.HBM((8, 32, 2 * K), jnp.float32),
        in_specs=[VMEM],
        out_specs=HBM,
        scratch_shapes=[pltpu.VMEM((32, 2 * K), jnp.float32), pltpu.SemaphoreType.DMA((8,))],
        compiler_params=pltpu.CompilerParams(vmem_limit_bytes=8 * 2**20),
        name="spread_start",
    )(start)


def steering_kernel(grid_ref, mics_ref, *refs):
    index = (
        grid_ref[:, 0:1] * mics_ref[0:1, :] + grid_ref[:, 1:2] * mics_ref[1:2, :]
    )
    turns = (index - jnp.round(index * (1.0 / MOD)) * float(MOD)) * (1.0 / MOD)
    square = turns * turns
    half_sine = turns * polynomial(SIN_TERMS, square)
    half_cosine = polynomial(COS_TERMS, square)
    cosine = 1.0 - 2.0 * half_sine * half_sine
    sine = 2.0 * half_sine * half_cosine
    for value, high_ref, low_ref in ((cosine, refs[-4], refs[-3]), (sine, refs[-2], refs[-1])):
        high_ref[...], low_ref[...] = halves(value)


def steering(grid, mics, first, count, before=()):
    block = pl.BlockSpec((256, 1024), lambda i: ((i + first) // 2, (i + first) % 2))
    return pl.pallas_call(
        steering_kernel,
        grid=(count,),
        in_specs=[
            pl.BlockSpec((256, 2), lambda i: ((i + first) // 2, 0)),
            pl.BlockSpec((2, 1024), lambda i: (0, (i + first) % 2)),
        ]
        + [HBM] * len(before),
        out_specs=(block,) * 4,
        out_shape=(pltpu.HBM((1024, 2048), jnp.bfloat16),) * 4,
        input_output_aliases={2 + index: index for index in range(len(before))},
        compiler_params=pltpu.CompilerParams(vmem_limit_bytes=24 * 2**20),
        cost_estimate=pl.CostEstimate(
            flops=45 * 256 * 1024 * count, bytes_accessed=8 * 256 * 1024 * count, transcendentals=0
        ),
        name="steering",
    )(grid, mics, *before)


def second_gram_kernel(
    mine_ref, other_ref, inverse_ref, row_ref, copies_ref, gram_ref, slice_ref, sems
):
    own = pl.multiple_of(row_ref[0] * 16, 16)
    raw = jnp.concatenate(
        [
            ref[:, :32, lanes].reshape(256, K)
            for ref in (mine_ref, other_ref)
            for lanes in (slice(0, K), slice(K, 2 * K))
        ],
        axis=0,
    )
    second = dot_nt(raw, inverse_ref[...])
    gram_ref[...] = dot_tn(second, second)
    slice_ref[...] = gram_ref[pl.ds(own, 16), :]
    drain(
        [
            pltpu.make_async_copy(slice_ref, copies_ref.at[index], sems.at[index])
            for index in range(16)
        ]
    )


def second_gram_slice(mine, other, inverse, row):
    return pl.pallas_call(
        second_gram_kernel,
        out_shape=pltpu.HBM((16, 16, K), jnp.float32),
        in_specs=[VMEM, VMEM, VMEM, SMEM],
        out_specs=HBM,
        scratch_shapes=[
            pltpu.VMEM((K, K), jnp.float32),
            pltpu.VMEM((16, K), jnp.float32),
            pltpu.SemaphoreType.DMA((16,)),
        ],
        compiler_params=pltpu.CompilerParams(vmem_limit_bytes=24 * 2**20),
        cost_estimate=pl.CostEstimate(
            flops=4 * 1024 * K * K, bytes_accessed=2**21, transcendentals=0
        ),
        name="second_gram",
    )(mine, other, inverse, row)


def project_kernel(half_ref, *refs):
    raw_refs, beside_refs = refs[:2], refs[2:8]
    cos_high, cos_low, sin_high, sin_low = refs[8:12]
    out_ref, high_ref, low_ref, slots, sems = refs[12:]
    step = pl.program_id(0)

    @pl.when(step == 0)
    def _():
        lower = half_ref[0] == 0
        sources = []
        for ref in raw_refs:
            parts = [
                ref[:, :32, lane : lane + HALF].reshape(256, HALF) for lane in range(0, 2 * K, HALF)
            ]
            sources.append(
                (jnp.where(lower, parts[0], parts[1]), jnp.where(lower, parts[2], parts[3]))
            )
        for ref in beside_refs:
            sources.append((ref[:, :, :HALF].reshape(256, HALF), ref[:, :, HALF:].reshape(256, HALF)))
        for index, (real, imag) in enumerate(sources):
            start = index * 256
            for base, value in (
                (0, jnp.concatenate([real, imag], axis=1)),
                (2048, jnp.concatenate([-imag, real], axis=1)),
            ):
                high, low = halves(value)
                high_ref[base + start : base + start + 256, :] = high
                low_ref[base + start : base + start + 256, :] = low

    high = jnp.concatenate([cos_high[...], sin_high[...]], axis=1)
    low = jnp.concatenate([cos_low[...], sin_low[...]], axis=1)
    product = jnp.dot(high, high_ref[...], preferred_element_type=jnp.float32)
    product += jnp.dot(high, low_ref[...], preferred_element_type=jnp.float32)
    product += jnp.dot(low, high_ref[...], preferred_element_type=jnp.float32)
    slots[pl.ds(2 * step, 2)] = product.reshape(2, 128, 256)

    def copy(index):
        both = pl.ds(2 * index, 2)
        return pltpu.make_async_copy(slots.at[both], out_ref.at[both], sems.at[index])

    copy(step).start()

    @pl.when(step == 3)
    def _():
        for index in range(4):
            copy(index).wait()


def project(half, raw, beside, steered):
    block = pl.BlockSpec((256, 2048), lambda i: (i, 0))
    return pl.pallas_call(
        project_kernel,
        grid=(4,),
        in_specs=[SMEM]
        + [pl.BlockSpec((8, 40, 512), lambda i: (0, 0, 0))] * 2
        + [pl.BlockSpec((8, 32, 256), lambda i: (0, 0, 0))] * 6
        + [block] * 4,
        out_specs=HBM,
        out_shape=pltpu.HBM((8, 128, 256), jnp.float32),
        scratch_shapes=[
            pltpu.VMEM((4096, 256), jnp.bfloat16),
            pltpu.VMEM((4096, 256), jnp.bfloat16),
            pltpu.VMEM((8, 128, 256), jnp.float32),
            pltpu.SemaphoreType.DMA((4,)),
        ],
        compiler_params=pltpu.CompilerParams(vmem_limit_bytes=40 * 2**20),
        cost_estimate=pl.CostEstimate(
            flops=3 * 2 * 1024 * 4096 * 256, bytes_accessed=18 * 2**20, transcendentals=0
        ),
        name="project",
    )(half, *raw, *beside, *[pltpu.with_memory_space_constraint(x, pltpu.HBM) for x in steered])


def half_of_vectors(pieces, half):
    lower = jnp.concatenate([pieces[..., :HALF], pieces[..., K : K + HALF]], axis=-1)
    upper = jnp.concatenate([pieces[..., HALF:K], pieces[..., K + HALF :]], axis=-1)
    return jnp.where(half == 0, lower, upper)


def body(csm_real, csm_imag, start_block, mic_coords, grid_coords, bin_index):
    row = lax.axis_index("row")
    core = row % 2
    own_core = core.reshape(1)
    col = lax.axis_index("col")
    half = col % 2
    points = grid_coords.reshape(2, 4, 2, 256)
    points = jnp.where(col // 2 % 2 == 0, points[:, :, 0], points[:, :, 1]).reshape(2, 1024)
    reduced = ((bin_index * points) % MOD).astype(jnp.float32).T

    mine = exchange(spread_start(start_block), "row", Z_GROUPS)
    *tiles, mic_coords, reduced = lax.optimization_barrier(
        (*prepare(csm_real, csm_imag, own_core), mic_coords, reduced)
    )
    places = [mic_coords] + [lax.ppermute(mic_coords, "col", ALONG_X[flip]) for flip in (1, 2, 3)]
    mine, *places = lax.optimization_barrier((mine, *places, *tiles))
    places, tiles = places[:4], places[4:]
    other = lax.ppermute(mine, "row", CORE_SWAP)
    first_partial = first_product(*tiles[:2], mine, other, own_core)

    places = jnp.stack(places, axis=1).reshape(2, 4, 8, 2, 32)
    even, odd = places[:, :, :, 0], places[:, :, :, 1]
    mics = jnp.stack([jnp.where(core == 0, even, odd), jnp.where(core == 0, odd, even)], axis=2)
    mics = mics.reshape(2, 2048).astype(jnp.float32)
    steered = steering(reduced, mics, 0, 3)
    first_pieces = exchange(first_partial, "col")
    first_pieces, steered = lax.optimization_barrier((first_pieces, steered))

    steered = steering(reduced, mics, 3, 2, steered)
    first = exchange(spread(first_pieces, 16)[1], "col")
    first, steered = lax.optimization_barrier((first, steered))
    sent, gram_rows, parts = sent_product(*tiles[4:], first, own_core)
    got = lax.ppermute(sent, "row", CORE_SWAP)
    kept = kept_product(*tiles[2:4], parts, gram_rows)
    pair = stage(kept, got)

    steered = steering(reduced, mics, 5, 2, steered)
    pieces = exchange(pair, "row", Z_GROUPS)
    pieces, steered = lax.optimization_barrier((pieces, steered))
    own, spread_out = spread(pieces, 8)

    steered = steering(reduced, mics, 7, 1, steered)
    mine = exchange(spread_out, "row", Z_GROUPS)
    mine, steered = lax.optimization_barrier((mine, steered))
    other = lax.ppermute(mine, "row", CORE_SWAP)
    taken = half_of_vectors(mine[:, :32], half)
    given = half_of_vectors(mine[:, :32], 1 - half)
    near = [
        lax.ppermute(taken if flip == 2 else given, "col", ALONG_X[flip]) for flip in (1, 2, 3)
    ]
    first_inverse = first_factor(mine, other, own_core)
    gram_copies = second_gram_slice(mine, other, first_inverse, row.reshape(1))
    near, gram_copies = lax.optimization_barrier((near, gram_copies))
    far = [lax.ppermute(block, "row", CORE_SWAP) for block in near]
    beside = [block for both in zip(near, far) for block in both]
    gram_pieces = exchange(gram_copies, "col")
    part = project(half.reshape(1), (mine, other), beside, steered)
    part, gram_pieces = lax.optimization_barrier((part, gram_pieces))
    pieces = exchange(part, "col", POINT_GROUPS)
    second_gram = lax.all_gather(jnp.sum(gram_pieces, axis=0), "row", axis=0, tiled=True)
    basis, both_inverse, weights = second_factor(second_gram, first_inverse, own)
    return (basis, finish(pieces, both_inverse, weights).reshape(128))


def solution(mesh):
    in_specs = (
        P("row", "col"),
        P("row", "col"),
        P(None, ("col", "row"), None),
        P(None, "col"),
        P(None, "row"),
        P(),
    )
    out_specs = (P(None, ("col", "row"), None), P(("row", "col")))
    return jax.shard_map(body, mesh=mesh, in_specs=in_specs, out_specs=out_specs, check_vma=False)
```

```python
import jax
import jax.numpy as jnp
from jax import lax
from jax.experimental import pallas as pl
from jax.experimental.pallas import tpu as pltpu
from jax.sharding import PartitionSpec as P

NU = 4
K = 256
MOD = 4093
HIGH = lax.Precision.HIGHEST

Z_GROUPS = [list(range(core, 16, 2)) for core in range(2)]
CORE_SWAP = [(index, index ^ 1) for index in range(16)]

ALONG_X = [[(index, index ^ flip) for index in range(16)] for flip in range(4)]
POINT_GROUPS = [[index for index in range(16) if index // 2 % 2 == part] for part in range(2)]
HALF = K // 2
SMEM = pl.BlockSpec(memory_space=pltpu.SMEM)
HBM = pl.BlockSpec(memory_space=pltpu.HBM)
VMEM = pl.BlockSpec(memory_space=pltpu.VMEM)

PANEL = 64
MICRO = 16


def dot(a, b):
    return jnp.dot(a, b, precision=HIGH, preferred_element_type=jnp.float32)


def dot_tn(a, b):
    return lax.dot_general(
        a, b, (((0,), (0,)), ((), ())), precision=HIGH, preferred_element_type=jnp.float32
    )


def dot_nt(a, b):
    return lax.dot_general(
        a, b, (((1,), (1,)), ((), ())), precision=HIGH, preferred_element_type=jnp.float32
    )


def eliminate(work_ref, upper_ref, inverse_ref):
    rows = lax.broadcasted_iota(jnp.int32, (K, K), 0)
    cols = lax.broadcasted_iota(jnp.int32, (K, K), 1)
    work_ref[:, K:] = (rows == cols).astype(jnp.float32)
    panel_row = lax.broadcasted_iota(jnp.int32, (PANEL, 128), 0)
    for start in range(0, K, PANEL):
        low = (start // 128) * 128
        high = K + ((start + PANEL + 127) // 128) * 128
        width = high - low
        offset = start - low
        panel = work_ref[start : start + PANEL, low:high]
        for first in range(0, PANEL, MICRO):
            columns = [
                jnp.broadcast_to(
                    panel[:, offset + first + k : offset + first + k + 1], (PANEL, 128)
                )
                for k in range(MICRO)
            ]
            for k in range(MICRO):
                j = first + k
                scale = jnp.where(panel_row > j, columns[k] * (1.0 / columns[k][j : j + 1, :]), 0.0)
                for later in range(k + 1, MICRO):
                    columns[later] = columns[later] - scale * columns[later][j : j + 1, :]
                panel = (
                    panel
                    - jnp.concatenate([scale] * (width // 128), axis=1) * panel[j : j + 1, :]
                )
        square_row = lax.broadcasted_iota(jnp.int32, (PANEL, PANEL), 0)
        square_col = lax.broadcasted_iota(jnp.int32, (PANEL, PANEL), 1)
        pivots = jnp.sum(
            jnp.where(square_row == square_col, panel[:, offset : offset + PANEL], 0.0),
            axis=1,
            keepdims=True,
        )
        panel = panel * (1.0 / jnp.sqrt(pivots))
        if upper_ref is not None:
            panel_cols = lax.broadcasted_iota(jnp.int32, (PANEL, K - low), 1) + low
            panel_rows = lax.broadcasted_iota(jnp.int32, (PANEL, K - low), 0) + start
            upper_ref[start : start + PANEL, :] = jnp.zeros((PANEL, K), jnp.float32)
            upper_ref[start : start + PANEL, low:K] = jnp.where(
                panel_cols >= panel_rows, panel[:, : K - low], 0.0
            )
        inverse_ref[start : start + PANEL, :] = jnp.zeros((PANEL, K), jnp.float32)
        inverse_ref[start : start + PANEL, : high - K] = panel[:, K - low :]
        after = start + PANEL
        if after < K:
            update = dot_tn(panel[:, after - low : K - low], panel)
            work_ref[after:, low:high] = work_ref[after:, low:high] - update


def first_factor_kernel(mine_ref, other_ref, core_ref, inverse_ref, work_ref):
    own = core_ref[0]
    for z in range(8):
        for core in range(2):
            part = jnp.where(own == core, mine_ref[z, 32:, :], other_ref[z, 32:, :])
            start = (2 * z + core) * 16
            work_ref[start : start + 8, :K] = part[:, :K]
            work_ref[start + 8 : start + 16, :K] = part[:, K:]
    eliminate(work_ref, None, inverse_ref)


def first_factor(mine, other, core):
    return pl.pallas_call(
        first_factor_kernel,
        out_shape=jax.ShapeDtypeStruct((K, K), jnp.float32),
        in_specs=[VMEM, VMEM, SMEM],
        out_specs=VMEM,
        scratch_shapes=[pltpu.VMEM((K, 2 * K), jnp.float32)],
        compiler_params=pltpu.CompilerParams(vmem_limit_bytes=16 * 2**20),
        cost_estimate=pl.CostEstimate(
            flops=4 * K**3, bytes_accessed=12 * K * K, transcendentals=K
        ),
        name="first_factor",
    )(mine, other, core)


def second_factor_kernel(
    gram_ref, first_ref, rows_ref, basis_ref, both_ref, weights_ref, upper_ref, inverse_ref, work_ref
):
    work_ref[:, :K] = gram_ref[...]
    eliminate(work_ref, upper_ref, inverse_ref)
    rows = lax.broadcasted_iota(jnp.int32, (K, K), 0)
    cols = lax.broadcasted_iota(jnp.int32, (K, K), 1)
    diagonal = jnp.sum(jnp.where(rows == cols, upper_ref[...], 0.0), axis=0, keepdims=True)
    weights_ref[...] = jnp.sqrt(jnp.sqrt(diagonal))
    both_ref[...] = dot(inverse_ref[...], first_ref[...])
    raw = jnp.concatenate([rows_ref[:32, :K], rows_ref[:32, K:]], axis=0)
    basis = dot_nt(dot_nt(raw, first_ref[...]), inverse_ref[...])
    basis_ref[0] = basis[:32]
    basis_ref[1] = basis[32:]


def second_factor(gram, first_inverse, rows):
    return pl.pallas_call(
        second_factor_kernel,
        out_shape=(
            jax.ShapeDtypeStruct((2, 32, K), jnp.float32),
            jax.ShapeDtypeStruct((K, K), jnp.float32),
            jax.ShapeDtypeStruct((1, K), jnp.float32),
        ),
        scratch_shapes=[
            pltpu.VMEM((K, K), jnp.float32),
            pltpu.VMEM((K, K), jnp.float32),
            pltpu.VMEM((K, 2 * K), jnp.float32),
        ],
        compiler_params=pltpu.CompilerParams(vmem_limit_bytes=16 * 2**20),
        cost_estimate=pl.CostEstimate(
            flops=6 * K**3, bytes_accessed=16 * K * K, transcendentals=K
        ),
        name="second_factor",
    )(gram, first_inverse, rows)


def finish_kernel(pieces_ref, both_ref, weights_ref, beam_ref):
    lower = pieces_ref[0]
    upper = pieces_ref[1]
    for index in range(2, 8, 2):
        lower = lower + pieces_ref[index]
        upper = upper + pieces_ref[index + 1]
    real_part = jnp.concatenate([lower[:, :HALF], upper[:, :HALF]], axis=1)
    imag_part = jnp.concatenate([lower[:, HALF:], upper[:, HALF:]], axis=1)
    projected = dot_nt(jnp.concatenate([real_part, imag_part], axis=0), both_ref[...])
    square = projected * projected
    weights = weights_ref[...]
    power = dot_nt(weights, square[:128] + square[128:]) / jnp.sum(weights)
    power = power * power
    beam_ref[...] = power * power


def finish(pieces, both, weights):
    return pl.pallas_call(
        finish_kernel,
        out_shape=jax.ShapeDtypeStruct((1, 128), jnp.float32),
        compiler_params=pltpu.CompilerParams(vmem_limit_bytes=16 * 2**20),
        name="finish",
    )(pieces, both, weights)


def turned(block):
    return jnp.concatenate([-block[:, K:], block[:, :K]], axis=1)


def exchange(pieces, axis, groups=None):
    return lax.all_to_all(pieces, axis, 0, 0, tiled=True, axis_index_groups=groups)


def drain(copies):
    for copy in copies:
        copy.start()
    for copy in copies:
        copy.wait()


def spread_kernel(pieces_ref, total_ref, copies_ref, sems):
    total_ref[...] = jnp.sum(pieces_ref[...], axis=0)
    drain(
        [
            pltpu.make_async_copy(total_ref, copies_ref.at[index], sems.at[index])
            for index in range(copies_ref.shape[0])
        ]
    )


def spread(pieces, count):
    piece = pieces.shape[1:]
    return pl.pallas_call(
        spread_kernel,
        out_shape=(
            jax.ShapeDtypeStruct(piece, jnp.float32),
            pltpu.HBM((count,) + piece, jnp.float32),
        ),
        out_specs=(
            pl.BlockSpec(memory_space=pltpu.VMEM),
            pl.BlockSpec(memory_space=pltpu.HBM),
        ),
        scratch_shapes=[pltpu.SemaphoreType.DMA((count,))],
        compiler_params=pltpu.CompilerParams(vmem_limit_bytes=16 * 2**20),
        name="spread",
    )(pieces)


def halves(value):
    high = value.astype(jnp.bfloat16)
    return high, (value - high.astype(jnp.float32)).astype(jnp.bfloat16)


def split_dot(high, low, parts):
    total = jnp.dot(low, parts[0], preferred_element_type=jnp.float32)
    total += jnp.dot(high, parts[1], preferred_element_type=jnp.float32)
    return total + jnp.dot(high, parts[0], preferred_element_type=jnp.float32)


def in_hbm(value):
    return pltpu.with_memory_space_constraint(value, pltpu.HBM)


def fetch(high_ref, low_ref, tiles_ref, sems):
    copies = [
        pltpu.make_async_copy(ref, tiles_ref.at[index], sems.at[index])
        for index, ref in enumerate((high_ref, low_ref))
    ]
    for copy in copies:
        copy.start()
    return copies


def prepare_kernel(
    real_ref, imag_ref, core_ref, tile_high, tile_low, kept_high, kept_low, sent_high, sent_low
):
    first_core = core_ref[0] == 0
    for base, ref in ((0, real_ref), (512, imag_ref)):
        lanes = slice(base, base + 512)
        value = ref[...]
        tile_high[:, lanes], tile_low[:, lanes] = halves(value)
        rows = value.T.reshape(8, 2, 32, 512)
        kept = jnp.where(first_core, rows[:, 0], rows[:, 1]).reshape(256, 512)
        sent = jnp.where(first_core, rows[:, 1], rows[:, 0]).reshape(256, 512)
        kept_high[:, lanes], kept_low[:, lanes] = halves(kept)
        sent_high[:, lanes], sent_low[:, lanes] = halves(sent)


def prepare(real, imag, core):
    shapes = [(512, 1024)] * 2 + [(256, 1024)] * 4
    return pl.pallas_call(
        prepare_kernel,
        out_shape=tuple(pltpu.HBM(shape, jnp.bfloat16) for shape in shapes),
        in_specs=[VMEM, VMEM, SMEM],
        out_specs=(VMEM,) * 6,
        compiler_params=pltpu.CompilerParams(vmem_limit_bytes=24 * 2**20),
        cost_estimate=pl.CostEstimate(
            flops=20 * 512 * 1024, bytes_accessed=8 * 2**20, transcendentals=0
        ),
        name="prepare",
    )(real, imag, core)


def first_product_kernel(
    high_ref, low_ref, mine_ref, other_ref, core_ref,
    out_ref, start_ref, parts_ref, rows_ref, tiles_ref, sems, tile_sems,
):
    fetched = fetch(high_ref, low_ref, tiles_ref, tile_sems)
    core = core_ref[0]
    for z in range(8):
        start_ref[2 * z + core] = mine_ref[z]
        start_ref[2 * z + 1 - core] = other_ref[z]
    start = start_ref[...].reshape(512, 2 * K)
    for base, value in ((0, start), (512, turned(start))):
        for index, part in enumerate(halves(value)):
            parts_ref[index, base : base + 512, :] = part
    parts = [parts_ref[index] for index in range(2)]
    for copy in fetched:
        copy.wait()
    copies = []
    for block in range(4):
        at = slice(block * 128, block * 128 + 128)
        product = split_dot(tiles_ref[0, at, :], tiles_ref[1, at, :], parts)
        four = pl.ds(block * 4, 4)
        rows_ref[four] = product.reshape(4, 32, 2 * K)
        copies.append(
            pltpu.make_async_copy(rows_ref.at[four], out_ref.at[four], sems.at[block])
        )
        copies[-1].start()
    for copy in copies:
        copy.wait()


def first_product(high, low, mine, other, core):
    return pl.pallas_call(
        first_product_kernel,
        out_shape=pltpu.HBM((16, 32, 2 * K), jnp.float32),
        in_specs=[HBM, HBM, VMEM, VMEM, SMEM],
        out_specs=HBM,
        scratch_shapes=[
            pltpu.VMEM((16, 32, 2 * K), jnp.float32),
            pltpu.VMEM((2, 1024, 2 * K), jnp.bfloat16),
            pltpu.VMEM((16, 32, 2 * K), jnp.float32),
            pltpu.VMEM((2, 512, 1024), jnp.bfloat16),
            pltpu.SemaphoreType.DMA((4,)),
            pltpu.SemaphoreType.DMA((2,)),
        ],
        compiler_params=pltpu.CompilerParams(vmem_limit_bytes=24 * 2**20),
        cost_estimate=pl.CostEstimate(
            flops=6 * 512 * 1024 * 512, bytes_accessed=5 * 2**20, transcendentals=0
        ),
        name="first_product",
    )(in_hbm(high), in_hbm(low), mine, other, core)


def sent_product_kernel(
    high_ref, low_ref, first_ref, core_ref,
    out_ref, kept_ref, parts_ref, gram_ref, tiles_ref, sems,
):
    fetched = fetch(high_ref, low_ref, tiles_ref, sems)
    first = first_ref[...].reshape(512, 2 * K)
    for base, value in ((0, first), (512, -turned(first))):
        for index, part in enumerate(halves(value)):
            parts_ref[index, base : base + 512, :] = part
    rows = jnp.concatenate([first[:, :K], first[:, K:]], axis=0)
    gram_ref[...] = dot_tn(rows, rows)
    core = core_ref[0]
    for z in range(8):
        for which, target, at in ((core, kept_ref, 0), (1 - core, out_ref, 32)):
            start = pl.multiple_of(z * 32 + which * 16, 16)
            target[z, at : at + 8, :K] = gram_ref[pl.ds(start, 8), :]
            target[z, at : at + 8, K:] = gram_ref[pl.ds(start + 8, 8), :]
    for copy in fetched:
        copy.wait()
    share(tiles_ref.at[0], tiles_ref.at[1], parts_ref, out_ref)


def share(high_ref, low_ref, parts_ref, out_ref):
    parts = [parts_ref[index] for index in range(2)]
    for block in range(2):
        at = slice(block * 128, block * 128 + 128)
        product = split_dot(high_ref[at, :], low_ref[at, :], parts)
        out_ref[block * 4 : block * 4 + 4, :32, :] = product.reshape(4, 32, 2 * K)


def sent_product(high, low, first, core):
    return pl.pallas_call(
        sent_product_kernel,
        out_shape=(
            jax.ShapeDtypeStruct((8, 40, 2 * K), jnp.float32),
            jax.ShapeDtypeStruct((8, 8, 2 * K), jnp.float32),
            jax.ShapeDtypeStruct((2, 1024, 2 * K), jnp.bfloat16),
        ),
        in_specs=[HBM, HBM, VMEM, SMEM],
        out_specs=(VMEM,) * 3,
        scratch_shapes=[
            pltpu.VMEM((K, K), jnp.float32),
            pltpu.VMEM((2, 256, 1024), jnp.bfloat16),
            pltpu.SemaphoreType.DMA((2,)),
        ],
        compiler_params=pltpu.CompilerParams(vmem_limit_bytes=24 * 2**20),
        cost_estimate=pl.CostEstimate(
            flops=6 * 256 * 1024 * 512, bytes_accessed=5 * 2**20, transcendentals=0
        ),
        name="sent_product",
    )(in_hbm(high), in_hbm(low), first, core)


def kept_product_kernel(high_ref, low_ref, parts_ref, gram_ref, out_ref):
    out_ref[:, 32:, :] = gram_ref[...]
    share(high_ref, low_ref, parts_ref, out_ref)


def kept_product(high, low, parts, gram):
    return pl.pallas_call(
        kept_product_kernel,
        out_shape=jax.ShapeDtypeStruct((8, 40, 2 * K), jnp.float32),
        in_specs=[VMEM] * 4,
        out_specs=VMEM,
        compiler_params=pltpu.CompilerParams(vmem_limit_bytes=24 * 2**20),
        cost_estimate=pl.CostEstimate(
            flops=6 * 256 * 1024 * 512, bytes_accessed=5 * 2**20, transcendentals=0
        ),
        name="kept_product",
    )(high, low, parts, gram)


def stage_kernel(*refs):
    terms, out_ref, total_ref, sem = refs[:-3], refs[-3], refs[-2], refs[-1]
    total = terms[0][...]
    for term in terms[1:]:
        total = total + term[...]
    total_ref[...] = total
    drain([pltpu.make_async_copy(total_ref, out_ref, sem)])


def stage(*terms):
    shape = jax.ShapeDtypeStruct(terms[0].shape, jnp.float32)
    return pl.pallas_call(
        stage_kernel,
        out_shape=pltpu.HBM(shape.shape, jnp.float32),
        out_specs=pl.BlockSpec(memory_space=pltpu.HBM),
        scratch_shapes=[pltpu.VMEM(shape.shape, jnp.float32), pltpu.SemaphoreType.DMA],
        compiler_params=pltpu.CompilerParams(vmem_limit_bytes=16 * 2**20),
        name="stage",
    )(*terms)


SIN_TERMS = (
    3.1415926535362906,
    -5.167712764624546,
    2.550163318947043,
    -0.5992521978220368,
    0.08205040179571269,
    -0.007028386383306818,
)
COS_TERMS = (
    0.9999999997799041,
    -4.9348021370788295,
    4.058709159556314,
    -1.335212003049894,
    0.23493731381328964,
    -0.024396324346460163,
)


def polynomial(terms, x):
    value = terms[-1]
    for term in terms[-2::-1]:
        value = value * x + term
    return value


def spread_start_kernel(start_ref, copies_ref, total_ref, sems):
    total_ref[:, :K] = start_ref[0]
    total_ref[:, K:] = start_ref[1]
    drain(
        [
            pltpu.make_async_copy(total_ref, copies_ref.at[index], sems.at[index])
            for index in range(8)
        ]
    )


def spread_start(start):
    return pl.pallas_call(
        spread_start_kernel,
        out_shape=pltpu.HBM((8, 32, 2 * K), jnp.float32),
        in_specs=[VMEM],
        out_specs=HBM,
        scratch_shapes=[pltpu.VMEM((32, 2 * K), jnp.float32), pltpu.SemaphoreType.DMA((8,))],
        compiler_params=pltpu.CompilerParams(vmem_limit_bytes=8 * 2**20),
        name="spread_start",
    )(start)


def steering_kernel(grid_ref, mics_ref, *refs):
    index = (
        grid_ref[:, 0:1] * mics_ref[0:1, :] + grid_ref[:, 1:2] * mics_ref[1:2, :]
    )
    turns = (index - jnp.round(index * (1.0 / MOD)) * float(MOD)) * (1.0 / MOD)
    square = turns * turns
    half_sine = turns * polynomial(SIN_TERMS, square)
    half_cosine = polynomial(COS_TERMS, square)
    cosine = 1.0 - 2.0 * half_sine * half_sine
    sine = 2.0 * half_sine * half_cosine
    for value, high_ref, low_ref in ((cosine, refs[-4], refs[-3]), (sine, refs[-2], refs[-1])):
        high_ref[...], low_ref[...] = halves(value)


def steering(grid, mics, first, count, before=()):
    block = pl.BlockSpec((256, 1024), lambda i: ((i + first) // 2, (i + first) % 2))
    return pl.pallas_call(
        steering_kernel,
        grid=(count,),
        in_specs=[
            pl.BlockSpec((256, 2), lambda i: ((i + first) // 2, 0)),
            pl.BlockSpec((2, 1024), lambda i: (0, (i + first) % 2)),
        ]
        + [HBM] * len(before),
        out_specs=(block,) * 4,
        out_shape=(pltpu.HBM((1024, 2048), jnp.bfloat16),) * 4,
        input_output_aliases={2 + index: index for index in range(len(before))},
        compiler_params=pltpu.CompilerParams(vmem_limit_bytes=24 * 2**20),
        cost_estimate=pl.CostEstimate(
            flops=45 * 256 * 1024 * count, bytes_accessed=8 * 256 * 1024 * count, transcendentals=0
        ),
        name="steering",
    )(grid, mics, *before)


def second_gram_kernel(mine_ref, other_ref, inverse_ref, row_ref, copies_ref, slice_ref, sems):
    own = pl.multiple_of(row_ref[0] * 16, 16)
    raw = jnp.concatenate(
        [
            ref[:, :32, lanes].reshape(256, K)
            for ref in (mine_ref, other_ref)
            for lanes in (slice(0, K), slice(K, 2 * K))
        ],
        axis=0,
    )
    second = dot_nt(raw, inverse_ref[...])
    turned_slice = dot_nt(inverse_ref[pl.ds(own, 16), :], raw)
    slice_ref[...] = dot(turned_slice, second)
    drain(
        [
            pltpu.make_async_copy(slice_ref, copies_ref.at[index], sems.at[index])
            for index in range(16)
        ]
    )


def second_gram_slice(mine, other, inverse, row):
    return pl.pallas_call(
        second_gram_kernel,
        out_shape=pltpu.HBM((16, 16, K), jnp.float32),
        in_specs=[VMEM, VMEM, VMEM, SMEM],
        out_specs=HBM,
        scratch_shapes=[pltpu.VMEM((16, K), jnp.float32), pltpu.SemaphoreType.DMA((16,))],
        compiler_params=pltpu.CompilerParams(vmem_limit_bytes=24 * 2**20),
        cost_estimate=pl.CostEstimate(
            flops=2 * 1024 * K * (K + 32), bytes_accessed=2**21, transcendentals=0
        ),
        name="second_gram",
    )(mine, other, inverse, row)


def project_kernel(half_ref, *refs):
    raw_refs, beside_refs = refs[:2], refs[2:8]
    cos_high, cos_low, sin_high, sin_low = refs[8:12]
    out_ref, high_ref, low_ref, slots, sems = refs[12:]
    step = pl.program_id(0)

    @pl.when(step == 0)
    def _():
        lower = half_ref[0] == 0
        sources = []
        for ref in raw_refs:
            parts = [
                ref[:, :32, lane : lane + HALF].reshape(256, HALF) for lane in range(0, 2 * K, HALF)
            ]
            sources.append(
                (jnp.where(lower, parts[0], parts[1]), jnp.where(lower, parts[2], parts[3]))
            )
        for ref in beside_refs:
            sources.append((ref[:, :, :HALF].reshape(256, HALF), ref[:, :, HALF:].reshape(256, HALF)))
        for index, (real, imag) in enumerate(sources):
            start = index * 256
            for base, value in (
                (0, jnp.concatenate([real, imag], axis=1)),
                (2048, jnp.concatenate([-imag, real], axis=1)),
            ):
                high, low = halves(value)
                high_ref[base + start : base + start + 256, :] = high
                low_ref[base + start : base + start + 256, :] = low

    high = jnp.concatenate([cos_high[...], sin_high[...]], axis=1)
    low = jnp.concatenate([cos_low[...], sin_low[...]], axis=1)
    product = jnp.dot(high, high_ref[...], preferred_element_type=jnp.float32)
    product += jnp.dot(high, low_ref[...], preferred_element_type=jnp.float32)
    product += jnp.dot(low, high_ref[...], preferred_element_type=jnp.float32)
    slots[pl.ds(2 * step, 2)] = product.reshape(2, 128, 256)

    def copy(index):
        both = pl.ds(2 * index, 2)
        return pltpu.make_async_copy(slots.at[both], out_ref.at[both], sems.at[index])

    copy(step).start()

    @pl.when(step == 3)
    def _():
        for index in range(4):
            copy(index).wait()


def project(half, raw, beside, steered):
    block = pl.BlockSpec((256, 2048), lambda i: (i, 0))
    return pl.pallas_call(
        project_kernel,
        grid=(4,),
        in_specs=[SMEM]
        + [pl.BlockSpec((8, 40, 512), lambda i: (0, 0, 0))] * 2
        + [pl.BlockSpec((8, 32, 256), lambda i: (0, 0, 0))] * 6
        + [block] * 4,
        out_specs=HBM,
        out_shape=pltpu.HBM((8, 128, 256), jnp.float32),
        scratch_shapes=[
            pltpu.VMEM((4096, 256), jnp.bfloat16),
            pltpu.VMEM((4096, 256), jnp.bfloat16),
            pltpu.VMEM((8, 128, 256), jnp.float32),
            pltpu.SemaphoreType.DMA((4,)),
        ],
        compiler_params=pltpu.CompilerParams(vmem_limit_bytes=40 * 2**20),
        cost_estimate=pl.CostEstimate(
            flops=3 * 2 * 1024 * 4096 * 256, bytes_accessed=18 * 2**20, transcendentals=0
        ),
        name="project",
    )(half, *raw, *beside, *[in_hbm(value) for value in steered])


def half_of_vectors(pieces, half):
    lower = jnp.concatenate([pieces[..., :HALF], pieces[..., K : K + HALF]], axis=-1)
    upper = jnp.concatenate([pieces[..., HALF:K], pieces[..., K + HALF :]], axis=-1)
    return jnp.where(half == 0, lower, upper)


def body(csm_real, csm_imag, start_block, mic_coords, grid_coords, bin_index):
    row = lax.axis_index("row")
    core = row % 2
    own_core = core.reshape(1)
    col = lax.axis_index("col")
    half = col % 2
    points = grid_coords.reshape(2, 4, 2, 256)
    points = jnp.where(col // 2 % 2 == 0, points[:, :, 0], points[:, :, 1]).reshape(2, 1024)
    reduced = ((bin_index * points) % MOD).astype(jnp.float32).T

    mine = exchange(spread_start(start_block), "row", Z_GROUPS)
    *tiles, mic_coords, reduced = lax.optimization_barrier(
        (*prepare(csm_real, csm_imag, own_core), mic_coords, reduced)
    )
    places = [mic_coords] + [lax.ppermute(mic_coords, "col", ALONG_X[flip]) for flip in (1, 2, 3)]
    mine, *places = lax.optimization_barrier((mine, *places, *tiles))
    places, tiles = places[:4], places[4:]
    other = lax.ppermute(mine, "row", CORE_SWAP)
    first_partial = first_product(*tiles[:2], mine, other, own_core)

    places = jnp.stack(places, axis=1).reshape(2, 4, 8, 2, 32)
    even, odd = places[:, :, :, 0], places[:, :, :, 1]
    mics = jnp.stack([jnp.where(core == 0, even, odd), jnp.where(core == 0, odd, even)], axis=2)
    mics = mics.reshape(2, 2048).astype(jnp.float32)
    steered = steering(reduced, mics, 0, 3)
    first_pieces = exchange(first_partial, "col")
    first_pieces, steered = lax.optimization_barrier((first_pieces, steered))

    steered = steering(reduced, mics, 3, 2, steered)
    first = exchange(spread(first_pieces, 16)[1], "col")
    first, steered = lax.optimization_barrier((first, steered))
    sent, gram_rows, parts = sent_product(*tiles[4:], first, own_core)
    got = lax.ppermute(sent, "row", CORE_SWAP)
    kept = kept_product(*tiles[2:4], parts, gram_rows)
    pair = stage(kept, got)

    steered = steering(reduced, mics, 5, 2, steered)
    pieces = exchange(pair, "row", Z_GROUPS)
    pieces, steered = lax.optimization_barrier((pieces, steered))
    own, spread_out = spread(pieces, 8)

    steered = steering(reduced, mics, 7, 1, steered)
    mine = exchange(spread_out, "row", Z_GROUPS)
    mine, steered = lax.optimization_barrier((mine, steered))
    other = lax.ppermute(mine, "row", CORE_SWAP)
    taken = half_of_vectors(mine[:, :32], half)
    given = half_of_vectors(mine[:, :32], 1 - half)
    near = [
        lax.ppermute(taken if flip == 2 else given, "col", ALONG_X[flip]) for flip in (1, 2, 3)
    ]
    first_inverse = first_factor(mine, other, own_core)
    gram_copies = second_gram_slice(mine, other, first_inverse, row.reshape(1))
    near, gram_copies = lax.optimization_barrier((near, gram_copies))
    far = [lax.ppermute(block, "row", CORE_SWAP) for block in near]
    beside = [block for both in zip(near, far) for block in both]
    gram_pieces = exchange(gram_copies, "col")
    part = project(half.reshape(1), (mine, other), beside, steered)
    part, gram_pieces = lax.optimization_barrier((part, gram_pieces))
    pieces = exchange(part, "col", POINT_GROUPS)
    second_gram = lax.all_gather(jnp.sum(gram_pieces, axis=0), "row", axis=0, tiled=True)
    basis, both_inverse, weights = second_factor(second_gram, first_inverse, own)
    return (basis, finish(pieces, both_inverse, weights).reshape(128))


def solution(mesh):
    in_specs = (
        P("row", "col"),
        P("row", "col"),
        P(None, ("col", "row"), None),
        P(None, "col"),
        P(None, "row"),
        P(),
    )
    out_specs = (P(None, ("col", "row"), None), P(("row", "col")))
    return jax.shard_map(body, mesh=mesh, in_specs=in_specs, out_specs=out_specs, check_vma=False)
```

```python
import jax
import jax.numpy as jnp
from jax import lax
from jax.experimental import pallas as pl
from jax.experimental.pallas import tpu as pltpu
from jax.sharding import PartitionSpec as P

NU = 4
K = 256
MOD = 4093
HIGH = lax.Precision.HIGHEST

Z_GROUPS = [list(range(core, 16, 2)) for core in range(2)]
CORE_SWAP = [(index, index ^ 1) for index in range(16)]

ALONG_X = [[(index, index ^ flip) for index in range(16)] for flip in range(4)]
POINT_GROUPS = [[index for index in range(16) if index // 2 % 2 == part] for part in range(2)]
HALF = K // 2
SMEM = pl.BlockSpec(memory_space=pltpu.SMEM)
HBM = pl.BlockSpec(memory_space=pltpu.HBM)
VMEM = pl.BlockSpec(memory_space=pltpu.VMEM)

PANEL = 64
MICRO = 16


def dot(a, b):
    return jnp.dot(a, b, precision=HIGH, preferred_element_type=jnp.float32)


def dot_tn(a, b):
    return lax.dot_general(
        a, b, (((0,), (0,)), ((), ())), precision=HIGH, preferred_element_type=jnp.float32
    )


def dot_nt(a, b):
    return lax.dot_general(
        a, b, (((1,), (1,)), ((), ())), precision=HIGH, preferred_element_type=jnp.float32
    )


def eliminate(work_ref, inverse_ref, squares_ref):
    rows = lax.broadcasted_iota(jnp.int32, (K, K), 0)
    cols = lax.broadcasted_iota(jnp.int32, (K, K), 1)
    work_ref[:, K:] = (rows == cols).astype(jnp.float32)
    panel_row = lax.broadcasted_iota(jnp.int32, (PANEL, 128), 0)
    for start in range(0, K, PANEL):
        low = (start // 128) * 128
        high = K + ((start + PANEL + 127) // 128) * 128
        width = high - low
        offset = start - low
        panel = work_ref[start : start + PANEL, low:high]
        for first in range(0, PANEL, MICRO):
            columns = [
                jnp.broadcast_to(
                    panel[:, offset + first + k : offset + first + k + 1], (PANEL, 128)
                )
                for k in range(MICRO)
            ]
            for k in range(MICRO):
                j = first + k
                scale = jnp.where(panel_row > j, columns[k] * (1.0 / columns[k][j : j + 1, :]), 0.0)
                for later in range(k + 1, MICRO):
                    columns[later] = columns[later] - scale * columns[later][j : j + 1, :]
                panel = (
                    panel
                    - jnp.concatenate([scale] * (width // 128), axis=1) * panel[j : j + 1, :]
                )
        square_row = lax.broadcasted_iota(jnp.int32, (PANEL, PANEL), 0)
        square_col = lax.broadcasted_iota(jnp.int32, (PANEL, PANEL), 1)
        diagonal = jnp.where(square_row == square_col, panel[:, offset : offset + PANEL], 0.0)
        panel = panel * (1.0 / jnp.sqrt(jnp.sum(diagonal, axis=1, keepdims=True)))
        if squares_ref is not None:
            squares_ref[:, start : start + PANEL] = jnp.sum(diagonal, axis=0, keepdims=True)
        inverse_ref[start : start + PANEL, :] = jnp.zeros((PANEL, K), jnp.float32)
        inverse_ref[start : start + PANEL, : high - K] = panel[:, K - low :]
        after = start + PANEL
        if after < K:
            update = dot_tn(panel[:, after - low : K - low], panel)
            work_ref[after:, low:high] = work_ref[after:, low:high] - update


def first_factor_kernel(mine_ref, other_ref, core_ref, inverse_ref, work_ref):
    own = core_ref[0]
    for z in range(8):
        for core in range(2):
            part = jnp.where(own == core, mine_ref[z, 32:, :], other_ref[z, 32:, :])
            start = (2 * z + core) * 16
            work_ref[start : start + 8, :K] = part[:, :K]
            work_ref[start + 8 : start + 16, :K] = part[:, K:]
    eliminate(work_ref, inverse_ref, None)


def first_factor(mine, other, core):
    return pl.pallas_call(
        first_factor_kernel,
        out_shape=jax.ShapeDtypeStruct((K, K), jnp.float32),
        in_specs=[VMEM, VMEM, SMEM],
        out_specs=VMEM,
        scratch_shapes=[pltpu.VMEM((K, 2 * K), jnp.float32)],
        compiler_params=pltpu.CompilerParams(vmem_limit_bytes=16 * 2**20),
        cost_estimate=pl.CostEstimate(
            flops=4 * K**3, bytes_accessed=12 * K * K, transcendentals=K
        ),
        name="first_factor",
    )(mine, other, core)


def second_factor_kernel(
    gram_ref, first_ref, rows_ref, basis_ref, both_ref, weights_ref, inverse_ref, work_ref
):
    work_ref[:, :K] = gram_ref[...]
    eliminate(work_ref, inverse_ref, weights_ref)
    weights_ref[...] = jnp.sqrt(jnp.sqrt(jnp.sqrt(weights_ref[...])))
    both_ref[...] = dot(inverse_ref[...], first_ref[...])
    raw = jnp.concatenate([rows_ref[:32, :K], rows_ref[:32, K:]], axis=0)
    basis = dot_nt(dot_nt(raw, first_ref[...]), inverse_ref[...])
    basis_ref[0] = basis[:32]
    basis_ref[1] = basis[32:]


def second_factor(gram, first_inverse, rows):
    return pl.pallas_call(
        second_factor_kernel,
        out_shape=(
            jax.ShapeDtypeStruct((2, 32, K), jnp.float32),
            jax.ShapeDtypeStruct((K, K), jnp.float32),
            jax.ShapeDtypeStruct((1, K), jnp.float32),
        ),
        scratch_shapes=[
            pltpu.VMEM((K, K), jnp.float32),
            pltpu.VMEM((K, 2 * K), jnp.float32),
        ],
        compiler_params=pltpu.CompilerParams(vmem_limit_bytes=16 * 2**20),
        cost_estimate=pl.CostEstimate(
            flops=6 * K**3, bytes_accessed=16 * K * K, transcendentals=K
        ),
        name="second_factor",
    )(gram, first_inverse, rows)


def finish_kernel(pieces_ref, both_ref, weights_ref, beam_ref):
    lower = pieces_ref[0]
    upper = pieces_ref[1]
    for index in range(2, 8, 2):
        lower = lower + pieces_ref[index]
        upper = upper + pieces_ref[index + 1]
    real_part = jnp.concatenate([lower[:, :HALF], upper[:, :HALF]], axis=1)
    imag_part = jnp.concatenate([lower[:, HALF:], upper[:, HALF:]], axis=1)
    projected = dot_nt(jnp.concatenate([real_part, imag_part], axis=0), both_ref[...])
    square = projected * projected
    weights = weights_ref[...]
    power = dot_nt(weights, square[:128] + square[128:]) / jnp.sum(weights)
    power = power * power
    beam_ref[...] = power * power


def finish(pieces, both, weights):
    return pl.pallas_call(
        finish_kernel,
        out_shape=jax.ShapeDtypeStruct((1, 128), jnp.float32),
        compiler_params=pltpu.CompilerParams(vmem_limit_bytes=16 * 2**20),
        name="finish",
    )(pieces, both, weights)


def turned(block):
    return jnp.concatenate([-block[:, K:], block[:, :K]], axis=1)


def exchange(pieces, axis, groups=None):
    return lax.all_to_all(pieces, axis, 0, 0, tiled=True, axis_index_groups=groups)


def drain(copies):
    for copy in copies:
        copy.start()
    for copy in copies:
        copy.wait()


def spread_kernel(pieces_ref, total_ref, copies_ref, sems):
    total_ref[...] = jnp.sum(pieces_ref[...], axis=0)
    drain(
        [
            pltpu.make_async_copy(total_ref, copies_ref.at[index], sems.at[index])
            for index in range(copies_ref.shape[0])
        ]
    )


def spread(pieces, count):
    piece = pieces.shape[1:]
    return pl.pallas_call(
        spread_kernel,
        out_shape=(
            jax.ShapeDtypeStruct(piece, jnp.float32),
            pltpu.HBM((count,) + piece, jnp.float32),
        ),
        out_specs=(
            pl.BlockSpec(memory_space=pltpu.VMEM),
            pl.BlockSpec(memory_space=pltpu.HBM),
        ),
        scratch_shapes=[pltpu.SemaphoreType.DMA((count,))],
        compiler_params=pltpu.CompilerParams(vmem_limit_bytes=16 * 2**20),
        name="spread",
    )(pieces)


def halves(value):
    high = value.astype(jnp.bfloat16)
    return high, (value - high.astype(jnp.float32)).astype(jnp.bfloat16)


def split_dot(high, low, parts):
    total = jnp.dot(low, parts[0], preferred_element_type=jnp.float32)
    total += jnp.dot(high, parts[1], preferred_element_type=jnp.float32)
    return total + jnp.dot(high, parts[0], preferred_element_type=jnp.float32)


def in_hbm(value):
    return pltpu.with_memory_space_constraint(value, pltpu.HBM)


def fetch(high_ref, low_ref, tiles_ref, sems):
    copies = [
        pltpu.make_async_copy(ref, tiles_ref.at[index], sems.at[index])
        for index, ref in enumerate((high_ref, low_ref))
    ]
    for copy in copies:
        copy.start()
    return copies


def prepare_kernel(
    real_ref, imag_ref, core_ref, tile_high, tile_low, kept_high, kept_low, sent_high, sent_low
):
    first_core = core_ref[0] == 0
    for base, ref in ((0, real_ref), (512, imag_ref)):
        lanes = slice(base, base + 512)
        value = ref[...]
        tile_high[:, lanes], tile_low[:, lanes] = halves(value)
        rows = value.T.reshape(8, 2, 32, 512)
        kept = jnp.where(first_core, rows[:, 0], rows[:, 1]).reshape(256, 512)
        sent = jnp.where(first_core, rows[:, 1], rows[:, 0]).reshape(256, 512)
        kept_high[:, lanes], kept_low[:, lanes] = halves(kept)
        sent_high[:, lanes], sent_low[:, lanes] = halves(sent)


def prepare(real, imag, core):
    shapes = [(512, 1024)] * 2 + [(256, 1024)] * 4
    return pl.pallas_call(
        prepare_kernel,
        out_shape=tuple(pltpu.HBM(shape, jnp.bfloat16) for shape in shapes),
        in_specs=[VMEM, VMEM, SMEM],
        out_specs=(VMEM,) * 6,
        compiler_params=pltpu.CompilerParams(vmem_limit_bytes=24 * 2**20),
        cost_estimate=pl.CostEstimate(
            flops=20 * 512 * 1024, bytes_accessed=8 * 2**20, transcendentals=0
        ),
        name="prepare",
    )(real, imag, core)


def first_product_kernel(
    high_ref, low_ref, mine_ref, other_ref, core_ref,
    out_ref, start_ref, parts_ref, rows_ref, tiles_ref, sems, tile_sems,
):
    fetched = fetch(high_ref, low_ref, tiles_ref, tile_sems)
    core = core_ref[0]
    for z in range(8):
        start_ref[2 * z + core] = mine_ref[z]
        start_ref[2 * z + 1 - core] = other_ref[z]
    start = start_ref[...].reshape(512, 2 * K)
    for base, value in ((0, start), (512, turned(start))):
        for index, part in enumerate(halves(value)):
            parts_ref[index, base : base + 512, :] = part
    parts = [parts_ref[index] for index in range(2)]
    for copy in fetched:
        copy.wait()
    copies = []
    for block in range(4):
        at = slice(block * 128, block * 128 + 128)
        product = split_dot(tiles_ref[0, at, :], tiles_ref[1, at, :], parts)
        four = pl.ds(block * 4, 4)
        rows_ref[four] = product.reshape(4, 32, 2 * K)
        copies.append(
            pltpu.make_async_copy(rows_ref.at[four], out_ref.at[four], sems.at[block])
        )
        copies[-1].start()
    for copy in copies:
        copy.wait()


def first_product(high, low, mine, other, core):
    return pl.pallas_call(
        first_product_kernel,
        out_shape=pltpu.HBM((16, 32, 2 * K), jnp.float32),
        in_specs=[HBM, HBM, VMEM, VMEM, SMEM],
        out_specs=HBM,
        scratch_shapes=[
            pltpu.VMEM((16, 32, 2 * K), jnp.float32),
            pltpu.VMEM((2, 1024, 2 * K), jnp.bfloat16),
            pltpu.VMEM((16, 32, 2 * K), jnp.float32),
            pltpu.VMEM((2, 512, 1024), jnp.bfloat16),
            pltpu.SemaphoreType.DMA((4,)),
            pltpu.SemaphoreType.DMA((2,)),
        ],
        compiler_params=pltpu.CompilerParams(vmem_limit_bytes=24 * 2**20),
        cost_estimate=pl.CostEstimate(
            flops=6 * 512 * 1024 * 512, bytes_accessed=5 * 2**20, transcendentals=0
        ),
        name="first_product",
    )(in_hbm(high), in_hbm(low), mine, other, core)


def sent_product_kernel(
    high_ref, low_ref, first_ref, core_ref, out_ref, kept_ref, parts_ref, gram_ref
):
    first = first_ref[...].reshape(512, 2 * K)
    for base, value in ((0, first), (512, -turned(first))):
        for index, part in enumerate(halves(value)):
            parts_ref[index, base : base + 512, :] = part
    rows = jnp.concatenate([first[:, :K], first[:, K:]], axis=0)
    gram_ref[...] = dot_tn(rows, rows)
    core = core_ref[0]
    for z in range(8):
        for which, target, at in ((core, kept_ref, 0), (1 - core, out_ref, 32)):
            start = pl.multiple_of(z * 32 + which * 16, 16)
            target[z, at : at + 8, :K] = gram_ref[pl.ds(start, 8), :]
            target[z, at : at + 8, K:] = gram_ref[pl.ds(start + 8, 8), :]
    share(high_ref, low_ref, parts_ref, out_ref)


def share(high_ref, low_ref, parts_ref, out_ref):
    parts = [parts_ref[index] for index in range(2)]
    for block in range(2):
        at = slice(block * 128, block * 128 + 128)
        product = split_dot(high_ref[at, :], low_ref[at, :], parts)
        out_ref[block * 4 : block * 4 + 4, :32, :] = product.reshape(4, 32, 2 * K)


def sent_product(high, low, first, core):
    return pl.pallas_call(
        sent_product_kernel,
        out_shape=(
            jax.ShapeDtypeStruct((8, 40, 2 * K), jnp.float32),
            jax.ShapeDtypeStruct((8, 8, 2 * K), jnp.float32),
            jax.ShapeDtypeStruct((2, 1024, 2 * K), jnp.bfloat16),
        ),
        in_specs=[VMEM] * 3 + [SMEM],
        out_specs=(VMEM,) * 3,
        scratch_shapes=[pltpu.VMEM((K, K), jnp.float32)],
        compiler_params=pltpu.CompilerParams(vmem_limit_bytes=24 * 2**20),
        cost_estimate=pl.CostEstimate(
            flops=6 * 256 * 1024 * 512, bytes_accessed=5 * 2**20, transcendentals=0
        ),
        name="sent_product",
    )(high, low, first, core)


def kept_product_kernel(high_ref, low_ref, parts_ref, gram_ref, out_ref):
    out_ref[:, 32:, :] = gram_ref[...]
    share(high_ref, low_ref, parts_ref, out_ref)


def kept_product(high, low, parts, gram):
    return pl.pallas_call(
        kept_product_kernel,
        out_shape=jax.ShapeDtypeStruct((8, 40, 2 * K), jnp.float32),
        in_specs=[VMEM] * 4,
        out_specs=VMEM,
        compiler_params=pltpu.CompilerParams(vmem_limit_bytes=24 * 2**20),
        cost_estimate=pl.CostEstimate(
            flops=6 * 256 * 1024 * 512, bytes_accessed=5 * 2**20, transcendentals=0
        ),
        name="kept_product",
    )(high, low, parts, gram)


def stage_kernel(*refs):
    terms, out_ref, total_ref, sem = refs[:-3], refs[-3], refs[-2], refs[-1]
    total = terms[0][...]
    for term in terms[1:]:
        total = total + term[...]
    total_ref[...] = total
    drain([pltpu.make_async_copy(total_ref, out_ref, sem)])


def stage(*terms):
    shape = jax.ShapeDtypeStruct(terms[0].shape, jnp.float32)
    return pl.pallas_call(
        stage_kernel,
        out_shape=pltpu.HBM(shape.shape, jnp.float32),
        out_specs=pl.BlockSpec(memory_space=pltpu.HBM),
        scratch_shapes=[pltpu.VMEM(shape.shape, jnp.float32), pltpu.SemaphoreType.DMA],
        compiler_params=pltpu.CompilerParams(vmem_limit_bytes=16 * 2**20),
        name="stage",
    )(*terms)


SIN_TERMS = (
    3.1415926535362906,
    -5.167712764624546,
    2.550163318947043,
    -0.5992521978220368,
    0.08205040179571269,
    -0.007028386383306818,
)
COS_TERMS = (
    0.9999999997799041,
    -4.9348021370788295,
    4.058709159556314,
    -1.335212003049894,
    0.23493731381328964,
    -0.024396324346460163,
)


def polynomial(terms, x):
    value = terms[-1]
    for term in terms[-2::-1]:
        value = value * x + term
    return value


def spread_start_kernel(start_ref, copies_ref, total_ref, sems):
    total_ref[:, :K] = start_ref[0]
    total_ref[:, K:] = start_ref[1]
    drain(
        [
            pltpu.make_async_copy(total_ref, copies_ref.at[index], sems.at[index])
            for index in range(8)
        ]
    )


def spread_start(start):
    return pl.pallas_call(
        spread_start_kernel,
        out_shape=pltpu.HBM((8, 32, 2 * K), jnp.float32),
        in_specs=[VMEM],
        out_specs=HBM,
        scratch_shapes=[pltpu.VMEM((32, 2 * K), jnp.float32), pltpu.SemaphoreType.DMA((8,))],
        compiler_params=pltpu.CompilerParams(vmem_limit_bytes=8 * 2**20),
        name="spread_start",
    )(start)


def steering_kernel(grid_ref, mics_ref, *refs):
    index = (
        grid_ref[:, 0:1] * mics_ref[0:1, :] + grid_ref[:, 1:2] * mics_ref[1:2, :]
    )
    turns = (index - jnp.round(index * (1.0 / MOD)) * float(MOD)) * (1.0 / MOD)
    square = turns * turns
    half_sine = turns * polynomial(SIN_TERMS, square)
    half_cosine = polynomial(COS_TERMS, square)
    cosine = 1.0 - 2.0 * half_sine * half_sine
    sine = 2.0 * half_sine * half_cosine
    for value, high_ref, low_ref in ((cosine, refs[-4], refs[-3]), (sine, refs[-2], refs[-1])):
        high_ref[...], low_ref[...] = halves(value)


def steering(grid, mics, first, count, before=()):
    block = pl.BlockSpec((256, 1024), lambda i: ((i + first) // 2, (i + first) % 2))
    return pl.pallas_call(
        steering_kernel,
        grid=(count,),
        in_specs=[
            pl.BlockSpec((256, 2), lambda i: ((i + first) // 2, 0)),
            pl.BlockSpec((2, 1024), lambda i: (0, (i + first) % 2)),
        ]
        + [HBM] * len(before),
        out_specs=(block,) * 4,
        out_shape=(pltpu.HBM((1024, 2048), jnp.bfloat16),) * 4,
        input_output_aliases={2 + index: index for index in range(len(before))},
        compiler_params=pltpu.CompilerParams(vmem_limit_bytes=24 * 2**20),
        cost_estimate=pl.CostEstimate(
            flops=45 * 256 * 1024 * count, bytes_accessed=8 * 256 * 1024 * count, transcendentals=0
        ),
        name="steering",
    )(grid, mics, *before)


def second_gram_kernel(mine_ref, other_ref, inverse_ref, row_ref, copies_ref, slice_ref, sems):
    own = pl.multiple_of(row_ref[0] * 16, 16)
    raw = jnp.concatenate(
        [
            ref[:, :32, lanes].reshape(256, K)
            for ref in (mine_ref, other_ref)
            for lanes in (slice(0, K), slice(K, 2 * K))
        ],
        axis=0,
    )
    second = dot_nt(raw, inverse_ref[...])
    turned_slice = dot_nt(inverse_ref[pl.ds(own, 16), :], raw)
    slice_ref[...] = dot(turned_slice, second)
    drain(
        [
            pltpu.make_async_copy(slice_ref, copies_ref.at[index], sems.at[index])
            for index in range(16)
        ]
    )


def second_gram_slice(mine, other, inverse, row):
    return pl.pallas_call(
        second_gram_kernel,
        out_shape=pltpu.HBM((16, 16, K), jnp.float32),
        in_specs=[VMEM, VMEM, VMEM, SMEM],
        out_specs=HBM,
        scratch_shapes=[pltpu.VMEM((16, K), jnp.float32), pltpu.SemaphoreType.DMA((16,))],
        compiler_params=pltpu.CompilerParams(vmem_limit_bytes=24 * 2**20),
        cost_estimate=pl.CostEstimate(
            flops=2 * 1024 * K * (K + 32), bytes_accessed=2**21, transcendentals=0
        ),
        name="second_gram",
    )(mine, other, inverse, row)


def project_kernel(half_ref, *refs):
    raw_refs, beside_refs = refs[:2], refs[2:8]
    cos_high, cos_low, sin_high, sin_low = refs[8:12]
    out_ref, high_ref, low_ref, slots, sems = refs[12:]
    step = pl.program_id(0)

    @pl.when(step == 0)
    def _():
        lower = half_ref[0] == 0
        sources = []
        for ref in raw_refs:
            parts = [
                ref[:, :32, lane : lane + HALF].reshape(256, HALF) for lane in range(0, 2 * K, HALF)
            ]
            sources.append(
                (jnp.where(lower, parts[0], parts[1]), jnp.where(lower, parts[2], parts[3]))
            )
        for ref in beside_refs:
            sources.append((ref[:, :, :HALF].reshape(256, HALF), ref[:, :, HALF:].reshape(256, HALF)))
        for index, (real, imag) in enumerate(sources):
            start = index * 256
            for base, value in (
                (0, jnp.concatenate([real, imag], axis=1)),
                (2048, jnp.concatenate([-imag, real], axis=1)),
            ):
                high, low = halves(value)
                high_ref[base + start : base + start + 256, :] = high
                low_ref[base + start : base + start + 256, :] = low

    high = jnp.concatenate([cos_high[...], sin_high[...]], axis=1)
    low = jnp.concatenate([cos_low[...], sin_low[...]], axis=1)
    product = jnp.dot(high, high_ref[...], preferred_element_type=jnp.float32)
    product += jnp.dot(high, low_ref[...], preferred_element_type=jnp.float32)
    product += jnp.dot(low, high_ref[...], preferred_element_type=jnp.float32)
    slots[pl.ds(2 * step, 2)] = product.reshape(2, 128, 256)

    def copy(index):
        both = pl.ds(2 * index, 2)
        return pltpu.make_async_copy(slots.at[both], out_ref.at[both], sems.at[index])

    copy(step).start()

    @pl.when(step == 3)
    def _():
        for index in range(4):
            copy(index).wait()


def project(half, raw, beside, steered):
    block = pl.BlockSpec((256, 2048), lambda i: (i, 0))
    return pl.pallas_call(
        project_kernel,
        grid=(4,),
        in_specs=[SMEM]
        + [pl.BlockSpec((8, 40, 512), lambda i: (0, 0, 0))] * 2
        + [pl.BlockSpec((8, 32, 256), lambda i: (0, 0, 0))] * 6
        + [block] * 4,
        out_specs=HBM,
        out_shape=pltpu.HBM((8, 128, 256), jnp.float32),
        scratch_shapes=[
            pltpu.VMEM((4096, 256), jnp.bfloat16),
            pltpu.VMEM((4096, 256), jnp.bfloat16),
            pltpu.VMEM((8, 128, 256), jnp.float32),
            pltpu.SemaphoreType.DMA((4,)),
        ],
        compiler_params=pltpu.CompilerParams(vmem_limit_bytes=40 * 2**20),
        cost_estimate=pl.CostEstimate(
            flops=3 * 2 * 1024 * 4096 * 256, bytes_accessed=18 * 2**20, transcendentals=0
        ),
        name="project",
    )(half, *raw, *beside, *[in_hbm(value) for value in steered])


def half_of_vectors(pieces, half):
    lower = jnp.concatenate([pieces[..., :HALF], pieces[..., K : K + HALF]], axis=-1)
    upper = jnp.concatenate([pieces[..., HALF:K], pieces[..., K + HALF :]], axis=-1)
    return jnp.where(half == 0, lower, upper)


def body(csm_real, csm_imag, start_block, mic_coords, grid_coords, bin_index):
    row = lax.axis_index("row")
    core = row % 2
    own_core = core.reshape(1)
    col = lax.axis_index("col")
    half = col % 2
    points = grid_coords.reshape(2, 4, 2, 256)
    points = jnp.where(col // 2 % 2 == 0, points[:, :, 0], points[:, :, 1]).reshape(2, 1024)
    reduced = ((bin_index * points) % MOD).astype(jnp.float32).T

    mine = exchange(spread_start(start_block), "row", Z_GROUPS)
    *tiles, mic_coords, reduced = lax.optimization_barrier(
        (*prepare(csm_real, csm_imag, own_core), mic_coords, reduced)
    )
    places = [mic_coords] + [lax.ppermute(mic_coords, "col", ALONG_X[flip]) for flip in (1, 2, 3)]
    mine, *places = lax.optimization_barrier((mine, *places, *tiles))
    places, tiles = places[:4], places[4:]
    other = lax.ppermute(mine, "row", CORE_SWAP)
    first_partial = first_product(*tiles[:2], mine, other, own_core)

    places = jnp.stack(places, axis=1).reshape(2, 4, 8, 2, 32)
    even, odd = places[:, :, :, 0], places[:, :, :, 1]
    mics = jnp.stack([jnp.where(core == 0, even, odd), jnp.where(core == 0, odd, even)], axis=2)
    mics = mics.reshape(2, 2048).astype(jnp.float32)
    steered = steering(reduced, mics, 0, 3)
    first_pieces = exchange(first_partial, "col")
    first_pieces, steered = lax.optimization_barrier((first_pieces, steered))

    steered = steering(reduced, mics, 3, 2, steered)
    first = exchange(spread(first_pieces, 16)[1], "col")
    first, steered = lax.optimization_barrier((first, steered))
    sent, gram_rows, parts = sent_product(*tiles[4:], first, own_core)
    got = lax.ppermute(sent, "row", CORE_SWAP)
    kept = kept_product(*tiles[2:4], parts, gram_rows)
    pair = stage(kept, got)

    steered = steering(reduced, mics, 5, 2, steered)
    pieces = exchange(pair, "row", Z_GROUPS)
    pieces, steered = lax.optimization_barrier((pieces, steered))
    own, spread_out = spread(pieces, 8)

    steered = steering(reduced, mics, 7, 1, steered)
    mine = exchange(spread_out, "row", Z_GROUPS)
    mine, steered = lax.optimization_barrier((mine, steered))
    other = lax.ppermute(mine, "row", CORE_SWAP)
    taken = half_of_vectors(mine[:, :32], half)
    given = half_of_vectors(mine[:, :32], 1 - half)
    near = [
        lax.ppermute(taken if flip == 2 else given, "col", ALONG_X[flip]) for flip in (1, 2, 3)
    ]
    first_inverse = first_factor(mine, other, own_core)
    gram_copies = second_gram_slice(mine, other, first_inverse, row.reshape(1))
    near, gram_copies = lax.optimization_barrier((near, gram_copies))
    far = [lax.ppermute(block, "row", CORE_SWAP) for block in near]
    beside = [block for both in zip(near, far) for block in both]
    gram_pieces = exchange(gram_copies, "col")
    part = project(half.reshape(1), (mine, other), beside, steered)
    part, gram_pieces = lax.optimization_barrier((part, gram_pieces))
    pieces = exchange(part, "col", POINT_GROUPS)
    second_gram = lax.all_gather(jnp.sum(gram_pieces, axis=0), "row", axis=0, tiled=True)
    basis, both_inverse, weights = second_factor(second_gram, first_inverse, own)
    return (basis, finish(pieces, both_inverse, weights).reshape(128))


def solution(mesh):
    in_specs = (
        P("row", "col"),
        P("row", "col"),
        P(None, ("col", "row"), None),
        P(None, "col"),
        P(None, "row"),
        P(),
    )
    out_specs = (P(None, ("col", "row"), None), P(("row", "col")))
    return jax.shard_map(body, mesh=mesh, in_specs=in_specs, out_specs=out_specs, check_vma=False)
```

```python
import jax
import jax.numpy as jnp
from jax import lax
from jax.experimental import pallas as pl
from jax.experimental.pallas import tpu as pltpu
from jax.sharding import PartitionSpec as P

NU = 4
K = 256
MOD = 4093
HIGH = lax.Precision.HIGHEST

Z_GROUPS = [list(range(core, 16, 2)) for core in range(2)]
CORE_SWAP = [(index, index ^ 1) for index in range(16)]

ALONG_X = [[(index, index ^ flip) for index in range(16)] for flip in range(4)]
POINT_GROUPS = [[index for index in range(16) if index // 2 % 2 == part] for part in range(2)]
HALF = K // 2
SMEM = pl.BlockSpec(memory_space=pltpu.SMEM)
HBM = pl.BlockSpec(memory_space=pltpu.HBM)
VMEM = pl.BlockSpec(memory_space=pltpu.VMEM)

PANEL = 64
MICRO = 16


def dot(a, b):
    return jnp.dot(a, b, precision=HIGH, preferred_element_type=jnp.float32)


def dot_tn(a, b):
    return lax.dot_general(
        a, b, (((0,), (0,)), ((), ())), precision=HIGH, preferred_element_type=jnp.float32
    )


def dot_nt(a, b):
    return lax.dot_general(
        a, b, (((1,), (1,)), ((), ())), precision=HIGH, preferred_element_type=jnp.float32
    )


def eliminate(work_ref, inverse_ref, squares_ref):
    rows = lax.broadcasted_iota(jnp.int32, (K, K), 0)
    cols = lax.broadcasted_iota(jnp.int32, (K, K), 1)
    work_ref[:, K:] = (rows == cols).astype(jnp.float32)
    panel_row = lax.broadcasted_iota(jnp.int32, (PANEL, 128), 0)
    for start in range(0, K, PANEL):
        low = (start // 128) * 128
        high = K + ((start + PANEL + 127) // 128) * 128
        width = high - low
        offset = start - low
        panel = work_ref[start : start + PANEL, low:high]
        for first in range(0, PANEL, MICRO):
            columns = [
                jnp.broadcast_to(
                    panel[:, offset + first + k : offset + first + k + 1], (PANEL, 128)
                )
                for k in range(MICRO)
            ]
            for k in range(MICRO):
                j = first + k
                scale = jnp.where(panel_row > j, columns[k] * (1.0 / columns[k][j : j + 1, :]), 0.0)
                for later in range(k + 1, MICRO):
                    columns[later] = columns[later] - scale * columns[later][j : j + 1, :]
                panel = (
                    panel
                    - jnp.concatenate([scale] * (width // 128), axis=1) * panel[j : j + 1, :]
                )
        square_row = lax.broadcasted_iota(jnp.int32, (PANEL, PANEL), 0)
        square_col = lax.broadcasted_iota(jnp.int32, (PANEL, PANEL), 1)
        diagonal = jnp.where(square_row == square_col, panel[:, offset : offset + PANEL], 0.0)
        panel = panel * (1.0 / jnp.sqrt(jnp.sum(diagonal, axis=1, keepdims=True)))
        if squares_ref is not None:
            squares_ref[:, start : start + PANEL] = jnp.sum(diagonal, axis=0, keepdims=True)
        inverse_ref[start : start + PANEL, :] = jnp.zeros((PANEL, K), jnp.float32)
        inverse_ref[start : start + PANEL, : high - K] = panel[:, K - low :]
        after = start + PANEL
        if after < K:
            update = dot_tn(panel[:, after - low : K - low], panel)
            work_ref[after:, low:high] = work_ref[after:, low:high] - update


def first_factor_kernel(mine_ref, other_ref, core_ref, inverse_ref, work_ref):
    own = core_ref[0]
    for z in range(8):
        for core in range(2):
            part = jnp.where(own == core, mine_ref[z, 32:, :], other_ref[z, 32:, :])
            start = (2 * z + core) * 16
            work_ref[start : start + 8, :K] = part[:, :K]
            work_ref[start + 8 : start + 16, :K] = part[:, K:]
    eliminate(work_ref, inverse_ref, None)


def first_factor(mine, other, core):
    return pl.pallas_call(
        first_factor_kernel,
        out_shape=jax.ShapeDtypeStruct((K, K), jnp.float32),
        in_specs=[VMEM, VMEM, SMEM],
        out_specs=VMEM,
        scratch_shapes=[pltpu.VMEM((K, 2 * K), jnp.float32)],
        compiler_params=pltpu.CompilerParams(vmem_limit_bytes=16 * 2**20),
        cost_estimate=pl.CostEstimate(
            flops=4 * K**3, bytes_accessed=12 * K * K, transcendentals=K
        ),
        name="first_factor",
    )(mine, other, core)


def second_factor_kernel(
    gram_ref, first_ref, rows_ref, basis_ref, both_ref, weights_ref, inverse_ref, work_ref
):
    work_ref[:, :K] = gram_ref[...]
    eliminate(work_ref, inverse_ref, weights_ref)
    weights_ref[...] = jnp.sqrt(jnp.sqrt(jnp.sqrt(weights_ref[...])))
    both_ref[...] = dot(inverse_ref[...], first_ref[...])
    raw = jnp.concatenate([rows_ref[:32, :K], rows_ref[:32, K:]], axis=0)
    basis = dot_nt(dot_nt(raw, first_ref[...]), inverse_ref[...])
    basis_ref[0] = basis[:32]
    basis_ref[1] = basis[32:]


def second_factor(gram, first_inverse, rows):
    return pl.pallas_call(
        second_factor_kernel,
        out_shape=(
            jax.ShapeDtypeStruct((2, 32, K), jnp.float32),
            jax.ShapeDtypeStruct((K, K), jnp.float32),
            jax.ShapeDtypeStruct((1, K), jnp.float32),
        ),
        scratch_shapes=[
            pltpu.VMEM((K, K), jnp.float32),
            pltpu.VMEM((K, 2 * K), jnp.float32),
        ],
        compiler_params=pltpu.CompilerParams(vmem_limit_bytes=16 * 2**20),
        cost_estimate=pl.CostEstimate(
            flops=6 * K**3, bytes_accessed=16 * K * K, transcendentals=K
        ),
        name="second_factor",
    )(gram, first_inverse, rows)


def finish_kernel(pieces_ref, both_ref, weights_ref, beam_ref):
    lower = pieces_ref[0]
    upper = pieces_ref[1]
    for index in range(2, 8, 2):
        lower = lower + pieces_ref[index]
        upper = upper + pieces_ref[index + 1]
    real_part = jnp.concatenate([lower[:, :HALF], upper[:, :HALF]], axis=1)
    imag_part = jnp.concatenate([lower[:, HALF:], upper[:, HALF:]], axis=1)
    projected = dot_nt(jnp.concatenate([real_part, imag_part], axis=0), both_ref[...])
    square = projected * projected
    weights = weights_ref[...]
    power = dot_nt(weights, square[:128] + square[128:]) / jnp.sum(weights)
    power = power * power
    beam_ref[...] = power * power


def finish(pieces, both, weights):
    return pl.pallas_call(
        finish_kernel,
        out_shape=jax.ShapeDtypeStruct((1, 128), jnp.float32),
        compiler_params=pltpu.CompilerParams(vmem_limit_bytes=16 * 2**20),
        name="finish",
    )(pieces, both, weights)


def turned(block):
    return jnp.concatenate([-block[:, K:], block[:, :K]], axis=1)


def exchange(pieces, axis, groups=None):
    return lax.all_to_all(pieces, axis, 0, 0, tiled=True, axis_index_groups=groups)


def drain(copies):
    for copy in copies:
        copy.start()
    for copy in copies:
        copy.wait()


def spread_kernel(pieces_ref, total_ref, copies_ref, sems):
    copies = []
    for part, rows in enumerate((pl.ds(0, 16), pl.ds(16, total_ref.shape[0] - 16))):
        total_ref[rows, :] = jnp.sum(pieces_ref[:, rows, :], axis=0)
        for index in range(copies_ref.shape[0]):
            copies.append(
                pltpu.make_async_copy(
                    total_ref.at[rows], copies_ref.at[index, rows], sems.at[part, index]
                )
            )
            copies[-1].start()
    for copy in copies:
        copy.wait()


def spread(pieces, count):
    piece = pieces.shape[1:]
    return pl.pallas_call(
        spread_kernel,
        out_shape=(
            jax.ShapeDtypeStruct(piece, jnp.float32),
            pltpu.HBM((count,) + piece, jnp.float32),
        ),
        out_specs=(
            pl.BlockSpec(memory_space=pltpu.VMEM),
            pl.BlockSpec(memory_space=pltpu.HBM),
        ),
        scratch_shapes=[pltpu.SemaphoreType.DMA((2, count))],
        compiler_params=pltpu.CompilerParams(vmem_limit_bytes=16 * 2**20),
        name="spread",
    )(pieces)


def halves(value):
    high = value.astype(jnp.bfloat16)
    return high, (value - high.astype(jnp.float32)).astype(jnp.bfloat16)


def split_dot(high, low, parts):
    total = jnp.dot(low, parts[0], preferred_element_type=jnp.float32)
    total += jnp.dot(high, parts[1], preferred_element_type=jnp.float32)
    return total + jnp.dot(high, parts[0], preferred_element_type=jnp.float32)


def in_hbm(value):
    return pltpu.with_memory_space_constraint(value, pltpu.HBM)


def fetch(high_ref, low_ref, tiles_ref, sems):
    copies = [
        pltpu.make_async_copy(ref, tiles_ref.at[index], sems.at[index])
        for index, ref in enumerate((high_ref, low_ref))
    ]
    for copy in copies:
        copy.start()
    return copies


def prepare_kernel(
    real_ref, imag_ref, core_ref, tile_high, tile_low, kept_high, kept_low, sent_high, sent_low
):
    first_core = core_ref[0] == 0
    for base, ref in ((0, real_ref), (512, imag_ref)):
        lanes = slice(base, base + 512)
        value = ref[...]
        tile_high[:, lanes], tile_low[:, lanes] = halves(value)
        rows = value.T.reshape(8, 2, 32, 512)
        kept = jnp.where(first_core, rows[:, 0], rows[:, 1]).reshape(256, 512)
        sent = jnp.where(first_core, rows[:, 1], rows[:, 0]).reshape(256, 512)
        kept_high[:, lanes], kept_low[:, lanes] = halves(kept)
        sent_high[:, lanes], sent_low[:, lanes] = halves(sent)


def prepare(real, imag, core):
    shapes = [(512, 1024)] * 2 + [(256, 1024)] * 4
    return pl.pallas_call(
        prepare_kernel,
        out_shape=tuple(pltpu.HBM(shape, jnp.bfloat16) for shape in shapes),
        in_specs=[VMEM, VMEM, SMEM],
        out_specs=(VMEM,) * 6,
        compiler_params=pltpu.CompilerParams(vmem_limit_bytes=24 * 2**20),
        cost_estimate=pl.CostEstimate(
            flops=20 * 512 * 1024, bytes_accessed=8 * 2**20, transcendentals=0
        ),
        name="prepare",
    )(real, imag, core)


def first_product_kernel(
    high_ref, low_ref, mine_ref, other_ref, core_ref,
    out_ref, start_ref, parts_ref, rows_ref, tiles_ref, sems, tile_sems,
):
    fetched = fetch(high_ref, low_ref, tiles_ref, tile_sems)
    core = core_ref[0]
    for z in range(8):
        start_ref[2 * z + core] = mine_ref[z]
        start_ref[2 * z + 1 - core] = other_ref[z]
    start = start_ref[...].reshape(512, 2 * K)
    for base, value in ((0, start), (512, turned(start))):
        for index, part in enumerate(halves(value)):
            parts_ref[index, base : base + 512, :] = part
    parts = [parts_ref[index] for index in range(2)]
    for copy in fetched:
        copy.wait()
    copies = []
    for block in range(4):
        at = slice(block * 128, block * 128 + 128)
        product = split_dot(tiles_ref[0, at, :], tiles_ref[1, at, :], parts)
        four = pl.ds(block * 4, 4)
        rows_ref[four] = product.reshape(4, 32, 2 * K)
        copies.append(
            pltpu.make_async_copy(rows_ref.at[four], out_ref.at[four], sems.at[block])
        )
        copies[-1].start()
    for copy in copies:
        copy.wait()


def first_product(high, low, mine, other, core):
    return pl.pallas_call(
        first_product_kernel,
        out_shape=pltpu.HBM((16, 32, 2 * K), jnp.float32),
        in_specs=[HBM, HBM, VMEM, VMEM, SMEM],
        out_specs=HBM,
        scratch_shapes=[
            pltpu.VMEM((16, 32, 2 * K), jnp.float32),
            pltpu.VMEM((2, 1024, 2 * K), jnp.bfloat16),
            pltpu.VMEM((16, 32, 2 * K), jnp.float32),
            pltpu.VMEM((2, 512, 1024), jnp.bfloat16),
            pltpu.SemaphoreType.DMA((4,)),
            pltpu.SemaphoreType.DMA((2,)),
        ],
        compiler_params=pltpu.CompilerParams(vmem_limit_bytes=24 * 2**20),
        cost_estimate=pl.CostEstimate(
            flops=6 * 512 * 1024 * 512, bytes_accessed=5 * 2**20, transcendentals=0
        ),
        name="first_product",
    )(in_hbm(high), in_hbm(low), mine, other, core)


def sent_product_kernel(
    high_ref, low_ref, first_ref, core_ref, out_ref, kept_ref, parts_ref, gram_ref
):
    first = first_ref[...].reshape(512, 2 * K)
    for base, value in ((0, first), (512, -turned(first))):
        for index, part in enumerate(halves(value)):
            parts_ref[index, base : base + 512, :] = part
    rows = jnp.concatenate([first[:, :K], first[:, K:]], axis=0)
    gram_ref[...] = dot_tn(rows, rows)
    core = core_ref[0]
    for z in range(8):
        for which, target, at in ((core, kept_ref, 0), (1 - core, out_ref, 32)):
            start = pl.multiple_of(z * 32 + which * 16, 16)
            target[z, at : at + 8, :K] = gram_ref[pl.ds(start, 8), :]
            target[z, at : at + 8, K:] = gram_ref[pl.ds(start + 8, 8), :]
    share(high_ref, low_ref, parts_ref, out_ref)


def share(high_ref, low_ref, parts_ref, out_ref):
    parts = [parts_ref[index] for index in range(2)]
    for block in range(2):
        at = slice(block * 128, block * 128 + 128)
        product = split_dot(high_ref[at, :], low_ref[at, :], parts)
        out_ref[block * 4 : block * 4 + 4, :32, :] = product.reshape(4, 32, 2 * K)


def sent_product(high, low, first, core):
    return pl.pallas_call(
        sent_product_kernel,
        out_shape=(
            jax.ShapeDtypeStruct((8, 40, 2 * K), jnp.float32),
            jax.ShapeDtypeStruct((8, 8, 2 * K), jnp.float32),
            jax.ShapeDtypeStruct((2, 1024, 2 * K), jnp.bfloat16),
        ),
        in_specs=[VMEM] * 3 + [SMEM],
        out_specs=(VMEM,) * 3,
        scratch_shapes=[pltpu.VMEM((K, K), jnp.float32)],
        compiler_params=pltpu.CompilerParams(vmem_limit_bytes=24 * 2**20),
        cost_estimate=pl.CostEstimate(
            flops=6 * 256 * 1024 * 512, bytes_accessed=5 * 2**20, transcendentals=0
        ),
        name="sent_product",
    )(high, low, first, core)


def kept_product_kernel(high_ref, low_ref, parts_ref, gram_ref, out_ref):
    out_ref[:, 32:, :] = gram_ref[...]
    share(high_ref, low_ref, parts_ref, out_ref)


def kept_product(high, low, parts, gram):
    return pl.pallas_call(
        kept_product_kernel,
        out_shape=jax.ShapeDtypeStruct((8, 40, 2 * K), jnp.float32),
        in_specs=[VMEM] * 4,
        out_specs=VMEM,
        compiler_params=pltpu.CompilerParams(vmem_limit_bytes=24 * 2**20),
        cost_estimate=pl.CostEstimate(
            flops=6 * 256 * 1024 * 512, bytes_accessed=5 * 2**20, transcendentals=0
        ),
        name="kept_product",
    )(high, low, parts, gram)


def stage_kernel(*refs):
    terms, out_ref, total_ref, sem = refs[:-3], refs[-3], refs[-2], refs[-1]
    total = terms[0][...]
    for term in terms[1:]:
        total = total + term[...]
    total_ref[...] = total
    drain([pltpu.make_async_copy(total_ref, out_ref, sem)])


def stage(*terms):
    shape = jax.ShapeDtypeStruct(terms[0].shape, jnp.float32)
    return pl.pallas_call(
        stage_kernel,
        out_shape=pltpu.HBM(shape.shape, jnp.float32),
        out_specs=pl.BlockSpec(memory_space=pltpu.HBM),
        scratch_shapes=[pltpu.VMEM(shape.shape, jnp.float32), pltpu.SemaphoreType.DMA],
        compiler_params=pltpu.CompilerParams(vmem_limit_bytes=16 * 2**20),
        name="stage",
    )(*terms)


SIN_TERMS = (
    3.1415926535362906,
    -5.167712764624546,
    2.550163318947043,
    -0.5992521978220368,
    0.08205040179571269,
    -0.007028386383306818,
)
COS_TERMS = (
    0.9999999997799041,
    -4.9348021370788295,
    4.058709159556314,
    -1.335212003049894,
    0.23493731381328964,
    -0.024396324346460163,
)


def polynomial(terms, x):
    value = terms[-1]
    for term in terms[-2::-1]:
        value = value * x + term
    return value


def spread_start_kernel(start_ref, copies_ref, total_ref, sems):
    total_ref[:, :K] = start_ref[0]
    total_ref[:, K:] = start_ref[1]
    drain(
        [
            pltpu.make_async_copy(total_ref, copies_ref.at[index], sems.at[index])
            for index in range(8)
        ]
    )


def spread_start(start):
    return pl.pallas_call(
        spread_start_kernel,
        out_shape=pltpu.HBM((8, 32, 2 * K), jnp.float32),
        in_specs=[VMEM],
        out_specs=HBM,
        scratch_shapes=[pltpu.VMEM((32, 2 * K), jnp.float32), pltpu.SemaphoreType.DMA((8,))],
        compiler_params=pltpu.CompilerParams(vmem_limit_bytes=8 * 2**20),
        name="spread_start",
    )(start)


def steering_kernel(grid_ref, mics_ref, *refs):
    index = (
        grid_ref[:, 0:1] * mics_ref[0:1, :] + grid_ref[:, 1:2] * mics_ref[1:2, :]
    )
    turns = (index - jnp.round(index * (1.0 / MOD)) * float(MOD)) * (1.0 / MOD)
    square = turns * turns
    half_sine = turns * polynomial(SIN_TERMS, square)
    half_cosine = polynomial(COS_TERMS, square)
    cosine = 1.0 - 2.0 * half_sine * half_sine
    sine = 2.0 * half_sine * half_cosine
    for value, high_ref, low_ref in ((cosine, refs[-4], refs[-3]), (sine, refs[-2], refs[-1])):
        high_ref[...], low_ref[...] = halves(value)


def steering(grid, mics, first, count, before=()):
    block = pl.BlockSpec((256, 1024), lambda i: ((i + first) // 2, (i + first) % 2))
    return pl.pallas_call(
        steering_kernel,
        grid=(count,),
        in_specs=[
            pl.BlockSpec((256, 2), lambda i: ((i + first) // 2, 0)),
            pl.BlockSpec((2, 1024), lambda i: (0, (i + first) % 2)),
        ]
        + [HBM] * len(before),
        out_specs=(block,) * 4,
        out_shape=(pltpu.HBM((1024, 2048), jnp.bfloat16),) * 4,
        input_output_aliases={2 + index: index for index in range(len(before))},
        compiler_params=pltpu.CompilerParams(vmem_limit_bytes=24 * 2**20),
        cost_estimate=pl.CostEstimate(
            flops=45 * 256 * 1024 * count, bytes_accessed=8 * 256 * 1024 * count, transcendentals=0
        ),
        name="steering",
    )(grid, mics, *before)


def second_gram_kernel(mine_ref, other_ref, inverse_ref, row_ref, copies_ref, slice_ref, sems):
    own = pl.multiple_of(row_ref[0] * 16, 16)
    raw = jnp.concatenate(
        [
            ref[:, :32, lanes].reshape(256, K)
            for ref in (mine_ref, other_ref)
            for lanes in (slice(0, K), slice(K, 2 * K))
        ],
        axis=0,
    )
    raw_high, raw_low = halves(raw)
    parts = halves(inverse_ref[...].T)
    second = split_dot(raw_high, raw_low, parts)
    slice_ref[...] = inverse_ref[pl.ds(own, 16), :]
    parts = halves(slice_ref[...].T)
    second_slice = split_dot(raw_high, raw_low, parts)
    slice_ref[...] = dot_tn(second_slice, second)
    drain(
        [
            pltpu.make_async_copy(slice_ref, copies_ref.at[index], sems.at[index])
            for index in range(16)
        ]
    )


def second_gram_slice(mine, other, inverse, row):
    return pl.pallas_call(
        second_gram_kernel,
        out_shape=pltpu.HBM((16, 16, K), jnp.float32),
        in_specs=[VMEM, VMEM, VMEM, SMEM],
        out_specs=HBM,
        scratch_shapes=[pltpu.VMEM((16, K), jnp.float32), pltpu.SemaphoreType.DMA((16,))],
        compiler_params=pltpu.CompilerParams(vmem_limit_bytes=24 * 2**20),
        cost_estimate=pl.CostEstimate(
            flops=2 * 1024 * K * (K + 32), bytes_accessed=2**21, transcendentals=0
        ),
        name="second_gram",
    )(mine, other, inverse, row)


def project_kernel(half_ref, *refs):
    raw_refs, beside_refs = refs[:2], refs[2:8]
    cos_high, cos_low, sin_high, sin_low = refs[8:12]
    out_ref, high_ref, low_ref, slots, sems = refs[12:]
    step = pl.program_id(0)

    @pl.when(step == 0)
    def _():
        lower = half_ref[0] == 0
        sources = []
        for ref in raw_refs:
            parts = [
                ref[:, :32, lane : lane + HALF].reshape(256, HALF) for lane in range(0, 2 * K, HALF)
            ]
            sources.append(
                (jnp.where(lower, parts[0], parts[1]), jnp.where(lower, parts[2], parts[3]))
            )
        for ref in beside_refs:
            sources.append((ref[:, :, :HALF].reshape(256, HALF), ref[:, :, HALF:].reshape(256, HALF)))
        for index, (real, imag) in enumerate(sources):
            start = index * 256
            for base, value in (
                (0, jnp.concatenate([real, imag], axis=1)),
                (2048, jnp.concatenate([-imag, real], axis=1)),
            ):
                high, low = halves(value)
                high_ref[base + start : base + start + 256, :] = high
                low_ref[base + start : base + start + 256, :] = low

    high = jnp.concatenate([cos_high[...], sin_high[...]], axis=1)
    low = jnp.concatenate([cos_low[...], sin_low[...]], axis=1)
    product = jnp.dot(high, high_ref[...], preferred_element_type=jnp.float32)
    product += jnp.dot(high, low_ref[...], preferred_element_type=jnp.float32)
    product += jnp.dot(low, high_ref[...], preferred_element_type=jnp.float32)
    slots[pl.ds(2 * step, 2)] = product.reshape(2, 128, 256)

    def copy(index):
        both = pl.ds(2 * index, 2)
        return pltpu.make_async_copy(slots.at[both], out_ref.at[both], sems.at[index])

    copy(step).start()

    @pl.when(step == 3)
    def _():
        for index in range(4):
            copy(index).wait()


def project(half, raw, beside, steered):
    block = pl.BlockSpec((256, 2048), lambda i: (i, 0))
    return pl.pallas_call(
        project_kernel,
        grid=(4,),
        in_specs=[SMEM]
        + [pl.BlockSpec((8, 40, 512), lambda i: (0, 0, 0))] * 2
        + [pl.BlockSpec((8, 32, 256), lambda i: (0, 0, 0))] * 6
        + [block] * 4,
        out_specs=HBM,
        out_shape=pltpu.HBM((8, 128, 256), jnp.float32),
        scratch_shapes=[
            pltpu.VMEM((4096, 256), jnp.bfloat16),
            pltpu.VMEM((4096, 256), jnp.bfloat16),
            pltpu.VMEM((8, 128, 256), jnp.float32),
            pltpu.SemaphoreType.DMA((4,)),
        ],
        compiler_params=pltpu.CompilerParams(vmem_limit_bytes=40 * 2**20),
        cost_estimate=pl.CostEstimate(
            flops=3 * 2 * 1024 * 4096 * 256, bytes_accessed=18 * 2**20, transcendentals=0
        ),
        name="project",
    )(half, *raw, *beside, *[in_hbm(value) for value in steered])


def half_of_vectors(pieces, half):
    lower = jnp.concatenate([pieces[..., :HALF], pieces[..., K : K + HALF]], axis=-1)
    upper = jnp.concatenate([pieces[..., HALF:K], pieces[..., K + HALF :]], axis=-1)
    return jnp.where(half == 0, lower, upper)


def body(csm_real, csm_imag, start_block, mic_coords, grid_coords, bin_index):
    row = lax.axis_index("row")
    core = row % 2
    own_core = core.reshape(1)
    col = lax.axis_index("col")
    half = col % 2
    points = grid_coords.reshape(2, 4, 2, 256)
    points = jnp.where(col // 2 % 2 == 0, points[:, :, 0], points[:, :, 1]).reshape(2, 1024)
    reduced = ((bin_index * points) % MOD).astype(jnp.float32).T

    mine = exchange(spread_start(start_block), "row", Z_GROUPS)
    *tiles, mic_coords, reduced = lax.optimization_barrier(
        (*prepare(csm_real, csm_imag, own_core), mic_coords, reduced)
    )
    places = [mic_coords] + [lax.ppermute(mic_coords, "col", ALONG_X[flip]) for flip in (1, 2, 3)]
    mine, *places = lax.optimization_barrier((mine, *places, *tiles))
    places, tiles = places[:4], places[4:]
    other = lax.ppermute(mine, "row", CORE_SWAP)
    first_partial = first_product(*tiles[:2], mine, other, own_core)

    places = jnp.stack(places, axis=1).reshape(2, 4, 8, 2, 32)
    even, odd = places[:, :, :, 0], places[:, :, :, 1]
    mics = jnp.stack([jnp.where(core == 0, even, odd), jnp.where(core == 0, odd, even)], axis=2)
    mics = mics.reshape(2, 2048).astype(jnp.float32)
    steered = steering(reduced, mics, 0, 3)
    first_pieces = exchange(first_partial, "col")
    first_pieces, steered = lax.optimization_barrier((first_pieces, steered))

    steered = steering(reduced, mics, 3, 2, steered)
    first = exchange(spread(first_pieces, 16)[1], "col")
    first, steered = lax.optimization_barrier((first, steered))
    sent, gram_rows, parts = sent_product(*tiles[4:], first, own_core)
    got = lax.ppermute(sent, "row", CORE_SWAP)
    kept = kept_product(*tiles[2:4], parts, gram_rows)
    pair = stage(kept, got)

    steered = steering(reduced, mics, 5, 2, steered)
    pieces = exchange(pair, "row", Z_GROUPS)
    pieces, steered = lax.optimization_barrier((pieces, steered))
    own, spread_out = spread(pieces, 8)

    steered = steering(reduced, mics, 7, 1, steered)
    mine = exchange(spread_out, "row", Z_GROUPS)
    mine, steered = lax.optimization_barrier((mine, steered))
    other = lax.ppermute(mine, "row", CORE_SWAP)
    taken = half_of_vectors(mine[:, :32], half)
    given = half_of_vectors(mine[:, :32], 1 - half)
    near = [
        lax.ppermute(taken if flip == 2 else given, "col", ALONG_X[flip]) for flip in (1, 2, 3)
    ]
    first_inverse = first_factor(mine, other, own_core)
    gram_copies = second_gram_slice(mine, other, first_inverse, row.reshape(1))
    near, gram_copies = lax.optimization_barrier((near, gram_copies))
    far = [lax.ppermute(block, "row", CORE_SWAP) for block in near]
    beside = [block for both in zip(near, far) for block in both]
    gram_pieces = exchange(gram_copies, "col")
    part = project(half.reshape(1), (mine, other), beside, steered)
    part, gram_pieces = lax.optimization_barrier((part, gram_pieces))
    pieces = exchange(part, "col", POINT_GROUPS)
    second_gram = lax.all_gather(jnp.sum(gram_pieces, axis=0), "row", axis=0, tiled=True)
    basis, both_inverse, weights = second_factor(second_gram, first_inverse, own)
    return (basis, finish(pieces, both_inverse, weights).reshape(128))


def solution(mesh):
    in_specs = (
        P("row", "col"),
        P("row", "col"),
        P(None, ("col", "row"), None),
        P(None, "col"),
        P(None, "row"),
        P(),
    )
    out_specs = (P(None, ("col", "row"), None), P(("row", "col")))
    return jax.shard_map(body, mesh=mesh, in_specs=in_specs, out_specs=out_specs, check_vma=False)
```
